32 devices in a mesh: dp: 8 (over y, x, core), fsdp: 4 (over z).
Axes of the slice: x: 2, y: 2, z: 4, core: 2. Of those that a mesh axis runs over, the one named last changes fastest.
Arguments:
- token_ids: int32 [64, 512], P(('dp', 'fsdp')), may hold values from 0 to 50303
- true_mask: int32 [64, 512], P(('dp', 'fsdp')), may hold values from 0 to 1, as said below
- keep_layer: int32 [64], P(('dp', 'fsdp')), may hold values 0 or 1
- picked: int32 [64, 64], P(('dp', 'fsdp')), may hold values from 0 to 511, as said below
- teacher_hidden: bfloat16 [64, 512, 768], P(('dp', 'fsdp')), may hold values from -8 to 8
- teacher_logits: bfloat16 [64, 64, 50304], P(('dp', 'fsdp')), may hold values from -12 to 12
- embed_table: float32 [50304, 768], P(('dp', 'fsdp'))
- pos_table: float32 [512, 768], P(None, ('dp', 'fsdp')), may hold values from -0.21875 to 0.21875
- query_key_value_weight: float32 [768, 2304], P(('dp', 'fsdp')), may hold values from -0.21875 to 0.21875
- output_weight: float32 [768, 768], P(('dp', 'fsdp')), may hold values from -0.875 to 0.875
- up_weight: float32 [768, 3072], P(('dp', 'fsdp')), may hold values from -0.21875 to 0.21875
- down_weight: float32 [3072, 768], P(('dp', 'fsdp')), may hold values from -0.109375 to 0.109375
- gains_biases: float32 [14, 768], P(None, ('dp', 'fsdp'))
- first_embed: float32 [50304, 768], P(('dp', 'fsdp')), may hold values from -4.5776367e-05 to 4.5776367e-05
- first_pos: float32 [512, 768], P(None, ('dp', 'fsdp')), may hold values from -4.5776367e-05 to 4.5776367e-05
- first_qkv: float32 [768, 2304], P(('dp', 'fsdp')), may hold values from -4.5776367e-05 to 4.5776367e-05
- first_out: float32 [768, 768], P(('dp', 'fsdp')), may hold values from -4.5776367e-05 to 4.5776367e-05
- first_up: float32 [768, 3072], P(('dp', 'fsdp')), may hold values from -4.5776367e-05 to 4.5776367e-05
- first_down: float32 [3072, 768], P(('dp', 'fsdp')), may hold values from -4.5776367e-05 to 4.5776367e-05
- first_gains: float32 [14, 768], P(None, ('dp', 'fsdp')), may hold values from -0.00018310547 to 0.00018310547
- second_embed: float32 [50304, 768], P(('dp', 'fsdp')), may hold values from 5.421191e-12 to 2.1684763e-11
- second_pos: float32 [512, 768], P(None, ('dp', 'fsdp')), may hold values from 5.421191e-12 to 2.1684763e-11
- second_qkv: float32 [768, 2304], P(('dp', 'fsdp')), may hold values from 5.421191e-12 to 2.1684763e-11
- second_out: float32 [768, 768], P(('dp', 'fsdp')), may hold values from 5.421191e-12 to 2.1684763e-11
- second_up: float32 [768, 3072], P(('dp', 'fsdp')), may hold values from 5.421191e-12 to 2.1684763e-11
- second_down: float32 [3072, 768], P(('dp', 'fsdp')), may hold values from 5.421191e-12 to 2.1684763e-11
- second_gains: float32 [14, 768], P(None, ('dp', 'fsdp')), may hold values from 8.673905e-11 to 3.469562e-10
Outputs:
- loss_sum: float32 [], replicated
- token_count: float32 [], replicated
- grad_norm: float32 [], replicated
- new_embed: float32 [50304, 768], P(('dp', 'fsdp'))
- new_pos: float32 [512, 768], P(None, ('dp', 'fsdp'))
- new_qkv: float32 [768, 2304], P(('dp', 'fsdp'))
- new_out: float32 [768, 768], P(('dp', 'fsdp'))
- new_up: float32 [768, 3072], P(('dp', 'fsdp'))
- new_down: float32 [3072, 768], P(('dp', 'fsdp'))
- new_gains: float32 [14, 768], P(None, ('dp', 'fsdp'))
- moment_embed: float32 [50304, 768], P(('dp', 'fsdp'))
- moment_pos: float32 [512, 768], P(None, ('dp', 'fsdp'))
- moment_qkv: float32 [768, 2304], P(('dp', 'fsdp'))
- moment_out: float32 [768, 768], P(('dp', 'fsdp'))
- moment_up: float32 [768, 3072], P(('dp', 'fsdp'))
- moment_down: float32 [3072, 768], P(('dp', 'fsdp'))
- moment_gains: float32 [14, 768], P(None, ('dp', 'fsdp'))
- square_embed: float32 [50304, 768], P(('dp', 'fsdp'))
- square_pos: float32 [512, 768], P(None, ('dp', 'fsdp'))
- square_qkv: float32 [768, 2304], P(('dp', 'fsdp'))
- square_out: float32 [768, 768], P(('dp', 'fsdp'))
- square_up: float32 [768, 3072], P(('dp', 'fsdp'))
- square_down: float32 [3072, 768], P(('dp', 'fsdp'))
- square_gains: float32 [14, 768], P(None, ('dp', 'fsdp'))
- matrix_norms: float32 [2, 7], replicated
The draws below stay inside these ranges and needn't reach their ends.
Inputs may be any that keep to these rules, and one draw needn't show every extreme that they name: `true_mask`: in each sequence the true tokens are the first ones, at least one. `picked`: each entry is a position of a true token of its sequence.
All inputs are finite; a program needn't handle non-finite values. No bound on the sum of `keep_layer` on one device may be relied on, other than what follows from the above.
Results may differ from the reference program's by a relative error of at most 0.0098.
The reference program's roundings to bfloat16 on the way count: a program that leaves them out, or rounds other values in their place, can miss the bound.
Values may be sent and summed in bfloat16 or wider, within the bound.
No kernel may reach another device: no remote copies, remote signals or barrier semaphores. Data moves between devices by JAX's collectives and lax.ppermute only.
A program may use at most 832 MiB of HBM per device.

```python
import math
import jax
import jax.numpy as jnp
import numpy as np
from jax import lax

D = 768
H = 12
HD = 64
FF = 3072
VOCAB = 50304
LEN = 512
PICK = 64
STEP = 10
SEQ_DEV = 2
SEQS = 64
PARAMS = 46115328
N_DP = 8
N_FSDP = 4


def token_lengths(key):
    device_rank = jnp.arange(SEQS) // SEQ_DEV
    outer_rank = device_rank // N_FSDP
    inner_rank = device_rank % N_FSDP
    longest = LEN * (N_DP - 1 + outer_rank) * (N_FSDP - 1 + inner_rank) // (4 * (N_DP - 1) * (N_FSDP - 1))
    longest = jnp.maximum(longest, 1)
    shortest = jnp.maximum(longest * 2 // 3, 1)
    drawn = jax.random.randint(key, (SEQS,), shortest, longest + 1)
    return jnp.where(jnp.arange(SEQS) == SEQS - 1, longest, drawn)


def draw_true_mask(key, part):
    lengths = token_lengths(key)
    return (jnp.arange(LEN)[None, :] < lengths[:, None]).astype(jnp.int32)


def draw_picked(key, part):
    lengths = token_lengths(key)
    key = jax.random.fold_in(key, 2)
    spots = jax.random.randint(key, (SEQS, PICK), 0, lengths[:, None])
    column_key = jax.random.fold_in(key, 5)
    last_column = jax.random.randint(column_key, (SEQS,), 0, PICK)
    at_last = jnp.arange(PICK)[None, :] == last_column[:, None]
    return jnp.where(at_last, lengths[:, None] - 1, spots).astype(jnp.int32)


def draw_embed_table(key, part):
    key = jax.random.fold_in(key, 3)
    row_place = jnp.arange(VOCAB, dtype=jnp.float32)[:, None] / VOCAB
    base_values = jax.random.normal(key, (VOCAB, D), jnp.float32)
    row_scale = 1.0 + 2.0 * row_place
    return base_values * row_scale * D ** (-0.5)


def draw_gains_biases(key, part):
    key = jax.random.fold_in(key, 4)
    column_place = jnp.arange(D, dtype=jnp.float32)[None, :] / D
    noise = jax.random.normal(key, (14, D), jnp.float32)
    rising = 0.5 + column_place
    row_number = jnp.arange(14)[:, None]
    is_gain = (row_number == 0) | (row_number == 5) | (row_number == 8)
    return jnp.where(is_gain, rising * (1.0 + 0.1 * noise), 0.3 * noise)


def draw_teacher_hidden(key, part):
    key = jax.random.fold_in(key, 6)
    feature_key = jax.random.fold_in(key, 1)
    place_key = jax.random.fold_in(key, 2)
    token_key = jax.random.fold_in(key, 3)
    feature_part = 0.4 * jnp.clip(jax.random.normal(feature_key, (1, 1, D), jnp.float32), -3.0, 3.0)
    place_part = 0.4 * jnp.clip(jax.random.normal(place_key, (1, LEN, D), jnp.float32), -3.0, 3.0)
    token_part = jnp.clip(jax.random.normal(token_key, (SEQS, LEN, D), jnp.float32), -4.0, 4.0)
    return (feature_part + place_part + token_part).astype(jnp.bfloat16)


def touch_ends(values, own_key, least, largest):
    place = [jax.random.randint(jax.random.fold_in(own_key, axis), (), 0, length) for axis, length in enumerate(values.shape)]
    widest = values.shape.index(max(values.shape))
    beside = place[:widest] + [(place[widest] + 1) % values.shape[widest]] + place[widest + 1:]
    return values.at[tuple(place)].set(least).at[tuple(beside)].set(largest)


def steps_of(rng, shape, pieces, low, top_value):
    def one(position, blocks):
        heights = jax.random.uniform(jax.random.fold_in(jax.random.fold_in(rng, 6), position), (blocks,), jnp.float32, low / len(pieces), top_value / len(pieces))
        return jnp.repeat(jnp.exp(heights), shape[position] // blocks).reshape((-1,) + (1,) * (len(shape) - position - 1))

    level = one(*pieces[0])
    for cut in pieces[1:]:
        level = level * one(*cut)
    return level


def rank_table(amount, skew):
    weights = [(1 << 20) // math.isqrt(rank ** skew) + 1 for rank in range(1, amount + 1)]
    spread = 1 + sum(weights) // (1 << 30)
    return np.cumsum(np.array([max(1, weight // spread) for weight in weights]))


def ranked(rng, extent, count, slope):
    listing = rank_table(count, slope)
    pick = jax.random.randint(jax.random.fold_in(rng, 1), extent, 0, int(listing[count - 1]))
    grade = jnp.searchsorted(jnp.asarray(listing, jnp.int32), pick, side="right")
    return jax.random.permutation(jax.random.fold_in(rng, 2), count)[grade].astype(jnp.int32)


def gaussian(own_key, dims, spread, limit, pieces=(), kind=jnp.bfloat16):
    entries = spread * jax.random.normal(own_key, dims, jnp.float32)
    if pieces:
        entries = entries * steps_of(own_key, dims, pieces, -0.22, 0.18)
    return jnp.clip(entries, -limit, limit).astype(kind)


def setup_inputs(seed: int = 0) -> dict:
    splits = jax.random.split(jax.random.key(seed), 28)
    token_ids = touch_ends(ranked(splits[0], (SEQS, LEN), VOCAB, 2), jax.random.fold_in(splits[0], 3), 0, VOCAB - 1).astype(jnp.int32)
    true_mask = draw_true_mask(jax.random.fold_in(splits[27], 71), 0)
    keep_layer = touch_ends((jax.random.randint(splits[2], (SEQS,), 0, 2) < 1).astype(jnp.int32), jax.random.fold_in(splits[2], 1), 0, 1)
    picked = draw_picked(jax.random.fold_in(splits[27], 71), 0)
    teacher_hidden = draw_teacher_hidden(jax.random.fold_in(splits[27], 71), 0)
    teacher_logits = gaussian(splits[5], (SEQS, PICK, VOCAB), 2.0, 12.0, ((0, 32),))
    embed_table = draw_embed_table(jax.random.fold_in(splits[27], 71), 0)
    pos_table = gaussian(splits[7], (LEN, D), D ** -0.5, 0.21875, ((1, 32),), jnp.float32)
    query_key_value_weight = gaussian(splits[8], (D, 3 * D), D ** -0.5, 0.21875, ((0, 32),), jnp.float32)
    output_weight = gaussian(splits[9], (D, D), (D * 32 // LEN) ** -0.5, 0.875, ((0, 32),), jnp.float32)
    up_weight = gaussian(splits[10], (D, FF), D ** -0.5, 0.21875, ((0, 32),), jnp.float32)
    down_weight = gaussian(splits[11], (FF, D), FF ** -0.5, 0.109375, ((0, 32),), jnp.float32)
    gains_biases = draw_gains_biases(jax.random.fold_in(splits[27], 71), 0)
    first_embed = gaussian(splits[13], (VOCAB, D), (0.0556 * PARAMS ** -0.5), 4.57763671875e-05, ((0, 32),), jnp.float32)
    first_pos = gaussian(splits[14], (LEN, D), (0.0556 * PARAMS ** -0.5), 4.57763671875e-05, ((1, 32),), jnp.float32)
    first_qkv = gaussian(splits[15], (D, 3 * D), (0.0556 * PARAMS ** -0.5), 4.57763671875e-05, ((0, 32),), jnp.float32)
    first_out = gaussian(splits[16], (D, D), (0.0556 * PARAMS ** -0.5), 4.57763671875e-05, ((0, 32),), jnp.float32)
    first_up = gaussian(splits[17], (D, FF), (0.0556 * PARAMS ** -0.5), 4.57763671875e-05, ((0, 32),), jnp.float32)
    first_down = gaussian(splits[18], (FF, D), (0.0556 * PARAMS ** -0.5), 4.57763671875e-05, ((0, 32),), jnp.float32)
    first_gains = gaussian(splits[19], (14, D), (0.222 * PARAMS ** -0.5), 0.00018310547, ((1, 32),), jnp.float32)
    second_embed = jnp.clip(jnp.exp(math.log(2.168476335995262e-11) - 1.3862944 * jax.random.uniform(splits[20], (VOCAB, D), jnp.float32) ** steps_of(splits[20], (VOCAB, D), ((0, 32),), -0.2, 0.2)), 5.421190839988155e-12, 2.168476335995262e-11)
    second_pos = jnp.clip(jnp.exp(math.log(2.168476335995262e-11) - 1.3862944 * jax.random.uniform(splits[21], (LEN, D), jnp.float32) ** steps_of(splits[21], (LEN, D), ((1, 32),), -0.2, 0.2)), 5.421190839988155e-12, 2.168476335995262e-11)
    second_qkv = jnp.clip(jnp.exp(math.log(2.168476335995262e-11) - 1.3862944 * jax.random.uniform(splits[22], (D, 3 * D), jnp.float32) ** steps_of(splits[22], (D, 3 * D), ((0, 32),), -0.2, 0.2)), 5.421190839988155e-12, 2.168476335995262e-11)
    second_out = jnp.clip(jnp.exp(math.log(2.168476335995262e-11) - 1.3862944 * jax.random.uniform(splits[23], (D, D), jnp.float32) ** steps_of(splits[23], (D, D), ((0, 32),), -0.2, 0.2)), 5.421190839988155e-12, 2.168476335995262e-11)
    second_up = jnp.clip(jnp.exp(math.log(2.168476335995262e-11) - 1.3862944 * jax.random.uniform(splits[24], (D, FF), jnp.float32) ** steps_of(splits[24], (D, FF), ((0, 32),), -0.2, 0.2)), 5.421190839988155e-12, 2.168476335995262e-11)
    second_down = jnp.clip(jnp.exp(math.log(2.168476335995262e-11) - 1.3862944 * jax.random.uniform(splits[25], (FF, D), jnp.float32) ** steps_of(splits[25], (FF, D), ((0, 32),), -0.2, 0.2)), 5.421190839988155e-12, 2.168476335995262e-11)
    second_gains = jnp.clip(jnp.exp(math.log(3.469562137592419e-10) - 1.3862944 * jax.random.uniform(splits[26], (14, D), jnp.float32) ** steps_of(splits[26], (14, D), ((1, 32),), -0.2, 0.2)), 8.673905343981048e-11, 3.469562137592419e-10)
    return {"token_ids": token_ids, "true_mask": true_mask, "keep_layer": keep_layer, "picked": picked, "teacher_hidden": teacher_hidden, "teacher_logits": teacher_logits, "embed_table": embed_table, "pos_table": pos_table, "query_key_value_weight": query_key_value_weight, "output_weight": output_weight, "up_weight": up_weight, "down_weight": down_weight, "gains_biases": gains_biases, "first_embed": first_embed, "first_pos": first_pos, "first_qkv": first_qkv, "first_out": first_out, "first_up": first_up, "first_down": first_down, "first_gains": first_gains, "second_embed": second_embed, "second_pos": second_pos, "second_qkv": second_qkv, "second_out": second_out, "second_up": second_up, "second_down": second_down, "second_gains": second_gains}


@jax.custom_vjp
def reduced_precision(v):
    return lax.optimization_barrier(v.astype(jnp.bfloat16)).astype(jnp.float32)

@jax.custom_vjp
def reduced_backward(v):
    return v

def low_keep(v):
    return (reduced_precision(v), None)

def low_pass(kept, grad):
    return (grad,)

def back_keep(v):
    return (v, None)

def back_low(kept, grad):
    return (reduced_precision(grad),)
reduced_precision.defvjp(low_keep, low_pass)
reduced_backward.defvjp(back_keep, back_low)
NORM_EPS = 1e-05
CLIP_NORM = 0.5
BETA_ONE = 0.9
BETA_TWO = 0.999
ADAM_EPS = 1e-06
DECAY_RATE = 0.01
LEARN_RATE = 0.3
MASKED_SCORE = -1e+30

def norm_rows(values, gain_row, shift_row):
    row_mean = lax.optimization_barrier(jnp.mean(values, axis=-1, keepdims=True))
    centered = values - row_mean
    row_var = lax.optimization_barrier(jnp.mean(centered * centered, axis=-1, keepdims=True))
    return centered * lax.rsqrt(row_var + NORM_EPS) * gain_row + shift_row

def matrix_product(form, left_op, right_op):
    return jnp.einsum(form, left_op, right_op, precision=lax.Precision.HIGHEST)

def encoder_layer(layer_inputs, key_live, query_key_value_weight, output_weight, up_weight, down_weight, vector_params):
    row_width = layer_inputs.shape[-1]
    shape_heads = layer_inputs.shape[:2] + (H, HD)
    joined_heads = matrix_product('txv,vc->txc', reduced_precision(layer_inputs), query_key_value_weight)
    queries = reduced_precision(reduced_backward(joined_heads[..., :row_width] + vector_params[2])).reshape(shape_heads)
    key_rows = reduced_precision(reduced_backward(joined_heads[..., row_width:2 * row_width])).reshape(shape_heads)
    values = reduced_precision(reduced_backward(joined_heads[..., 2 * row_width:] + vector_params[3])).reshape(shape_heads)
    scores = reduced_backward(matrix_product('sqhe,skhe->shqk', queries, key_rows) * HD ** (-0.5))
    scores = jnp.where(key_live[:, None, None, :], scores, MASKED_SCORE)
    softmaxed = reduced_precision(jax.nn.softmax(scores, axis=-1))
    mixed_output = reduced_precision(reduced_backward(matrix_product('shqk,skhe->sqhe', softmaxed, values).reshape(layer_inputs.shape)))
    attention_result = reduced_backward(matrix_product('txv,vc->txc', mixed_output, output_weight) + vector_params[4])
    first_normed = norm_rows(layer_inputs + attention_result, vector_params[5], vector_params[6])
    hidden_state = reduced_backward(matrix_product('kwb,bx->kwx', reduced_precision(first_normed), up_weight) + vector_params[10:14].reshape(-1))
    gelu_activated = reduced_precision(jax.nn.gelu(hidden_state, approximate=False))
    feed_forward_output = reduced_backward(matrix_product('epk,kh->eph', gelu_activated, down_weight) + vector_params[7])
    return norm_rows(first_normed + feed_forward_output, vector_params[8], vector_params[9])

def total_loss(masters, token_ids, true_mask, keep_layer, picked, target_hidden, target_logits):
    embed_low, pos_low, qkv_low, out_low, up_low, down_low, vector_params = [reduced_precision(weight) for weight in masters]

    def block_loss(id_rows, live_rows, keep_rows, picked_rows, block_hidden, block_logits):
        embedded = jnp.take(embed_low, id_rows, axis=0) + pos_low[None]
        layer_inputs = norm_rows(embedded, vector_params[0], vector_params[1])
        layer_out = encoder_layer(layer_inputs, live_rows > 0, qkv_low, out_low, up_low, down_low, vector_params)
        final_rows = jnp.where((keep_rows > 0)[:, None, None], layer_out, layer_inputs)
        hidden_gap = final_rows - block_hidden
        weighted = live_rows.astype(jnp.float32)[:, :, None]
        hidden_loss = jnp.sum(weighted * hidden_gap * hidden_gap)
        chosen = jnp.take_along_axis(final_rows, picked_rows[:, :, None], axis=1)
        logits = reduced_backward(matrix_product('spd,vd->spv', reduced_precision(chosen), embed_low))
        mismatch = logits - block_logits
        return hidden_loss + jnp.sum(mismatch * mismatch)
    checked = jax.checkpoint(block_loss)

    def scan_body(running, block_data):
        return (running + checked(*block_data), None)
    blocks = tuple((member.reshape((SEQS // SEQ_DEV, SEQ_DEV) + member.shape[1:]) for member in (token_ids, true_mask, keep_layer, picked, target_hidden, target_logits)))
    loss_total, _ = lax.scan(scan_body, jnp.zeros((), jnp.float32), blocks)
    return loss_total

def reference(token_ids, true_mask, keep_layer, picked, teacher_hidden, teacher_logits, embed_table, pos_table, query_key_value_weight, output_weight, up_weight, down_weight, gains_biases, first_embed, first_pos, first_qkv, first_out, first_up, first_down, first_gains, second_embed, second_pos, second_qkv, second_out, second_up, second_down, second_gains):
    masters = (embed_table, pos_table, query_key_value_weight, output_weight, up_weight, down_weight, gains_biases)
    firsts = (first_embed, first_pos, first_qkv, first_out, first_up, first_down, first_gains)
    seconds = (second_embed, second_pos, second_qkv, second_out, second_up, second_down, second_gains)
    target_hidden = teacher_hidden.astype(jnp.float32)
    target_logits = teacher_logits.astype(jnp.float32)

    def loss_of(weights):
        return total_loss(weights, token_ids, true_mask, keep_layer, picked, target_hidden, target_logits)
    loss_sum, pull_back = jax.vjp(loss_of, masters)
    raw_grads = pull_back(jnp.ones_like(loss_sum))[0]
    token_count = jnp.sum(true_mask.astype(jnp.float32))
    gradients = [member / token_count for member in raw_grads]
    grad_norm = jnp.sqrt(jnp.sum(jnp.stack([jnp.sum(member * member) for member in gradients])))
    clip_factor = jnp.minimum(1.0, CLIP_NORM / grad_norm)
    new_weights = []
    moments = []
    squares = []
    weight_norms = []
    update_norms = []
    for weight, gradient, moment, square in zip(masters, gradients, firsts, seconds):
        clipped = gradient * clip_factor
        moment_new = BETA_ONE * moment + (1.0 - BETA_ONE) * clipped
        square_new = BETA_TWO * square + (1.0 - BETA_TWO) * clipped * clipped
        update = moment_new / (1.0 - BETA_ONE ** STEP) / (jnp.sqrt(square_new / (1.0 - BETA_TWO ** STEP)) + ADAM_EPS) + DECAY_RATE * weight
        weight_norm = jnp.sqrt(jnp.sum(weight * weight))
        update_norm = jnp.sqrt(jnp.sum(update * update))
        new_weights.append(weight - LEARN_RATE * (weight_norm / update_norm) * update)
        moments.append(moment_new)
        squares.append(square_new)
        weight_norms.append(weight_norm)
        update_norms.append(update_norm)
    matrix_norms = jnp.stack([jnp.stack(weight_norms), jnp.stack(update_norms)])
    return (loss_sum, token_count, grad_norm, new_weights[0], new_weights[1], new_weights[2], new_weights[3], new_weights[4], new_weights[5], new_weights[6], moments[0], moments[1], moments[2], moments[3], moments[4], moments[5], moments[6], squares[0], squares[1], squares[2], squares[3], squares[4], squares[5], squares[6], matrix_norms)
```

```python
import functools

import jax
import jax.numpy as jnp
from jax import lax
from jax.experimental import pallas as pl
from jax.experimental.pallas import tpu as pltpu
from jax.sharding import Mesh
from jax.sharding import PartitionSpec as P

H = 12
HD = 64
STEP = 10


NORM_EPS = 1e-05
CLIP_NORM = 0.5
BETA_ONE = 0.9
BETA_TWO = 0.999
ADAM_EPS = 1e-06
DECAY_RATE = 0.01
LEARN_RATE = 0.3
MASKED_SCORE = -1e30

SPLIT = ("plane", "pair")
AXES = ("plane", "pair", "fsdp")
VMEM = 60 * 2**20


def norm_rows(values, gain_row, shift_row):
    row_mean = jnp.mean(values, axis=-1, keepdims=True)
    centered = values - row_mean
    row_var = jnp.mean(centered * centered, axis=-1, keepdims=True)
    return centered * lax.rsqrt(row_var + NORM_EPS) * gain_row + shift_row


def normal_cdf(values):
    return 0.5 + 0.5 * lax.erf(values * 0.5**0.5)


def gelu_slope(values):
    density = jnp.exp(-0.5 * values * values) * (2.0 * jnp.pi) ** -0.5
    return normal_cdf(values) + values * density


def dense(left_op, right_op):
    return jnp.dot(left_op, right_op, preferred_element_type=jnp.float32)


def dense_tn(left_op, right_op):
    return lax.dot_general(
        left_op, right_op, (((0,), (0,)), ((), ())), preferred_element_type=jnp.float32
    )


def dense_nt(left_op, right_op):
    return lax.dot_general(
        left_op, right_op, (((1,), (1,)), ((), ())), preferred_element_type=jnp.float32
    )


def pair_lanes(shape, member):
    lane = lax.broadcasted_iota(jnp.int32, shape, 1)
    return (lane >= HD) if member else (lane < HD)


def softmax_rows(query_rows, key_rows, length):
    scores = dense_nt(query_rows, key_rows)
    spot = lax.broadcasted_iota(jnp.int32, scores.shape, 1)
    scores = jnp.where(spot < length, scores, MASKED_SCORE)
    exponent = jnp.exp(scores - jnp.max(scores, axis=1, keepdims=True))
    return exponent / jnp.sum(exponent, axis=1, keepdims=True)


def row_spans(seq_len):
    half = seq_len // 2
    return ((0, half), (half, seq_len))


def mix_kernel(length_ref, query_ref, key_ref, value_ref, mixed_ref):
    seq_len = query_ref.shape[0]
    length = length_ref[pl.program_id(0)]

    for low, high in row_spans(seq_len):

        @pl.when((length > low) & (length <= high))
        def _():
            step = high // 2 if low else high
            keys, values = key_ref[0:high, :], value_ref[0:high, :]
            for row in range(0, high, step):
                queries = query_ref[row : row + step, :] * 0.125
                parts = []
                for member in (0, 1):
                    lanes = pair_lanes(queries.shape, member)
                    chance = softmax_rows(
                        jnp.where(lanes, queries, jnp.zeros_like(queries)), keys, length
                    )
                    parts.append(dense(chance.astype(jnp.bfloat16), values))
                mixed_ref[row : row + step, :] = jnp.where(
                    pair_lanes(parts[0].shape, 1), parts[1], parts[0]
                ).astype(jnp.bfloat16)
            if high < seq_len:
                mixed_ref[high:, :] = jnp.zeros((seq_len - high, 2 * HD), jnp.bfloat16)

    @pl.when(length == 0)
    def _():
        mixed_ref[...] = jnp.zeros_like(mixed_ref)


def unmix_kernel(
    length_ref, query_ref, key_ref, value_ref, grad_ref, query_out, key_out, value_out
):
    seq_len = query_ref.shape[0]
    length = length_ref[pl.program_id(0)]
    outs = (query_out, key_out, value_out)

    for low, high in row_spans(seq_len):

        @pl.when((length > low) & (length <= high))
        def _():
            step = high // 2 if low else high
            keys, values = key_ref[0:high, :], value_ref[0:high, :]
            key_total, value_total = None, None
            for row in range(0, high, step):
                plain = query_ref[row : row + step, :]
                queries = plain * 0.125
                grads = grad_ref[row : row + step, :]
                parts = []
                for member in (0, 1):
                    lanes = pair_lanes(queries.shape, member)
                    zero = jnp.zeros_like(queries)
                    chance = softmax_rows(jnp.where(lanes, queries, zero), keys, length)
                    slope = dense_nt(jnp.where(lanes, grads, zero), values)
                    slope = chance * (slope - jnp.sum(slope * chance, axis=1, keepdims=True))
                    slope = slope.astype(jnp.bfloat16)
                    parts.append(
                        (
                            dense(slope, keys),
                            dense_tn(slope, plain),
                            dense_tn(chance.astype(jnp.bfloat16), grads),
                        )
                    )
                query_part, key_part, value_part = [
                    jnp.where(pair_lanes(first.shape, 1), second, first)
                    for first, second in zip(*parts)
                ]
                query_out[row : row + step, :] = (query_part * 0.125).astype(jnp.bfloat16)
                key_total = key_part if key_total is None else key_total + key_part
                value_total = value_part if value_total is None else value_total + value_part
            key_out[0:high, :] = (key_total * 0.125).astype(jnp.bfloat16)
            value_out[0:high, :] = value_total.astype(jnp.bfloat16)
            if high < seq_len:
                for ref in outs:
                    ref[high:, :] = jnp.zeros((seq_len - high, 2 * HD), jnp.bfloat16)

    @pl.when(length == 0)
    def _():
        for ref in outs:
            ref[...] = jnp.zeros_like(ref)


def attend(lengths, packed, grad_mixed=None):
    seq_count = lengths.shape[0]
    seq_len = packed.shape[0] // seq_count
    pairs = H // 2

    def block(first):
        return pl.BlockSpec((seq_len, 2 * HD), lambda s, h, _: (s, first + h))

    out = jax.ShapeDtypeStruct((packed.shape[0], H * HD), jnp.bfloat16)
    forward = grad_mixed is None
    operands = (packed, packed, packed) + (() if forward else (grad_mixed,))
    products = seq_count * H * seq_len * seq_len
    return pl.pallas_call(
        mix_kernel if forward else unmix_kernel,
        out_shape=out if forward else (out, out, out),
        grid_spec=pltpu.PrefetchScalarGridSpec(
            num_scalar_prefetch=1,
            grid=(seq_count, pairs),
            in_specs=[block(0), block(pairs), block(2 * pairs)] + ([] if forward else [block(0)]),
            out_specs=block(0) if forward else (block(0),) * 3,
        ),
        compiler_params=pltpu.CompilerParams(vmem_limit_bytes=VMEM),
        cost_estimate=pl.CostEstimate(
            flops=products * HD * (16 if forward else 40),
            bytes_accessed=packed.shape[0] * H * HD * (8 if forward else 14),
            transcendentals=products,
        ),
    )(lengths, *operands)


def parcel_kernel(own_rows, tiles, wide, source, parcel_ref, slots, sems):
    part, parts = pl.program_id(0), pl.num_programs(0)

    def first_tile(index):
        return jnp.minimum(own_rows * index // 128, tiles - wide)

    def fetch(index):
        lane = pl.multiple_of(first_tile(index) * 128, 128)
        slot = lax.rem(index, 2)
        return pltpu.make_async_copy(
            source.at[:, pl.ds(lane, wide * 128)], slots.at[slot], sems.at[slot]
        )

    @pl.when(part == 0)
    def _():
        fetch(0).start()

    @pl.when(part + 1 < parts)
    def _():
        fetch(part + 1).start()

    fetch(part).wait()
    shift = own_rows * part - 128 * first_tile(part)
    width = parcel_ref.shape[2]
    values = slots[lax.rem(part, 2)].astype(jnp.float32)
    values = pltpu.roll(values, lax.rem(wide * 128 - shift, wide * 128), axis=1)[:, :width]
    lane = lax.broadcasted_iota(jnp.int32, values.shape, 1)
    parcel_ref[0] = jnp.where(lane < own_rows, values, 0.0).astype(jnp.bfloat16)


def parcels_of(flat_teacher, own_rows, padded, n_dev):
    n_pick, vocab = flat_teacher.shape
    tiles = vocab // 128
    wide = min(tiles, max((own_rows * r % 128 + padded + 127) // 128 for r in range(n_dev)))
    return pl.pallas_call(
        functools.partial(parcel_kernel, own_rows, tiles, wide),
        out_shape=jax.ShapeDtypeStruct((n_dev, n_pick, padded), jnp.bfloat16),
        grid=(n_dev,),
        in_specs=[pl.BlockSpec(memory_space=pl.ANY)],
        out_specs=pl.BlockSpec((1, n_pick, padded), lambda r: (r, 0, 0)),
        scratch_shapes=[
            pltpu.VMEM((2, n_pick, wide * 128), jnp.bfloat16),
            pltpu.SemaphoreType.DMA((2,)),
        ],
        compiler_params=pltpu.CompilerParams(vmem_limit_bytes=VMEM),
        cost_estimate=pl.CostEstimate(
            flops=4 * n_pick * vocab, bytes_accessed=4 * n_pick * vocab, transcendentals=0
        ),
    )(flat_teacher)


def head_kernel(n_fs, place_ref, chosen_ref, target_ref, *refs):
    tables = refs[:n_fs]
    slope_ref, part_ref, loss_ref = refs[n_fs:]
    chosen = chosen_ref[...]
    senders, _, n_pick, width = target_ref.shape
    total, loss = None, None
    for step in range(n_fs):
        table = tables[step][...]
        target = target_ref[:, place_ref[step]].reshape(senders * n_pick, width)
        gap = dense_nt(chosen, table) - target.astype(jnp.float32)
        square = jnp.sum((gap * gap).reshape(-1, 8, width), axis=0)
        loss = square if loss is None else loss + square
        slope = (2.0 * gap).astype(jnp.bfloat16)
        slope_ref[step] = slope
        part = dense(slope, table)
        total = part if total is None else total + part
    part_ref[...] = total.astype(part_ref.dtype)

    @pl.when(pl.program_id(0) == 0)
    def _():
        loss_ref[...] = jnp.zeros_like(loss_ref)

    loss_ref[...] += loss


def head_products(places, all_chosen, targets, tables):
    n_dp, n_fs, n_pick, padded = targets.shape
    row_width = all_chosen.shape[1]
    rows = 2 * n_pick
    whole = pl.BlockSpec((padded, row_width), lambda m, _: (0, 0))
    return pl.pallas_call(
        functools.partial(head_kernel, n_fs),
        out_shape=(
            jax.ShapeDtypeStruct((n_fs, n_dp * n_pick, padded), jnp.bfloat16),
            jax.ShapeDtypeStruct((n_dp * n_pick, row_width), jnp.bfloat16),
            jax.ShapeDtypeStruct((8, padded), jnp.float32),
        ),
        grid_spec=pltpu.PrefetchScalarGridSpec(
            num_scalar_prefetch=1,
            grid=(n_dp // 2,),
            in_specs=[
                pl.BlockSpec((rows, row_width), lambda m, _: (m, 0)),
                pl.BlockSpec((2, n_fs, n_pick, padded), lambda m, _: (m, 0, 0, 0)),
            ]
            + [whole] * n_fs,
            out_specs=(
                pl.BlockSpec((n_fs, rows, padded), lambda m, _: (0, m, 0)),
                pl.BlockSpec((rows, row_width), lambda m, _: (m, 0)),
                pl.BlockSpec((8, padded), lambda m, _: (0, 0)),
            ),
        ),
        compiler_params=pltpu.CompilerParams(vmem_limit_bytes=VMEM),
        cost_estimate=pl.CostEstimate(
            flops=4 * n_dp * n_pick * n_fs * padded * row_width,
            bytes_accessed=4 * n_dp * n_pick * n_fs * padded + 2 * n_fs * padded * row_width,
            transcendentals=0,
        ),
    )(places, all_chosen, targets, *tables)


def sum_to_owners(values):
    n_plane, n_fs = lax.axis_size("plane"), lax.axis_size("fsdp")
    member = lax.axis_index("pair")
    rows, width = values.shape
    shaped = values.reshape(n_plane, 2, rows // (2 * n_plane), width)
    kept = lax.dynamic_index_in_dim(shaped, member, 1, False)
    given = lax.dynamic_index_in_dim(shaped, 1 - member, 1, False)
    got = lax.ppermute(given, "pair", [(0, 1), (1, 0)])
    part = (kept.astype(jnp.float32) + got.astype(jnp.float32)).astype(jnp.bfloat16)
    part = lax.all_to_all(part, "plane", split_axis=0, concat_axis=0)
    part = jnp.sum(part.astype(jnp.float32), axis=0).astype(jnp.bfloat16)
    part = part.reshape(n_fs, -1, width)
    part = lax.all_to_all(part, "fsdp", split_axis=0, concat_axis=0)
    return jnp.sum(part.astype(jnp.float32), axis=0)


def total_over(values, axes):
    n_dev = lax.axis_size(axes)
    tile = jnp.zeros((8, 128), jnp.float32).at[0, : values.shape[0]].set(values)
    every = lax.all_to_all(
        jnp.broadcast_to(tile[None], (n_dev, 8, 128)), axes, split_axis=0, concat_axis=0
    )
    return jnp.sum(every, axis=0)[0, : values.shape[0]]


def route_plan(ids, live, own_rows, n_dev):
    place = jnp.arange(ids.shape[0])
    owner = ids // own_rows
    same = (ids[:, None] == ids[None, :]) & live[None, :]
    leader = jnp.min(jnp.where(same, place[None, :], ids.shape[0]), axis=1)
    first = live & (leader == place)
    before = (owner[:, None] == owner[None, :]) & (place[None, :] < leader[:, None])
    rank = jnp.sum(before & first[None, :], axis=1, dtype=jnp.int32)
    room = max(16, 1280 // n_dev)
    rounds = jnp.max(jnp.where(first, rank, 0)) // room + 1
    return ids, live, owner, first, rank, room, rounds, own_rows, n_dev


def slots_of(plan, turn):
    ids, live, owner, first, rank, room, rounds, own_rows, n_dev = plan
    here = live & (rank >= turn * room) & (rank < (turn + 1) * room)
    return jnp.where(here, owner * room + rank - turn * room, -1)


def exchange_wanted(plan, turn, axes):
    ids, live, owner, first, rank, room, rounds, own_rows, n_dev = plan
    slots = slots_of(plan, turn)
    local = jnp.where(first, ids - owner * own_rows + 1, 0)
    hit = jnp.arange(n_dev * room)[:, None] == slots[None, :]
    asked = jnp.max(jnp.where(hit, local[None, :], 0), axis=1) - 1
    message = jnp.concatenate(
        [
            asked.reshape(n_dev, room),
            jnp.broadcast_to(rounds, (n_dev, 128 - room)).astype(jnp.int32),
        ],
        axis=1,
    ).reshape(n_dev, 1, 128)
    heard = lax.all_to_all(message, axes, split_axis=0, concat_axis=0).reshape(n_dev, 128)
    return heard[:, :room].reshape(-1), jnp.max(heard[:, room:])


def fetch_rows(plan, turn, wanted, table_low, axes):
    room, own_rows, n_dev = plan[5], plan[7], plan[8]
    one_hot = (wanted[:, None] == jnp.arange(own_rows)[None, :]).astype(jnp.bfloat16)
    rows = dense(one_hot, table_low).astype(jnp.bfloat16)
    rows = lax.all_to_all(rows.reshape(n_dev, room, -1), axes, split_axis=0, concat_axis=0)
    back = (slots_of(plan, turn)[:, None] == jnp.arange(n_dev * room)[None, :]).astype(
        jnp.bfloat16
    )
    return dense(back, rows.reshape(n_dev * room, -1))


def more_rows(plan, rounds, token_rows, table_low, axes):
    def body(state):
        turn, total = state
        wanted, _ = exchange_wanted(plan, turn, axes)
        return turn + 1, total + fetch_rows(plan, turn, wanted, table_low, axes)

    return lax.while_loop(lambda state: state[0] < rounds, body, (jnp.int32(1), token_rows))[1]


def send_rows(plan, turn, wanted, flat_grad, own_rows, axes):
    room, n_dev = plan[5], plan[8]
    spread = (jnp.arange(n_dev * room)[:, None] == slots_of(plan, turn)[None, :]).astype(
        jnp.bfloat16
    )
    high = flat_grad.astype(jnp.bfloat16)
    rest = (flat_grad - high.astype(jnp.float32)).astype(jnp.bfloat16)
    sums = (dense(spread, high) + dense(spread, rest)).astype(jnp.bfloat16)
    got = lax.all_to_all(sums.reshape(n_dev, room, -1), axes, split_axis=0, concat_axis=0)
    one_hot = (jnp.arange(own_rows)[:, None] == wanted[None, :]).astype(jnp.bfloat16)
    return dense(one_hot, got.reshape(n_dev * room, -1))


def more_sent(plan, rounds, term_rows, flat_grad, own_rows, axes):
    def body(state):
        turn, total = state
        wanted, _ = exchange_wanted(plan, turn, axes)
        return turn + 1, total + send_rows(plan, turn, wanted, flat_grad, own_rows, axes)

    return lax.while_loop(lambda state: state[0] < rounds, body, (jnp.int32(1), term_rows))[1]


def layer_forward(layer_inputs, lengths, matrices, vector_params):
    qkv_low, out_low, up_low, down_low = matrices
    row_width = layer_inputs.shape[2]
    flat_in = layer_inputs.reshape(-1, row_width)
    flat_low = flat_in.astype(jnp.bfloat16)
    qkv_bias = jnp.concatenate(
        [vector_params[2], jnp.zeros_like(vector_params[2]), vector_params[3]]
    )
    packed = (dense(flat_low, qkv_low) + qkv_bias).astype(jnp.bfloat16)
    mixed_output = attend(lengths, packed)
    joined_one = flat_in + (dense(mixed_output, out_low) + vector_params[4])
    first_normed = norm_rows(joined_one, vector_params[5], vector_params[6])
    normed_low = first_normed.astype(jnp.bfloat16)
    hidden_state = dense(normed_low, up_low) + vector_params[10:14].reshape(-1)
    gelu_activated = (hidden_state * normal_cdf(hidden_state)).astype(jnp.bfloat16)
    joined_two = first_normed + (dense(gelu_activated, down_low) + vector_params[7])
    result = norm_rows(joined_two, vector_params[8], vector_params[9]).reshape(layer_inputs.shape)
    saved_state = (
        flat_low,
        packed,
        mixed_output,
        joined_one,
        normed_low,
        hidden_state,
        gelu_activated,
        joined_two,
    )
    return (result, saved_state)


def layer_backward(grad_out, lengths, matrices, vector_params, saved_state):
    qkv_low, out_low, up_low, down_low = matrices
    (
        flat_low,
        packed,
        mixed_output,
        joined_one,
        normed_low,
        hidden_state,
        gelu_activated,
        joined_two,
    ) = saved_state
    row_width = flat_low.shape[1]
    _, back_two = jax.vjp(norm_rows, joined_two, vector_params[8], vector_params[9])
    grad_joined_two, gain_two, shift_two = back_two(grad_out)
    grad_feed = grad_joined_two.astype(jnp.bfloat16)
    grad_hidden = (dense_nt(grad_feed, down_low) * gelu_slope(hidden_state)).astype(jnp.bfloat16)
    down_grad = dense_tn(gelu_activated, grad_feed).astype(jnp.bfloat16)
    up_grad = dense_tn(normed_low, grad_hidden).astype(jnp.bfloat16)
    grad_normed = grad_joined_two + dense_nt(grad_hidden, up_low)
    _, back_one = jax.vjp(norm_rows, joined_one, vector_params[5], vector_params[6])
    grad_joined_one, gain_one, shift_one = back_one(grad_normed)
    grad_attention = grad_joined_one.astype(jnp.bfloat16)
    grad_mixed = dense_nt(grad_attention, out_low).astype(jnp.bfloat16)
    out_grad = dense_tn(mixed_output, grad_attention).astype(jnp.bfloat16)
    grad_mixed, down_grad, up_grad, out_grad = lax.optimization_barrier(
        (grad_mixed, down_grad, up_grad, out_grad)
    )
    down_sum, up_sum, out_sum = [sum_to_owners(g) for g in (down_grad, up_grad, out_grad)]
    grad_packed = jnp.concatenate(attend(lengths, packed, grad_mixed), axis=1)
    grad_inputs = grad_joined_one + dense_nt(grad_packed, qkv_low)
    matrix_grads = (
        dense_tn(flat_low, grad_packed).astype(jnp.bfloat16),
        out_sum,
        up_sum,
        down_sum,
    )
    packed_sum = jnp.sum(grad_packed, axis=0, dtype=jnp.float32)
    vector_rows = jnp.stack(
        [
            packed_sum[:row_width],
            packed_sum[2 * row_width :],
            jnp.sum(grad_attention, axis=0, dtype=jnp.float32),
            gain_one,
            shift_one,
            jnp.sum(grad_feed, axis=0, dtype=jnp.float32),
            gain_two,
            shift_two,
        ]
    )
    up_rows = jnp.sum(grad_hidden, axis=0, dtype=jnp.float32).reshape(4, row_width)
    return (grad_inputs, matrix_grads, jnp.concatenate([vector_rows, up_rows]))


def on_device(
    token_ids,
    true_mask,
    keep_layer,
    picked,
    teacher_hidden,
    teacher_logits,
    embed_table,
    pos_table,
    query_key_value_weight,
    output_weight,
    up_weight,
    down_weight,
    gains_biases,
    first_embed,
    first_pos,
    first_qkv,
    first_out,
    first_up,
    first_down,
    first_gains,
    second_embed,
    second_pos,
    second_qkv,
    second_out,
    second_up,
    second_down,
    second_gains,
):
    axes = AXES
    n_dp, n_fs = lax.axis_size(SPLIT), lax.axis_size("fsdp")
    n_dev = n_dp * n_fs
    i_fs = lax.axis_index("fsdp")
    masters = (
        embed_table,
        pos_table,
        query_key_value_weight,
        output_weight,
        up_weight,
        down_weight,
        gains_biases,
    )
    firsts = (first_embed, first_pos, first_qkv, first_out, first_up, first_down, first_gains)
    seconds = (
        second_embed,
        second_pos,
        second_qkv,
        second_out,
        second_up,
        second_down,
        second_gains,
    )
    seq_count, seq_len = token_ids.shape
    own_rows, row_width = embed_table.shape
    ff = up_weight.shape[1]
    in_rows = query_key_value_weight.shape[0]
    n_tok = seq_count * seq_len
    n_pick = picked.shape[0] * picked.shape[1]
    vocab = own_rows * n_dev
    block_rows = own_rows * n_fs

    table_low = embed_table.astype(jnp.bfloat16)
    pack_width = 3 * row_width + row_width + ff + ff + seq_len
    gain_width = -(-14 // 128) * 128
    packed_low = jnp.concatenate(
        [
            query_key_value_weight,
            output_weight,
            up_weight,
            down_weight.reshape(in_rows, ff),
            pos_table.T,
            jnp.pad(gains_biases.T, ((0, 0), (0, gain_width - 14))),
        ],
        axis=1,
    ).astype(jnp.bfloat16)
    gathered = lax.all_gather(packed_low, axes, axis=0, tiled=True)
    qkv_full = gathered[:, : 3 * row_width]
    out_full = gathered[:, 3 * row_width : 4 * row_width]
    up_full = gathered[:, 4 * row_width : 4 * row_width + ff]
    down_full = gathered[:, 4 * row_width + ff : 4 * row_width + 2 * ff].reshape(ff, row_width)
    pos_full = gathered[:, 4 * row_width + 2 * ff : pack_width].astype(jnp.float32).T
    vector_params = gathered[:, pack_width : pack_width + 14].astype(jnp.float32).T
    matrices = (qkv_full, out_full, up_full, down_full)

    plan = route_plan(token_ids.reshape(-1), true_mask.reshape(-1) > 0, own_rows, n_dev)
    wanted, rounds = exchange_wanted(plan, 0, axes)
    token_rows = fetch_rows(plan, 0, wanted, table_low, axes)
    token_rows = more_rows(plan, rounds, token_rows, table_low, axes)

    padded = -(-own_rows // 16) * 16
    targets = parcels_of(teacher_logits.reshape(n_pick, vocab), own_rows, padded, n_dev)
    targets = lax.all_to_all(
        targets.reshape(n_dp, n_fs, n_pick, padded), SPLIT, split_axis=0, concat_axis=0
    )
    ring = [(z, (z + 1) % n_fs) for z in range(n_fs)]
    tables = [jnp.pad(table_low, ((0, padded - own_rows), (0, 0)))]
    for _ in range(n_fs - 1):
        tables.append(lax.ppermute(tables[-1], "fsdp", ring))
    places = lax.rem(i_fs - jnp.arange(n_fs, dtype=jnp.int32) + n_fs, n_fs)

    embedded = token_rows.reshape(seq_count, seq_len, row_width) + pos_full[None]
    layer_inputs = norm_rows(embedded, vector_params[0], vector_params[1])
    lengths = jnp.sum(true_mask, axis=1) * (keep_layer > 0)
    layer_out, saved_state = layer_forward(layer_inputs, lengths, matrices, vector_params)
    keep_rows = (keep_layer > 0)[:, None, None]
    final_rows = jnp.where(keep_rows, layer_out, layer_inputs)
    weighted = true_mask.astype(jnp.float32)[:, :, None]
    hidden_gap = final_rows - teacher_hidden.astype(jnp.float32)
    loss_part = jnp.sum(weighted * hidden_gap * hidden_gap)
    grad_final = 2.0 * weighted * hidden_gap
    pick_hot = (picked[:, :, None] == jnp.arange(seq_len)[None, None, :]).astype(jnp.bfloat16)
    chosen = (
        jnp.einsum(
            "spt,std->spd",
            pick_hot,
            final_rows.astype(jnp.bfloat16),
            preferred_element_type=jnp.float32,
        )
        .reshape(-1, row_width)
        .astype(jnp.bfloat16)
    )
    all_chosen = lax.all_to_all(
        jnp.broadcast_to(chosen[None], (n_dp,) + chosen.shape), SPLIT, split_axis=0, concat_axis=0
    ).reshape(n_dp * n_pick, row_width)
    slopes, chosen_part, head_loss = head_products(places, all_chosen, targets, tables)
    loss_part = loss_part + jnp.sum(head_loss)
    grad_chosen = lax.all_to_all(
        chosen_part.reshape(n_dp, n_pick, row_width), SPLIT, split_axis=0, concat_axis=0
    )
    order = [step for step in range(1, n_fs)] + [0]
    head_parts = [dense_tn(slopes[step], all_chosen) for step in order]
    grad_chosen, *head_parts = lax.optimization_barrier((grad_chosen, *head_parts))
    grad_chosen = jnp.sum(grad_chosen.astype(jnp.float32), axis=0)
    head_sum = head_parts[0]
    for part in head_parts[1:]:
        moved = lax.ppermute(head_sum.astype(jnp.bfloat16), "fsdp", ring)
        head_sum = moved.astype(jnp.float32) + part
    head_sum = head_sum[:own_rows]

    grad_hot = grad_chosen.reshape(seq_count, -1, row_width)
    grad_high = grad_hot.astype(jnp.bfloat16)
    grad_rest = (grad_hot - grad_high.astype(jnp.float32)).astype(jnp.bfloat16)
    for piece in (grad_high, grad_rest):
        grad_final = grad_final + jnp.einsum(
            "spt,spd->std", pick_hot, piece, preferred_element_type=jnp.float32
        )
    grad_layer = jnp.where(keep_rows, grad_final, 0.0)
    grad_inputs, matrix_grads, vector_grads = layer_backward(
        grad_layer.reshape(-1, row_width), lengths, matrices, vector_params, saved_state
    )
    grad_inputs = jnp.where(keep_rows, 0.0, grad_final) + grad_inputs.reshape(grad_final.shape)
    _, back_zero = jax.vjp(norm_rows, embedded, vector_params[0], vector_params[1])
    grad_embedded, gain_zero, shift_zero = back_zero(grad_inputs)
    grad_pos = jnp.sum(grad_embedded, axis=0)
    flat_grad = grad_embedded.reshape(-1, row_width)
    term_rows = send_rows(plan, 0, wanted, flat_grad, own_rows, axes)
    term_rows = more_sent(plan, rounds, term_rows, flat_grad, own_rows, axes)
    table_grad = head_sum + term_rows
    vector_all = jnp.concatenate([jnp.stack([gain_zero, shift_zero]), vector_grads])

    last = sum_to_owners(
        jnp.concatenate(
            [
                matrix_grads[0],
                grad_pos.T.astype(jnp.bfloat16),
                jnp.pad(vector_all.T, ((0, 0), (0, gain_width - 14))).astype(jnp.bfloat16),
            ],
            axis=1,
        )
    )
    out_grad, up_grad, down_grad = matrix_grads[1:]
    reduced = (
        last[:, 3 * row_width : 3 * row_width + seq_len].T,
        last[:, : 3 * row_width],
        out_grad,
        up_grad,
        down_grad,
        last[:, 3 * row_width + seq_len : 3 * row_width + seq_len + 14].T,
    )
    gradients = (table_grad,) + tuple(reduced)
    grad_squares = jnp.stack([jnp.sum(member * member) for member in gradients])
    weight_squares = jnp.stack([jnp.sum(member * member) for member in masters])
    totals = total_over(
        jnp.concatenate(
            [jnp.stack([loss_part, jnp.sum(weighted)]), grad_squares, weight_squares]
        ),
        axes,
    )
    loss_sum, token_count = totals[0], totals[1]
    grad_squares, weight_squares = totals[2:9], totals[9:16]
    grad_norm = jnp.sqrt(jnp.sum(grad_squares)) / token_count
    factor = jnp.minimum(1.0, CLIP_NORM / grad_norm) / token_count
    updates = []
    new_moments = []
    new_squares = []
    for weight, gradient, moment, square in zip(masters, gradients, firsts, seconds):
        clipped = gradient * factor
        moment_new = BETA_ONE * moment + (1.0 - BETA_ONE) * clipped
        square_new = BETA_TWO * square + (1.0 - BETA_TWO) * clipped * clipped
        updates.append(
            moment_new
            / (1.0 - BETA_ONE**STEP)
            / (jnp.sqrt(square_new / (1.0 - BETA_TWO**STEP)) + ADAM_EPS)
            + DECAY_RATE * weight
        )
        new_moments.append(moment_new)
        new_squares.append(square_new)
    update_squares = total_over(
        jnp.stack([jnp.sum(update * update) for update in updates]), axes
    )
    weight_norms = jnp.sqrt(weight_squares)
    update_norms = jnp.sqrt(update_squares)
    ratios = weight_norms / update_norms
    new_weights = [
        weight - LEARN_RATE * ratios[position] * update
        for position, (weight, update) in enumerate(zip(masters, updates))
    ]
    matrix_norms = jnp.stack([weight_norms, update_norms])
    return (
        loss_sum,
        token_count,
        grad_norm,
        new_weights[0],
        new_weights[1],
        new_weights[2],
        new_weights[3],
        new_weights[4],
        new_weights[5],
        new_weights[6],
        new_moments[0],
        new_moments[1],
        new_moments[2],
        new_moments[3],
        new_moments[4],
        new_moments[5],
        new_moments[6],
        new_squares[0],
        new_squares[1],
        new_squares[2],
        new_squares[3],
        new_squares[4],
        new_squares[5],
        new_squares[6],
        matrix_norms,
    )


def solution(mesh):
    split = Mesh(
        mesh.devices.reshape(mesh.shape["dp"] // 2, 2, mesh.shape["fsdp"]), AXES
    )
    placed = (
        P(AXES, None),
        P(AXES, None),
        P(AXES),
        P(AXES, None),
        P(AXES, None, None),
        P(AXES, None, None),
        P(AXES, None),
        P(None, AXES),
        P(AXES, None),
        P(AXES, None),
        P(AXES, None),
        P(AXES, None),
        P(None, AXES),
        P(AXES, None),
        P(None, AXES),
        P(AXES, None),
        P(AXES, None),
        P(AXES, None),
        P(AXES, None),
        P(None, AXES),
        P(AXES, None),
        P(None, AXES),
        P(AXES, None),
        P(AXES, None),
        P(AXES, None),
        P(AXES, None),
        P(None, AXES),
    )
    return jax.shard_map(
        on_device,
        mesh=split,
        in_specs=placed,
        out_specs=(
            P(),
            P(),
            P(),
            P(AXES, None),
            P(None, AXES),
            P(AXES, None),
            P(AXES, None),
            P(AXES, None),
            P(AXES, None),
            P(None, AXES),
            P(AXES, None),
            P(None, AXES),
            P(AXES, None),
            P(AXES, None),
            P(AXES, None),
            P(AXES, None),
            P(None, AXES),
            P(AXES, None),
            P(None, AXES),
            P(AXES, None),
            P(AXES, None),
            P(AXES, None),
            P(AXES, None),
            P(None, AXES),
            P(),
        ),
        check_vma=False,
    )
```

```python
import functools

import jax
import jax.numpy as jnp
from jax import lax
from jax.experimental import pallas as pl
from jax.experimental.pallas import tpu as pltpu
from jax.sharding import Mesh
from jax.sharding import PartitionSpec as P

H = 12
HD = 64
STEP = 10


NORM_EPS = 1e-05
CLIP_NORM = 0.5
BETA_ONE = 0.9
BETA_TWO = 0.999
ADAM_EPS = 1e-06
DECAY_RATE = 0.01
LEARN_RATE = 0.3
MASKED_SCORE = -1e30

SPLIT = ("plane", "pair")
AXES = ("plane", "pair", "fsdp")
VMEM = 60 * 2**20
NO_COST = pl.CostEstimate(flops=0, bytes_accessed=0, transcendentals=0)


def normal_cdf(values):
    return 0.5 + 0.5 * lax.erf(values * 0.5**0.5)


def dense(left_op, right_op):
    return jnp.dot(left_op, right_op, preferred_element_type=jnp.float32)


def dense_tn(left_op, right_op):
    return lax.dot_general(
        left_op, right_op, (((0,), (0,)), ((), ())), preferred_element_type=jnp.float32
    )


def dense_nt(left_op, right_op):
    return lax.dot_general(
        left_op, right_op, (((1,), (1,)), ((), ())), preferred_element_type=jnp.float32
    )


def pair_lanes(shape, member):
    lane = lax.broadcasted_iota(jnp.int32, shape, 1)
    return (lane >= HD) if member else (lane < HD)


def softmax_rows(query_rows, key_rows, length):
    scores = dense_nt(query_rows, key_rows)
    spot = lax.broadcasted_iota(jnp.int32, scores.shape, 1)
    scores = jnp.where(spot < length, scores, MASKED_SCORE)
    exponent = jnp.exp(scores - jnp.max(scores, axis=1, keepdims=True))
    return exponent / jnp.sum(exponent, axis=1, keepdims=True)


def row_spans(seq_len):
    half = seq_len // 2
    return ((0, half), (half, seq_len))


def mix_kernel(length_ref, query_ref, key_ref, value_ref, mixed_ref):
    seq_len = query_ref.shape[0]
    length = length_ref[pl.program_id(0)]

    for low, high in row_spans(seq_len):

        @pl.when((length > low) & (length <= high))
        def _():
            step = high // 2 if low else high
            keys, values = key_ref[0:high, :], value_ref[0:high, :]
            for row in range(0, high, step):
                queries = query_ref[row : row + step, :] * 0.125
                parts = []
                for member in (0, 1):
                    lanes = pair_lanes(queries.shape, member)
                    chance = softmax_rows(
                        jnp.where(lanes, queries, jnp.zeros_like(queries)), keys, length
                    )
                    parts.append(dense(chance.astype(jnp.bfloat16), values))
                mixed_ref[row : row + step, :] = jnp.where(
                    pair_lanes(parts[0].shape, 1), parts[1], parts[0]
                ).astype(jnp.bfloat16)
            if high < seq_len:
                mixed_ref[high:, :] = jnp.zeros((seq_len - high, 2 * HD), jnp.bfloat16)

    @pl.when(length == 0)
    def _():
        mixed_ref[...] = jnp.zeros_like(mixed_ref)


def unmix_kernel(
    length_ref, query_ref, key_ref, value_ref, grad_ref, query_out, key_out, value_out
):
    seq_len = query_ref.shape[0]
    length = length_ref[pl.program_id(0)]
    outs = (query_out, key_out, value_out)

    for low, high in row_spans(seq_len):

        @pl.when((length > low) & (length <= high))
        def _():
            step = high // 2 if low else high
            keys, values = key_ref[0:high, :], value_ref[0:high, :]
            key_total, value_total = None, None
            for row in range(0, high, step):
                plain = query_ref[row : row + step, :]
                queries = plain * 0.125
                grads = grad_ref[row : row + step, :]
                parts = []
                for member in (0, 1):
                    lanes = pair_lanes(queries.shape, member)
                    zero = jnp.zeros_like(queries)
                    chance = softmax_rows(jnp.where(lanes, queries, zero), keys, length)
                    slope = dense_nt(jnp.where(lanes, grads, zero), values)
                    slope = chance * (slope - jnp.sum(slope * chance, axis=1, keepdims=True))
                    slope = slope.astype(jnp.bfloat16)
                    parts.append(
                        (
                            dense(slope, keys),
                            dense_tn(slope, plain),
                            dense_tn(chance.astype(jnp.bfloat16), grads),
                        )
                    )
                query_part, key_part, value_part = [
                    jnp.where(pair_lanes(first.shape, 1), second, first)
                    for first, second in zip(*parts)
                ]
                query_out[row : row + step, :] = (query_part * 0.125).astype(jnp.bfloat16)
                key_total = key_part if key_total is None else key_total + key_part
                value_total = value_part if value_total is None else value_total + value_part
            key_out[0:high, :] = (key_total * 0.125).astype(jnp.bfloat16)
            value_out[0:high, :] = value_total.astype(jnp.bfloat16)
            if high < seq_len:
                for ref in outs:
                    ref[high:, :] = jnp.zeros((seq_len - high, 2 * HD), jnp.bfloat16)

    @pl.when(length == 0)
    def _():
        for ref in outs:
            ref[...] = jnp.zeros_like(ref)


def attend(lengths, packed, grad_mixed=None):
    seq_count = lengths.shape[0]
    seq_len = packed.shape[0] // seq_count
    pairs = H // 2

    def block(first):
        return pl.BlockSpec((seq_len, 2 * HD), lambda s, h, _: (s, first + h))

    out = jax.ShapeDtypeStruct((packed.shape[0], H * HD), jnp.bfloat16)
    forward = grad_mixed is None
    operands = (packed, packed, packed) + (() if forward else (grad_mixed,))
    return pl.pallas_call(
        mix_kernel if forward else unmix_kernel,
        out_shape=out if forward else (out, out, out),
        grid_spec=pltpu.PrefetchScalarGridSpec(
            num_scalar_prefetch=1,
            grid=(seq_count, pairs),
            in_specs=[block(0), block(pairs), block(2 * pairs)] + ([] if forward else [block(0)]),
            out_specs=block(0) if forward else (block(0),) * 3,
        ),
        compiler_params=pltpu.CompilerParams(vmem_limit_bytes=VMEM),
        cost_estimate=NO_COST,
    )(lengths, *operands)


def norm_parts(values):
    centered = values - jnp.mean(values, axis=1, keepdims=True)
    spread = lax.rsqrt(jnp.mean(centered * centered, axis=1, keepdims=True) + NORM_EPS)
    return centered * spread, spread


def norm_back(grads, unit_rows, spread, gain_row):
    scaled = grads * gain_row
    inner = jnp.mean(scaled * unit_rows, axis=1, keepdims=True)
    rows = spread * (scaled - jnp.mean(scaled, axis=1, keepdims=True) - unit_rows * inner)
    return rows, eight_rows(grads * unit_rows), eight_rows(grads)


def eight_rows(values):
    return jnp.sum(values.reshape(-1, 8, values.shape[1]), axis=0)


def picks_hot(picked_ref, first_row, rows):
    spot = lax.broadcasted_iota(jnp.int32, (picked_ref.shape[0], rows), 1) + first_row
    return (picked_ref[...] == spot).astype(jnp.bfloat16)


def enter_kernel(
    length_ref, token_ref, place_ref, vector_ref, weight_ref, embedded_ref, input_ref, low_ref, packed_ref
):
    block, seq = pl.program_id(0), pl.program_id(1)
    rows = token_ref.shape[0]
    vectors = vector_ref[...].astype(jnp.float32).T
    embedded = token_ref[...] + place_ref[...].astype(jnp.float32).T
    embedded_ref[...] = embedded
    inputs = norm_parts(embedded)[0] * vectors[0:1] + vectors[1:2]
    input_ref[...] = inputs
    low = inputs.astype(jnp.bfloat16)
    low_ref[...] = low

    @pl.when(length_ref[seq] > block * rows)
    def _():
        width = low.shape[1]
        for part, bias in enumerate((vectors[2:3], None, vectors[3:4])):
            columns = slice(part * width, (part + 1) * width)
            values = dense(low, weight_ref[:, columns])
            if bias is not None:
                values = values + bias
            packed_ref[:, columns] = values.astype(jnp.bfloat16)


def feed_kernel(
    length_ref,
    true_ref,
    mixed_ref,
    input_ref,
    teacher_ref,
    picked_ref,
    vector_ref,
    bias_ref,
    out_ref,
    up_ref,
    down_ref,
    joined_one_ref,
    normed_ref,
    slope_ref,
    active_ref,
    joined_two_ref,
    grad_ref,
    chosen_ref,
    loss_ref,
    final_ref,
):
    seq, block = pl.program_id(0), pl.program_id(1)
    rows, width = mixed_ref.shape
    alive = length_ref[seq] > block * rows
    final_ref[...] = input_ref[...]

    @pl.when(alive)
    def _():
        vectors = vector_ref[...].astype(jnp.float32).T
        joined = input_ref[...] + (dense(mixed_ref[...], out_ref[...]) + vectors[4:5])
        joined_one_ref[...] = joined
        normed = norm_parts(joined)[0] * vectors[5:6] + vectors[6:7]
        low = normed.astype(jnp.bfloat16)
        normed_ref[...] = low
        fed = None
        for column in range(0, up_ref.shape[1], width):
            columns = slice(column, column + width)
            hidden = dense(low, up_ref[:, columns]) + bias_ref[:, columns]
            share = normal_cdf(hidden)
            density = jnp.exp(-0.5 * hidden * hidden) * (2.0 * jnp.pi) ** -0.5
            slope_ref[:, columns] = (share + hidden * density).astype(jnp.bfloat16)
            active = (hidden * share).astype(jnp.bfloat16)
            active_ref[:, columns] = active
            part = dense(active, down_ref[:, columns])
            fed = part if fed is None else fed + part
        joined = normed + (fed + vectors[7:8])
        joined_two_ref[...] = joined
        final_ref[...] = norm_parts(joined)[0] * vectors[8:9] + vectors[9:10]

    @pl.when(jnp.logical_not(alive))
    def _():
        normed_ref[...] = jnp.zeros_like(normed_ref)
        active_ref[...] = jnp.zeros_like(active_ref)

    final = final_ref[...]
    row = lax.broadcasted_iota(jnp.int32, final.shape, 0) + block * rows
    gap = jnp.where(row < true_ref[seq], final - teacher_ref[...].astype(jnp.float32), 0.0)
    grad_ref[...] = 2.0 * gap
    hot = picks_hot(picked_ref, block * rows, rows)
    chosen = dense(hot, final.astype(jnp.bfloat16)).astype(jnp.bfloat16)

    @pl.when(block == 0)
    def _():
        chosen_ref[...] = chosen

    @pl.when(block > 0)
    def _():
        chosen_ref[...] += chosen

    @pl.when((block == 0) & (seq == 0))
    def _():
        loss_ref[...] = jnp.zeros_like(loss_ref)

    loss_ref[...] += eight_rows(gap * gap)


def unfeed_kernel(
    length_ref,
    grad_ref,
    head_ref,
    picked_ref,
    joined_one_ref,
    slope_ref,
    joined_two_ref,
    vector_ref,
    out_ref,
    up_ref,
    down_ref,
    final_ref,
    joined_out,
    mixed_out,
    attention_out,
    feed_out,
    hidden_out,
    sums_ref,
    hidden_sum_ref,
):
    seq, block = pl.program_id(0), pl.program_id(1)
    rows, width = grad_ref.shape
    alive = length_ref[seq] > block * rows
    head = jnp.sum(head_ref[...].astype(jnp.float32), axis=0)
    high = head.astype(jnp.bfloat16)
    rest = (head - high.astype(jnp.float32)).astype(jnp.bfloat16)
    hot = picks_hot(picked_ref, block * rows, rows)
    grads = grad_ref[...] + dense_tn(hot, high) + dense_tn(hot, rest)
    final_ref[...] = grads

    @pl.when((block == 0) & (seq == 0))
    def _():
        sums_ref[...] = jnp.zeros_like(sums_ref)
        hidden_sum_ref[...] = jnp.zeros_like(hidden_sum_ref)

    @pl.when(alive)
    def _():
        vectors = vector_ref[...].astype(jnp.float32).T
        unit_rows, spread = norm_parts(joined_two_ref[...])
        grad_two, gain_two, shift_two = norm_back(grads, unit_rows, spread, vectors[8:9])
        feed = grad_two.astype(jnp.bfloat16)
        feed_out[...] = feed
        back = grad_two
        for column in range(0, up_ref.shape[1], width):
            columns = slice(column, column + width)
            hidden = dense_nt(feed, down_ref[:, columns])
            hidden = (hidden * slope_ref[:, columns].astype(jnp.float32)).astype(jnp.bfloat16)
            hidden_out[:, columns] = hidden
            hidden_sum_ref[:, columns] += eight_rows(hidden.astype(jnp.float32))
            back = back + dense_nt(hidden, up_ref[:, columns])
        unit_rows, spread = norm_parts(joined_one_ref[...])
        grad_one, gain_one, shift_one = norm_back(back, unit_rows, spread, vectors[5:6])
        joined_out[...] = grad_one
        attention = grad_one.astype(jnp.bfloat16)
        attention_out[...] = attention
        mixed_out[...] = dense_nt(attention, out_ref[...]).astype(jnp.bfloat16)
        sums_ref[0] += eight_rows(attention.astype(jnp.float32))
        sums_ref[1] += gain_one
        sums_ref[2] += shift_one
        sums_ref[3] += eight_rows(feed.astype(jnp.float32))
        sums_ref[4] += gain_two
        sums_ref[5] += shift_two

    @pl.when(jnp.logical_not(alive))
    def _():
        for ref in (joined_out, mixed_out, attention_out, feed_out, hidden_out):
            ref[...] = jnp.zeros_like(ref)


def leave_kernel(
    length_ref,
    keep_ref,
    query_ref,
    key_ref,
    value_ref,
    joined_ref,
    final_ref,
    embedded_ref,
    vector_ref,
    weight_ref,
    high_ref,
    rest_ref,
    place_ref,
    sums_ref,
    place_sum,
):
    block, seq = pl.program_id(0), pl.program_id(1)
    rows, width = joined_ref.shape
    alive = length_ref[seq] > block * rows
    vectors = vector_ref[...].astype(jnp.float32).T
    dropped = (keep_ref[seq] == 0).astype(jnp.float32)

    @pl.when((block == 0) & (seq == 0))
    def _():
        sums_ref[...] = jnp.zeros_like(sums_ref)

    @pl.when(seq == 0)
    def _():
        place_sum[...] = jnp.zeros_like(place_sum)

    def finish(grads):
        unit_rows, spread = norm_parts(embedded_ref[...])
        grads, gain, shift = norm_back(grads, unit_rows, spread, vectors[0:1])
        sums_ref[0] += gain
        sums_ref[1] += shift
        high = grads.astype(jnp.bfloat16)
        high_ref[...] = high
        rest_ref[...] = (grads - high.astype(jnp.float32)).astype(jnp.bfloat16)
        place_sum[...] += grads

    @pl.when(alive)
    def _():
        grads = joined_ref[...]
        for part, ref in enumerate((query_ref, key_ref, value_ref)):
            grads = grads + dense_nt(ref[...], weight_ref[:, part * width : (part + 1) * width])
        sums_ref[2] += eight_rows(query_ref[...].astype(jnp.float32))
        sums_ref[3] += eight_rows(value_ref[...].astype(jnp.float32))
        finish(grads)

    @pl.when(jnp.logical_not(alive))
    def _():
        finish(final_ref[...] * dropped)

    @pl.when(seq == pl.num_programs(1) - 1)
    def _():
        place_ref[...] = place_sum[...].T.astype(jnp.bfloat16)


def deal_out(product, member_ref, kept_ref, given_ref, halves):
    halves[...] = product.reshape(halves.shape).astype(halves.dtype)
    member = member_ref[0]
    kept_ref[...] = halves[:, member]
    given_ref[...] = halves[:, 1 - member]


def early_kernel(
    member_ref,
    mixed_ref,
    attention_ref,
    normed_ref,
    hidden_ref,
    active_ref,
    feed_ref,
    kept_ref,
    given_ref,
    halves,
):
    place, blocks = pl.program_id(0), pl.num_programs(0) // 2
    cases = (
        (place == 0, mixed_ref, attention_ref),
        ((place > 0) & (place <= blocks), normed_ref, hidden_ref),
        (place > blocks, active_ref, feed_ref),
    )
    for wanted, left_ref, right_ref in cases:

        @pl.when(wanted)
        def _():
            product = dense_tn(left_ref[...], right_ref[...])
            deal_out(product, member_ref, kept_ref, given_ref, halves)


def late_kernel(
    member_ref,
    low_ref,
    query_ref,
    key_ref,
    value_ref,
    place_ref,
    sums_one_ref,
    sums_two_ref,
    up_ref,
    kept_ref,
    given_ref,
    halves,
    columns,
    vectors,
):
    for part, ref in enumerate((query_ref, key_ref, value_ref)):

        @pl.when(pl.program_id(0) == part)
        def _():
            product = dense_tn(low_ref[...], ref[...])
            deal_out(product, member_ref, kept_ref, given_ref, halves)

    @pl.when(pl.program_id(0) == 3)
    def _():
        vectors[...] = jnp.zeros_like(vectors)
        for row in range(4):
            vectors[row : row + 1, :] = jnp.sum(sums_two_ref[row], axis=0, keepdims=True)
        for row in range(6):
            vectors[4 + row : 5 + row, :] = jnp.sum(sums_one_ref[row], axis=0, keepdims=True)
        vectors[10:14, :] = up_ref[...]
        columns[...] = jnp.zeros_like(columns)
        width = place_ref.shape[1]
        columns[:, :width] = place_ref[...].astype(jnp.float32)
        columns[:, width : width + vectors.shape[0]] = vectors[...].T
        deal_out(columns[...], member_ref, kept_ref, given_ref, halves)


def head_grad_kernel(slope_ref, last_ref, chosen_ref, grad_ref):
    @pl.when(pl.program_id(0) != pl.num_programs(0) - 2)
    def _():
        grad_ref[0] = dense_tn(slope_ref[0], chosen_ref[...]).astype(grad_ref.dtype)

    @pl.when(pl.program_id(0) == pl.num_programs(0) - 2)
    def _():
        grad_ref[0] = dense_tn(last_ref[0], chosen_ref[...]).astype(grad_ref.dtype)


def head_first_kernel(slope_ref, chosen_ref, grad_ref):
    grad_ref[...] = dense_tn(slope_ref[0], chosen_ref[...]).astype(grad_ref.dtype)


def row_kernel(kernel, prefetch, operands, outs, grid, scratch=()):
    return pl.pallas_call(
        kernel,
        out_shape=tuple(jax.ShapeDtypeStruct(shape, kind) for shape, kind, _, _ in outs),
        grid_spec=pltpu.PrefetchScalarGridSpec(
            num_scalar_prefetch=len(prefetch),
            grid=grid,
            in_specs=[pl.BlockSpec(block, where) for _, block, where in operands],
            out_specs=tuple(pl.BlockSpec(block, where) for _, _, block, where in outs),
            scratch_shapes=list(scratch),
        ),
        compiler_params=pltpu.CompilerParams(vmem_limit_bytes=VMEM),
        cost_estimate=NO_COST,
    )(*prefetch, *[array for array, _, _ in operands])


def parcel_kernel(own_rows, tiles, wide, source, parcel_ref, slots, sems):
    part, parts = pl.program_id(0), pl.num_programs(0)

    def first_tile(index):
        return jnp.minimum(own_rows * index // 128, tiles - wide)

    def fetch(index):
        lane = pl.multiple_of(first_tile(index) * 128, 128)
        slot = lax.rem(index, 2)
        return pltpu.make_async_copy(
            source.at[:, pl.ds(lane, wide * 128)],
            slots.at[slot, :, pl.ds(0, wide * 128)],
            sems.at[slot],
        )

    @pl.when(part == 0)
    def _():
        fetch(0).start()

    @pl.when(part + 1 < parts)
    def _():
        fetch(part + 1).start()

    fetch(part).wait()
    shift = own_rows * part - 128 * first_tile(part)
    slot, skip, turn = lax.rem(part, 2), shift // 128, lax.rem(128 - lax.rem(shift, 128), 128)
    n_pick, width = parcel_ref.shape[1:]
    lane = lax.broadcasted_iota(jnp.int32, (n_pick, 128), 1)

    def turned(tile):
        start = pl.multiple_of((tile + skip) * 128, 128)
        values = slots[slot, :, pl.ds(start, 128)].astype(jnp.float32)
        return pltpu.roll(values, turn, axis=1)

    low = turned(0)
    for tile in range(width // 128):
        high = turned(tile + 1)
        values = jnp.where(lane < 128 - lax.rem(shift, 128), low, high)
        values = jnp.where(lane + 128 * tile < own_rows, values, 0.0)
        parcel_ref[0, :, 128 * tile : 128 * (tile + 1)] = values.astype(jnp.bfloat16)
        low = high


def parcels_of(flat_teacher, own_rows, lanes, n_dev):
    n_pick, vocab = flat_teacher.shape
    tiles = vocab // 128
    wide = min(tiles, lanes // 128 + 1)
    return pl.pallas_call(
        functools.partial(parcel_kernel, own_rows, tiles, wide),
        out_shape=jax.ShapeDtypeStruct((n_dev, n_pick, lanes), jnp.bfloat16),
        grid=(n_dev,),
        in_specs=[pl.BlockSpec(memory_space=pl.ANY)],
        out_specs=pl.BlockSpec((1, n_pick, lanes), lambda r: (r, 0, 0)),
        scratch_shapes=[
            pltpu.VMEM((2, n_pick, (wide + 2) * 128), jnp.bfloat16),
            pltpu.SemaphoreType.DMA((2,)),
        ],
        compiler_params=pltpu.CompilerParams(vmem_limit_bytes=VMEM),
        cost_estimate=NO_COST,
    )(flat_teacher)


def head_kernel(steps, place_ref, chosen_ref, target_ref, *refs):
    tables = refs[:steps]
    before = refs[steps:-3]
    slope_ref, part_ref, loss_ref = refs[-3:]
    chosen = chosen_ref[...]
    senders, _, n_pick, _ = target_ref.shape
    total, loss = before[0][...] if before else None, None
    for step in range(steps):
        table = tables[step][...]
        width = table.shape[0]
        target = target_ref[:, place_ref[step]].reshape(senders * n_pick, -1)[:, :width]
        gap = dense_nt(chosen, table) - target.astype(jnp.float32)
        square = jnp.sum((gap * gap).reshape(-1, 8, width), axis=0)
        loss = square if loss is None else loss + square
        slope = (2.0 * gap).astype(jnp.bfloat16)
        slope_ref[step] = slope
        part = dense(slope, table)
        total = part if total is None else total + part
    part_ref[...] = total.astype(part_ref.dtype)

    @pl.when(pl.program_id(0) == 0)
    def _():
        loss_ref[...] = jnp.zeros_like(loss_ref)

    loss_ref[...] += loss


def head_products(places, all_chosen, targets, tables, before, part_type):
    n_dp, n_fs, n_pick, lanes = targets.shape
    row_width = all_chosen.shape[1]
    padded = tables[0].shape[0]
    rows, steps = 2 * n_pick, len(tables)
    whole = pl.BlockSpec((padded, row_width), lambda m, _: (0, 0))
    some = pl.BlockSpec((rows, row_width), lambda m, _: (m, 0))
    return pl.pallas_call(
        functools.partial(head_kernel, steps),
        out_shape=(
            jax.ShapeDtypeStruct((steps, n_dp * n_pick, padded), jnp.bfloat16),
            jax.ShapeDtypeStruct((n_dp * n_pick, row_width), part_type),
            jax.ShapeDtypeStruct((8, padded), jnp.float32),
        ),
        grid_spec=pltpu.PrefetchScalarGridSpec(
            num_scalar_prefetch=1,
            grid=(n_dp // 2,),
            in_specs=[
                some,
                pl.BlockSpec((2, n_fs, n_pick, lanes), lambda m, _: (m, 0, 0, 0)),
            ]
            + [whole] * steps
            + [some] * len(before),
            out_specs=(
                pl.BlockSpec((steps, rows, padded), lambda m, _: (0, m, 0)),
                some,
                pl.BlockSpec((8, padded), lambda m, _: (0, 0)),
            ),
        ),
        compiler_params=pltpu.CompilerParams(vmem_limit_bytes=VMEM),
        cost_estimate=NO_COST,
    )(places, all_chosen, targets, *tables, *before)


def sum_over_peers(part, axis):
    size, me = lax.axis_size(axis), lax.axis_index(axis)
    arrived = [lax.dynamic_index_in_dim(part, me, 0, False).astype(jnp.float32)]
    for apart in range(1, size):
        given = lax.dynamic_index_in_dim(part, me ^ apart, 0, False)
        got = lax.ppermute(given, axis, [(peer, peer ^ apart) for peer in range(size)])
        arrived.append(got.astype(jnp.float32))
    return sum(arrived)


def sum_in_pair(kept, given):
    got = lax.ppermute(given, "pair", [(0, 1), (1, 0)])
    return (kept.astype(jnp.float32) + got.astype(jnp.float32)).astype(jnp.bfloat16)


def sum_in_plane(part):
    part = sum_over_peers(part, "plane").astype(jnp.bfloat16)
    return part.reshape(lax.axis_size("fsdp"), -1, part.shape[-1])


def sum_in_line(part):
    return sum_over_peers(part, "fsdp")


def route_plan(ids, live, own_rows, n_dev):
    place = jnp.arange(ids.shape[0])
    owner = ids // own_rows
    same = (ids[:, None] == ids[None, :]) & live[None, :]
    leader = jnp.min(jnp.where(same, place[None, :], ids.shape[0]), axis=1)
    first = live & (leader == place)
    before = (owner[:, None] == owner[None, :]) & (place[None, :] < leader[:, None])
    rank = jnp.sum(before & first[None, :], axis=1, dtype=jnp.int32)
    room = max(16, 1280 // n_dev)
    rounds = jnp.max(jnp.where(first, rank, 0)) // room + 1
    return ids, live, owner, first, rank, room, rounds, own_rows, n_dev


def slots_of(plan, turn):
    ids, live, owner, first, rank, room, rounds, own_rows, n_dev = plan
    here = live & (rank >= turn * room) & (rank < (turn + 1) * room)
    return jnp.where(here, owner * room + rank - turn * room, -1)


def exchange_wanted(plan, turn, axes):
    ids, live, owner, first, rank, room, rounds, own_rows, n_dev = plan
    slots = slots_of(plan, turn)
    local = jnp.where(first, ids - owner * own_rows + 1, 0)
    hit = jnp.arange(n_dev * room)[:, None] == slots[None, :]
    asked = jnp.max(jnp.where(hit, local[None, :], 0), axis=1) - 1
    message = jnp.concatenate(
        [
            asked.reshape(n_dev, room),
            jnp.broadcast_to(rounds, (n_dev, 128 - room)).astype(jnp.int32),
        ],
        axis=1,
    ).reshape(n_dev, 1, 128)
    heard = lax.all_to_all(message, axes, split_axis=0, concat_axis=0).reshape(n_dev, 128)
    return heard[:, :room].reshape(-1), jnp.max(heard[:, room:])


def ask_rows(plan, wanted, table_low, axes):
    room, own_rows, n_dev = plan[5], plan[7], plan[8]
    one_hot = (wanted[:, None] == jnp.arange(own_rows)[None, :]).astype(jnp.bfloat16)
    rows = dense(one_hot, table_low).astype(jnp.bfloat16)
    return lax.all_to_all(rows.reshape(n_dev, room, -1), axes, split_axis=0, concat_axis=0)


def place_rows(plan, turn, rows):
    room, n_dev = plan[5], plan[8]
    back = (slots_of(plan, turn)[:, None] == jnp.arange(n_dev * room)[None, :]).astype(
        jnp.bfloat16
    )
    return dense(back, rows.reshape(n_dev * room, -1))


def more_rows(plan, rounds, token_rows, table_low, axes):
    def body(state):
        turn, total = state
        wanted, _ = exchange_wanted(plan, turn, axes)
        rows = ask_rows(plan, wanted, table_low, axes)
        return turn + 1, total + place_rows(plan, turn, rows)

    return lax.while_loop(lambda state: state[0] < rounds, body, (jnp.int32(1), token_rows))[1]


def rows_to_give(plan, turn, flat_grad):
    room, n_dev = plan[5], plan[8]
    spread = (jnp.arange(n_dev * room)[:, None] == slots_of(plan, turn)[None, :]).astype(
        jnp.bfloat16
    )
    high, rest = flat_grad
    sums = (dense(spread, high) + dense(spread, rest)).astype(jnp.bfloat16)
    return sums.reshape(n_dev, room, -1)


def give_rows(sums, axes):
    got = lax.all_to_all(sums, axes, split_axis=0, concat_axis=0)
    return got.reshape(-1, sums.shape[-1])


def more_given(plan, rounds, flat_grad, own_rows, axes):
    def body(state):
        turn, total = state
        wanted, _ = exchange_wanted(plan, turn, axes)
        one_hot = (jnp.arange(own_rows)[:, None] == wanted[None, :]).astype(jnp.bfloat16)
        got = give_rows(rows_to_give(plan, turn, flat_grad), axes)
        return turn + 1, total + dense(one_hot, got)

    nothing = jnp.zeros((own_rows, flat_grad[0].shape[1]), jnp.float32)
    return lax.while_loop(lambda state: state[0] < rounds, body, (jnp.int32(1), nothing))[1]


def at_lane(tile, lane, value):
    row = lax.broadcasted_iota(jnp.int32, tile.shape, 0)
    column = lax.broadcasted_iota(jnp.int32, tile.shape, 1)
    return tile + jnp.where((row == 0) & (column == lane), value, 0.0)


def total_sum(values):
    return jnp.sum(jnp.sum(values, axis=0, keepdims=True), axis=1, keepdims=True)


def table_kernel(
    own_rows,
    wanted_ref,
    returned_ref,
    extra_ref,
    moved_ref,
    part_ref,
    tile_ref,
    out_ref,
    up_ref,
    down_ref,
    last_ref,
    grad_ref,
    place_ref,
    qkv_ref,
    vector_ref,
    sum_ref,
):
    rows = grad_ref.shape[0]
    first = pl.program_id(0) * rows
    spot = lax.broadcasted_iota(jnp.int32, (rows, wanted_ref.shape[1]), 0) + first
    hot = (spot == wanted_ref[...]).astype(jnp.bfloat16)
    grads = dense(hot, returned_ref[...]) + extra_ref[...]
    grads = grads + (moved_ref[...].astype(jnp.float32) + part_ref[0].astype(jnp.float32))
    row = lax.broadcasted_iota(jnp.int32, grads.shape, 0) + first
    grads = jnp.where(row < own_rows, grads, 0.0)
    grad_ref[...] = grads

    @pl.when(pl.program_id(0) == 0)
    def _():
        sum_ref[...] = tile_ref[...]
        wide, places = qkv_ref.shape[1], place_ref.shape[1]
        qkv_ref[...] = last_ref[:, :wide]
        place_ref[...] = last_ref[:, wide : wide + places]
        vectors = last_ref[:, wide + places : wide + places + 128].T
        vector_ref[...] = vectors[: vector_ref.shape[0], :]
        for other in (out_ref, up_ref, down_ref, place_ref, qkv_ref, vector_ref):
            sum_ref[...] = at_lane(sum_ref[...], 0, total_sum(other[...] * other[...]))

    sum_ref[...] = at_lane(sum_ref[...], 0, total_sum(grads * grads))


def update_kernel(own_rows, every_ref, *refs):
    weights, grads, firsts, seconds = [refs[7 * k : 7 * k + 7] for k in range(4)]
    moments, squares, updates = [refs[7 * k : 7 * k + 7] for k in range(4, 7)]
    total_ref, sum_ref = refs[49:]
    totals = jnp.sum(every_ref[...], axis=0)
    count = totals[0:1, 2:3]
    norm = jnp.sqrt(totals[0:1, 0:1]) / count
    factor = jnp.minimum(1.0, CLIP_NORM / norm) / count

    def step(place, live=None):
        weight = weights[place][...]
        clipped = grads[place][...] * factor
        moment = BETA_ONE * firsts[place][...] + (1.0 - BETA_ONE) * clipped
        square = BETA_TWO * seconds[place][...] + (1.0 - BETA_TWO) * clipped * clipped
        update = (
            moment
            * (1.0 / (1.0 - BETA_ONE**STEP))
            / (jnp.sqrt(square * (1.0 / (1.0 - BETA_TWO**STEP))) + ADAM_EPS)
            + DECAY_RATE * weight
        )
        moments[place][...] = moment
        squares[place][...] = square
        updates[place][...] = update
        if live is not None:
            update = jnp.where(live, update, 0.0)
        sum_ref[...] = at_lane(sum_ref[...], place, total_sum(update * update))

    @pl.when(pl.program_id(0) == 0)
    def _():
        total_ref[...] = at_lane(totals, 127, norm)
        sum_ref[...] = jnp.zeros_like(sum_ref)
        for place in range(1, 7):
            step(place)

    row = lax.broadcasted_iota(jnp.int32, weights[0].shape, 0)
    step(0, row + pl.program_id(0) * weights[0].shape[0] < own_rows)


def weight_kernel(every_ref, total_ref, *refs):
    weights, updates, outs = refs[:7], refs[7:14], refs[14:21]
    sum_ref = refs[21]
    update_norms = jnp.sqrt(jnp.sum(every_ref[...], axis=0))

    def step(place):
        norm = jnp.sqrt(total_ref[0:1, 3 + place : 4 + place])
        ratio = LEARN_RATE * (norm / update_norms[0:1, place : place + 1])
        outs[place][...] = weights[place][...] - ratio * updates[place][...]

    @pl.when(pl.program_id(0) == 0)
    def _():
        sum_ref[...] = update_norms
        for place in range(1, 7):
            step(place)

    step(0)


def hidden_order(values, row_width):
    lead = values.shape[:-1]
    return jnp.swapaxes(values.reshape(lead + (row_width, -1)), -1, -2).reshape(lead + (-1,))


def hidden_back(values, row_width):
    lead = values.shape[:-1]
    return jnp.swapaxes(values.reshape(lead + (-1, row_width)), -1, -2).reshape(lead + (-1,))


def column_blocks(values, row_width):
    return [values[:, c : c + row_width] for c in range(0, values.shape[1], row_width)]


def on_device(
    token_ids,
    true_mask,
    keep_layer,
    picked,
    teacher_hidden,
    teacher_logits,
    embed_table,
    pos_table,
    query_key_value_weight,
    output_weight,
    up_weight,
    down_weight,
    gains_biases,
    first_embed,
    first_pos,
    first_qkv,
    first_out,
    first_up,
    first_down,
    first_gains,
    second_embed,
    second_pos,
    second_qkv,
    second_out,
    second_up,
    second_down,
    second_gains,
):
    axes = AXES
    n_dp, n_fs = lax.axis_size(SPLIT), lax.axis_size("fsdp")
    n_dev = n_dp * n_fs
    i_fs = lax.axis_index("fsdp")
    masters = (
        embed_table,
        pos_table,
        query_key_value_weight,
        output_weight,
        up_weight,
        down_weight,
        gains_biases,
    )
    firsts = (first_embed, first_pos, first_qkv, first_out, first_up, first_down, first_gains)
    seconds = (
        second_embed,
        second_pos,
        second_qkv,
        second_out,
        second_up,
        second_down,
        second_gains,
    )
    seq_count, seq_len = token_ids.shape
    own_rows, row_width = embed_table.shape
    ff = up_weight.shape[1]
    in_rows = query_key_value_weight.shape[0]
    n_tok = seq_count * seq_len
    n_pick = picked.shape[0] * picked.shape[1]
    vocab = own_rows * n_dev
    block_rows = own_rows * n_fs

    table_low = embed_table.astype(jnp.bfloat16)
    pack_width = 3 * row_width + row_width + ff + ff + seq_len
    gain_width = -(-14 // 128) * 128
    packed_low = jnp.concatenate(
        [
            query_key_value_weight,
            output_weight,
            hidden_order(up_weight, row_width),
            down_weight.reshape(in_rows, ff),
            pos_table.T,
            jnp.pad(gains_biases.T, ((0, 0), (0, gain_width - 14))),
        ],
        axis=1,
    ).astype(jnp.bfloat16)
    gathered = lax.all_gather(packed_low, axes, axis=0, tiled=True)
    plan = route_plan(token_ids.reshape(-1), true_mask.reshape(-1) > 0, own_rows, n_dev)
    wanted, rounds = exchange_wanted(plan, 0, axes)
    ring = [(z, (z + 1) % n_fs) for z in range(n_fs)]
    padded = -(-own_rows // 16) * 16
    lanes = -(-own_rows // 128) * 128
    first_table = jnp.pad(table_low, ((0, padded - own_rows), (0, 0)))
    arrived = ask_rows(plan, wanted, table_low, axes)

    targets = parcels_of(teacher_logits.reshape(n_pick, vocab), own_rows, lanes, n_dev)
    arrived, targets = lax.optimization_barrier((arrived, targets))
    targets = lax.all_to_all(
        targets.reshape(n_dp, n_fs, n_pick, lanes), SPLIT, split_axis=0, concat_axis=0
    )
    arrived, first_table = lax.optimization_barrier((arrived, first_table))
    tables = [first_table, lax.ppermute(first_table, "fsdp", ring)]

    i_dp = lax.axis_index(SPLIT)
    token_rows = place_rows(plan, 0, arrived)
    token_rows = more_rows(plan, rounds, token_rows, table_low, axes)

    def pass_table(*later):
        newest, *later = lax.optimization_barrier((tables[-1], *later))
        if len(tables) < n_fs:
            tables.append(lax.ppermute(newest, "fsdp", ring))
        return later

    places = lax.rem(i_fs - jnp.arange(n_fs, dtype=jnp.int32) + n_fs, n_fs)

    rows = seq_len // 2
    n_block = seq_len // rows
    keeps = (keep_layer > 0).astype(jnp.int32)
    trues = jnp.sum(true_mask, axis=1)
    lengths = trues * keeps
    pick_column = picked.reshape(-1, 1)
    bf16, f32 = jnp.bfloat16, jnp.float32

    def by_seq(width, array=None):
        spec = ((rows, width), lambda s, b, *_: (s * n_block + b, 0))
        return spec if array is None else (array, *spec)

    def by_block(width, array=None):
        spec = ((rows, width), lambda b, s, *_: (s * n_block + b, 0))
        return spec if array is None else (array, *spec)

    def whole(shape):
        return (shape, lambda *_: (0,) * len(shape))

    def weight(width, place):
        return (gathered, (row_width, width), lambda *_: (0, place))

    vectors = weight(gain_width, pack_width // gain_width)
    qkv_weight = weight(3 * row_width, 0)
    out_weight = weight(row_width, 3)
    up_weight_low, down_weight_low = weight(ff, 1), weight(ff, 2)
    first_place = (4 * row_width + 2 * ff) // rows
    embedded, flat_in, flat_low, packed = row_kernel(
        enter_kernel,
        (lengths,),
        [
            by_block(row_width, token_rows),
            (gathered, (row_width, rows), lambda b, s, *_: (0, first_place + b)),
            vectors,
            qkv_weight,
        ],
        [
            ((n_tok, row_width), f32, *by_block(row_width)),
            ((n_tok, row_width), f32, *by_block(row_width)),
            ((n_tok, row_width), bf16, *by_block(row_width)),
            ((n_tok, 3 * row_width), bf16, *by_block(3 * row_width)),
        ],
        (n_block, seq_count),
    )
    mixed_output = attend(lengths, packed)
    (mixed_output,) = pass_table(mixed_output)
    up_bias = hidden_order(
        gathered[:, pack_width + 10 : pack_width + 14].astype(f32).T.reshape(1, -1), row_width
    )
    pick_count = picked.shape[1]
    picks = (pick_column, (pick_count, 1), lambda s, b, *_: (s, 0))
    (
        joined_one,
        normed_low,
        gelu_slopes,
        gelu_activated,
        joined_two,
        grad_start,
        chosen,
        hidden_loss,
    ) = row_kernel(
        feed_kernel,
        (lengths, trues),
        [
            by_seq(row_width, mixed_output),
            by_seq(row_width, flat_in),
            by_seq(row_width, teacher_hidden.reshape(n_tok, row_width)),
            picks,
            vectors,
            (up_bias, *whole((1, ff))),
            out_weight,
            up_weight_low,
            down_weight_low,
        ],
        [
            ((n_tok, row_width), f32, *by_seq(row_width)),
            ((n_tok, row_width), bf16, *by_seq(row_width)),
            ((n_tok, ff), bf16, *by_seq(ff)),
            ((n_tok, ff), bf16, *by_seq(ff)),
            ((n_tok, row_width), f32, *by_seq(row_width)),
            ((n_tok, row_width), f32, *by_seq(row_width)),
            ((n_pick, row_width), bf16, (pick_count, row_width), lambda s, b, *_: (s, 0)),
            ((8, row_width), f32, *whole((8, row_width))),
        ],
        (seq_count, n_block),
        [pltpu.VMEM((rows, row_width), f32)],
    )
    loss_part = jnp.sum(hidden_loss)

    if n_fs > 2:
        (chosen,) = pass_table(chosen)
    by_distance = jnp.stack(
        [chosen]
        + [
            lax.ppermute(chosen, SPLIT, [(p, p ^ apart) for p in range(n_dp)])
            for apart in range(1, n_dp)
        ]
    )
    all_chosen = jnp.concatenate(
        [lax.dynamic_index_in_dim(by_distance, i_dp ^ p, 0, False) for p in range(n_dp)]
    )
    while len(tables) < n_fs:
        (all_chosen,) = pass_table(all_chosen)
    slopes, chosen_part, head_loss = head_products(
        places[:-1], all_chosen, targets, tables[:-1], [], jnp.float32
    )
    last_slopes, chosen_part, last_loss = head_products(
        places[-1:], all_chosen, targets, tables[-1:], [chosen_part], jnp.bfloat16
    )
    loss_part = loss_part + jnp.sum(head_loss + last_loss)
    many = n_dp * n_pick
    all_picked = (all_chosen, (many, row_width), lambda d: (0, 0))
    (head_part,) = row_kernel(
        head_first_kernel,
        (),
        [(slopes, (1, many, padded), lambda d: (1, 0, 0)), all_picked],
        [((padded, row_width), bf16, (padded, row_width), lambda d: (0, 0))],
        (1,),
    )
    head_sums = [lax.ppermute(head_part, "fsdp", ring)]
    last_slopes, grad_chosen = lax.optimization_barrier((last_slopes, chosen_part))
    grad_chosen = lax.all_to_all(
        grad_chosen.reshape(n_dp, n_pick, row_width), SPLIT, split_axis=0, concat_axis=0
    )
    (head_parts,) = row_kernel(
        head_grad_kernel,
        (),
        [
            (
                slopes,
                (1, many, padded),
                lambda d: (jnp.where(d < n_fs - 3, d + 2, 0), 0, 0),
            ),
            (last_slopes, (1, many, padded), lambda d: (0, 0, 0)),
            all_picked,
        ],
        [
            (
                (n_fs - 1, padded, row_width),
                bf16,
                (1, padded, row_width),
                lambda d: (d, 0, 0),
            )
        ],
        (n_fs - 1,),
    )

    def pass_sum(*later):
        newest, *later = lax.optimization_barrier((head_sums[-1], *later))
        step = len(head_sums)
        if step + 1 < n_fs:
            total = newest.astype(f32) + head_parts[step - 1].astype(f32)
            head_sums.append(lax.ppermute(total.astype(bf16), "fsdp", ring))
        return later

    grad_chosen, head_parts = pass_sum(grad_chosen, head_parts)
    for _ in range(n_fs - 4):
        (grad_chosen,) = pass_sum(grad_chosen)

    (
        grad_final,
        grad_joined_one,
        grad_mixed,
        grad_attention,
        grad_feed,
        grad_hidden,
        sums_one,
        hidden_sums,
    ) = row_kernel(
        unfeed_kernel,
        (lengths,),
        [
            by_seq(row_width, grad_start),
            (grad_chosen, (n_dp, pick_count, row_width), lambda s, b, *_: (0, s, 0)),
            picks,
            by_seq(row_width, joined_one),
            by_seq(ff, gelu_slopes),
            by_seq(row_width, joined_two),
            vectors,
            out_weight,
            up_weight_low,
            down_weight_low,
        ],
        [
            ((n_tok, row_width), f32, *by_seq(row_width)),
            ((n_tok, row_width), f32, *by_seq(row_width)),
            ((n_tok, row_width), bf16, *by_seq(row_width)),
            ((n_tok, row_width), bf16, *by_seq(row_width)),
            ((n_tok, row_width), bf16, *by_seq(row_width)),
            ((n_tok, ff), bf16, *by_seq(ff)),
            ((6, 8, row_width), f32, *whole((6, 8, row_width))),
            ((8, ff), f32, *whole((8, ff))),
        ],
        (seq_count, n_block),
    )
    member = lax.axis_index("pair").reshape(1).astype(jnp.int32)
    n_plane = lax.axis_size("plane")
    share = row_width // (2 * n_plane)
    halves = pltpu.VMEM((n_plane, 2, share, row_width), bf16)

    def dealt(columns):
        out = (
            (n_plane, share, columns * row_width),
            bf16,
            (n_plane, share, row_width),
            lambda j, *_: (0, 0, j),
        )
        return [out, out]

    def full(array):
        return (array, *whole(array.shape))

    blocks = ff // row_width
    early_kept, early_given = row_kernel(
        early_kernel,
        (member,),
        [
            full(mixed_output),
            full(grad_attention),
            full(normed_low),
            (
                grad_hidden,
                (n_tok, row_width),
                lambda j, *_: (0, jnp.clip(j - 1, 0, blocks - 1)),
            ),
            (
                gelu_activated,
                (n_tok, row_width),
                lambda j, *_: (0, jnp.clip(j - 1 - blocks, 0, blocks - 1)),
            ),
            full(grad_feed),
        ],
        dealt(1 + 2 * blocks),
        (1 + 2 * blocks,),
        [halves],
    )
    up_rows = hidden_back(jnp.sum(hidden_sums, axis=0, keepdims=True), row_width)
    early_kept, early_given = pass_sum(early_kept, early_given)
    early = sum_in_pair(early_kept, early_given)
    tile = jnp.zeros((8, 128), f32)
    scalars = [loss_part, jnp.sum(true_mask.astype(f32))]
    scalars += [jnp.sum(member * member) for member in masters]
    for place, value in enumerate(scalars):
        tile = at_lane(tile, place + 1, value)
    grad_mixed, early, tile, up_rows = lax.optimization_barrier(
        (grad_mixed, early, tile, up_rows)
    )
    early = sum_in_plane(early)
    grad_parts = attend(lengths, packed, grad_mixed)
    high_grad, rest_grad, place_grad, sums_two = row_kernel(
        leave_kernel,
        (lengths, keeps),
        [by_block(row_width, part) for part in grad_parts]
        + [
            by_block(row_width, grad_joined_one),
            by_block(row_width, grad_final),
            by_block(row_width, embedded),
            vectors,
            qkv_weight,
        ],
        [
            ((n_tok, row_width), bf16, *by_block(row_width)),
            ((n_tok, row_width), bf16, *by_block(row_width)),
            ((row_width, seq_len), bf16, (row_width, rows), lambda b, s, *_: (0, b)),
            ((4, 8, row_width), f32, *whole((4, 8, row_width))),
        ],
        (n_block, seq_count),
        [pltpu.VMEM((rows, row_width), f32)],
    )
    flat_grad = (high_grad, rest_grad)
    given_rows = rows_to_give(plan, 0, flat_grad)
    given_rows, *grad_parts = lax.optimization_barrier((given_rows, *grad_parts))
    returned = give_rows(given_rows, axes)
    extra_rows = more_given(plan, rounds, flat_grad, own_rows, axes)
    late_kept, late_given = row_kernel(
        late_kernel,
        (member,),
        [full(flat_low)]
        + [full(part) for part in grad_parts]
        + [
            full(place_grad),
            full(sums_one),
            full(sums_two),
            full(up_rows.reshape(4, row_width)),
        ],
        dealt(4),
        (4,),
        [
            halves,
            pltpu.VMEM((row_width, row_width), f32),
            pltpu.VMEM((gain_width, row_width), f32),
        ],
    )
    late_kept, late_given, early, extra_rows, head_sums[-1] = lax.optimization_barrier(
        (late_kept, late_given, early, extra_rows, head_sums[-1])
    )
    last = sum_in_plane(sum_in_pair(late_kept, late_given))
    early = sum_in_line(early)
    returned, last = lax.optimization_barrier((returned, last))
    last = sum_in_line(last)
    early_grads = (
        early[:, :row_width],
        hidden_back(early[:, row_width : row_width + ff], row_width),
        early[:, row_width + ff :].reshape(-1, row_width),
    )
    rows = 208
    steps = -(-own_rows // rows)

    def by_row(array=None, width=row_width):
        spec = ((rows, width), lambda r, *_: (r, 0))
        return spec if array is None else (array, *spec)

    table_grad, place_sums, qkv_sums, vector_sums, tile = row_kernel(
        functools.partial(table_kernel, own_rows),
        (),
        [
            full(wanted.reshape(1, -1)),
            full(returned),
            by_row(extra_rows),
            by_row(head_sums[-1]),
            (head_parts, (1, rows, row_width), lambda r: (n_fs - 2, r, 0)),
            full(tile),
        ]
        + [full(grad) for grad in early_grads]
        + [full(last)],
        [
            ((own_rows, row_width), f32, *by_row()),
            ((in_rows, seq_len), f32, *whole((in_rows, seq_len))),
            ((in_rows, 3 * row_width), f32, *whole((in_rows, 3 * row_width))),
            (gains_biases.shape, f32, *whole(gains_biases.shape)),
            ((8, 128), f32, *whole((8, 128))),
        ],
        (steps,),
    )

    def exchange(tile):
        return lax.all_to_all(
            jnp.broadcast_to(tile[None], (n_dev, 8, 128)), axes, split_axis=0, concat_axis=0
        )

    def turned(arrays):
        return [array.T if place == 1 else array for place, array in enumerate(arrays)]

    def specs(arrays):
        return [by_row(arrays[0])] + [full(array) for array in arrays[1:]]

    weights = turned(masters)
    like = [
        (array.shape, f32, *(whole(array.shape) if place else by_row()))
        for place, array in enumerate(weights)
    ]
    tile_out = ((8, 128), f32, *whole((8, 128)))
    *results, totals, tile = row_kernel(
        functools.partial(update_kernel, own_rows),
        (),
        [full(exchange(tile))]
        + specs(weights)
        + specs([table_grad, place_sums, qkv_sums, *early_grads, vector_sums])
        + specs(turned(firsts))
        + specs(turned(seconds)),
        like * 3 + [tile_out, tile_out],
        (steps,),
    )
    new_moments, new_squares = turned(results[:7]), turned(results[7:14])
    *new_weights, update_norms = row_kernel(
        weight_kernel,
        (),
        [full(exchange(tile)), full(totals)] + specs(weights) + specs(results[14:]),
        like + [tile_out],
        (steps,),
    )
    new_weights = turned(new_weights)
    loss_sum, token_count, grad_norm = totals[0, 1], totals[0, 2], totals[0, 127]
    matrix_norms = jnp.stack([jnp.sqrt(totals[0, 3:10]), update_norms[0, :7]])
    return (
        loss_sum,
        token_count,
        grad_norm,
        new_weights[0],
        new_weights[1],
        new_weights[2],
        new_weights[3],
        new_weights[4],
        new_weights[5],
        new_weights[6],
        new_moments[0],
        new_moments[1],
        new_moments[2],
        new_moments[3],
        new_moments[4],
        new_moments[5],
        new_moments[6],
        new_squares[0],
        new_squares[1],
        new_squares[2],
        new_squares[3],
        new_squares[4],
        new_squares[5],
        new_squares[6],
        matrix_norms,
    )


def solution(mesh):
    split = Mesh(
        mesh.devices.reshape(mesh.shape["dp"] // 2, 2, mesh.shape["fsdp"]), AXES
    )
    placed = (
        P(AXES, None),
        P(AXES, None),
        P(AXES),
        P(AXES, None),
        P(AXES, None, None),
        P(AXES, None, None),
        P(AXES, None),
        P(None, AXES),
        P(AXES, None),
        P(AXES, None),
        P(AXES, None),
        P(AXES, None),
        P(None, AXES),
        P(AXES, None),
        P(None, AXES),
        P(AXES, None),
        P(AXES, None),
        P(AXES, None),
        P(AXES, None),
        P(None, AXES),
        P(AXES, None),
        P(None, AXES),
        P(AXES, None),
        P(AXES, None),
        P(AXES, None),
        P(AXES, None),
        P(None, AXES),
    )
    return jax.shard_map(
        on_device,
        mesh=split,
        in_specs=placed,
        out_specs=(
            P(),
            P(),
            P(),
            P(AXES, None),
            P(None, AXES),
            P(AXES, None),
            P(AXES, None),
            P(AXES, None),
            P(AXES, None),
            P(None, AXES),
            P(AXES, None),
            P(None, AXES),
            P(AXES, None),
            P(AXES, None),
            P(AXES, None),
            P(AXES, None),
            P(None, AXES),
            P(AXES, None),
            P(None, AXES),
            P(AXES, None),
            P(AXES, None),
            P(AXES, None),
            P(AXES, None),
            P(None, AXES),
            P(),
        ),
        check_vma=False,
    )
```

```python
import functools

import jax
import jax.numpy as jnp
from jax import lax
from jax.experimental import pallas as pl
from jax.experimental.pallas import tpu as pltpu
from jax.sharding import Mesh
from jax.sharding import PartitionSpec as P

H = 12
HD = 64
STEP = 10


NORM_EPS = 1e-05
CLIP_NORM = 0.5
BETA_ONE = 0.9
BETA_TWO = 0.999
ADAM_EPS = 1e-06
DECAY_RATE = 0.01
LEARN_RATE = 0.3
MASKED_SCORE = -1e30

SPLIT = ("plane", "pair")
AXES = ("plane", "pair", "fsdp")
VMEM = 60 * 2**20
NO_COST = pl.CostEstimate(flops=0, bytes_accessed=0, transcendentals=0)


def normal_cdf(values):
    return 0.5 + 0.5 * lax.erf(values * 0.5**0.5)


def dense(left_op, right_op):
    return jnp.dot(left_op, right_op, preferred_element_type=jnp.float32)


def dense_tn(left_op, right_op):
    return lax.dot_general(
        left_op, right_op, (((0,), (0,)), ((), ())), preferred_element_type=jnp.float32
    )


def dense_nt(left_op, right_op):
    return lax.dot_general(
        left_op, right_op, (((1,), (1,)), ((), ())), preferred_element_type=jnp.float32
    )


def pair_lanes(shape, member):
    lane = lax.broadcasted_iota(jnp.int32, shape, 1)
    return (lane >= HD) if member else (lane < HD)


def softmax_rows(query_rows, key_rows, length):
    scores = dense_nt(query_rows, key_rows)
    spot = lax.broadcasted_iota(jnp.int32, (1, scores.shape[1]), 1)
    scores = scores + jnp.where(spot < length, 0.0, MASKED_SCORE)
    exponent = jnp.exp(scores - jnp.max(scores, axis=1, keepdims=True))
    return exponent * (1.0 / jnp.sum(exponent, axis=1, keepdims=True))


def softmax_columns(key_rows, query_rows, length):
    scores = dense_nt(key_rows, query_rows)
    spot = lax.broadcasted_iota(jnp.int32, (scores.shape[0], 1), 0)
    scores = scores + jnp.where(spot < length, 0.0, MASKED_SCORE)
    exponent = jnp.exp(scores - jnp.max(scores, axis=0, keepdims=True))
    return exponent * (1.0 / jnp.sum(exponent, axis=0, keepdims=True))


def row_spans(seq_len):
    half = seq_len // 2
    return ((0, half), (half, seq_len))


def mix_kernel(length_ref, query_ref, key_ref, value_ref, mixed_ref):
    seq_len = query_ref.shape[0]
    length = length_ref[pl.program_id(0)]

    for low, high in row_spans(seq_len):

        @pl.when((length > low) & (length <= high))
        def _():
            step = high
            keys, values = key_ref[0:high, :], value_ref[0:high, :]
            for row in range(0, high, step):
                queries = query_ref[row : row + step, :] * 0.125
                parts = []
                for member in (0, 1):
                    lanes = pair_lanes(queries.shape, member)
                    chance = softmax_rows(
                        jnp.where(lanes, queries, jnp.zeros_like(queries)), keys, length
                    )
                    parts.append(dense(chance.astype(jnp.bfloat16), values))
                mixed_ref[row : row + step, :] = jnp.where(
                    pair_lanes(parts[0].shape, 1), parts[1], parts[0]
                ).astype(jnp.bfloat16)
            if high < seq_len:
                mixed_ref[high:, :] = jnp.zeros((seq_len - high, 2 * HD), jnp.bfloat16)

    @pl.when(length == 0)
    def _():
        mixed_ref[...] = jnp.zeros_like(mixed_ref)


def unmix_kernel(
    length_ref, query_ref, key_ref, value_ref, grad_ref, query_out, key_out, value_out
):
    seq_len = query_ref.shape[0]
    length = length_ref[pl.program_id(0)]
    outs = (query_out, key_out, value_out)

    for low, high in row_spans(seq_len):

        @pl.when((length > low) & (length <= high))
        def _():
            step = high
            keys, values = key_ref[0:high, :], value_ref[0:high, :]
            key_total, value_total = None, None
            for row in range(0, high, step):
                plain = query_ref[row : row + step, :]
                queries = plain * 0.125
                grads = grad_ref[row : row + step, :]
                parts = []
                for member in (0, 1):
                    lanes = pair_lanes(queries.shape, member)
                    zero = jnp.zeros_like(queries)
                    chance = softmax_columns(keys, jnp.where(lanes, queries, zero), length)
                    slope = dense_nt(values, jnp.where(lanes, grads, zero))
                    slope = chance * (slope - jnp.sum(slope * chance, axis=0, keepdims=True))
                    slope = slope.astype(jnp.bfloat16)
                    parts.append(
                        (
                            dense_tn(slope, keys),
                            dense(slope, plain),
                            dense(chance.astype(jnp.bfloat16), grads),
                        )
                    )
                query_part, key_part, value_part = [
                    jnp.where(pair_lanes(first.shape, 1), second, first)
                    for first, second in zip(*parts)
                ]
                query_out[row : row + step, :] = (query_part * 0.125).astype(jnp.bfloat16)
                key_total = key_part if key_total is None else key_total + key_part
                value_total = value_part if value_total is None else value_total + value_part
            key_out[0:high, :] = (key_total * 0.125).astype(jnp.bfloat16)
            value_out[0:high, :] = value_total.astype(jnp.bfloat16)
            if high < seq_len:
                for ref in outs:
                    ref[high:, :] = jnp.zeros((seq_len - high, 2 * HD), jnp.bfloat16)

    @pl.when(length == 0)
    def _():
        for ref in outs:
            ref[...] = jnp.zeros_like(ref)


def attend(lengths, packed, grad_mixed=None):
    seq_count = lengths.shape[0]
    seq_len = packed.shape[0] // seq_count
    pairs = H // 2

    def block(first):
        return pl.BlockSpec((seq_len, 2 * HD), lambda s, h, _: (s, first + h))

    out = jax.ShapeDtypeStruct((packed.shape[0], H * HD), jnp.bfloat16)
    forward = grad_mixed is None
    operands = (packed, packed, packed) + (() if forward else (grad_mixed,))
    return pl.pallas_call(
        mix_kernel if forward else unmix_kernel,
        out_shape=out if forward else (out, out, out),
        grid_spec=pltpu.PrefetchScalarGridSpec(
            num_scalar_prefetch=1,
            grid=(seq_count, pairs),
            in_specs=[block(0), block(pairs), block(2 * pairs)] + ([] if forward else [block(0)]),
            out_specs=block(0) if forward else (block(0),) * 3,
        ),
        compiler_params=pltpu.CompilerParams(vmem_limit_bytes=VMEM),
        cost_estimate=NO_COST,
    )(lengths, *operands)


def norm_parts(values):
    centered = values - jnp.mean(values, axis=1, keepdims=True)
    spread = lax.rsqrt(jnp.mean(centered * centered, axis=1, keepdims=True) + NORM_EPS)
    return centered * spread, spread


def norm_back(grads, unit_rows, spread, gain_row):
    scaled = grads * gain_row
    inner = jnp.mean(scaled * unit_rows, axis=1, keepdims=True)
    rows = spread * (scaled - jnp.mean(scaled, axis=1, keepdims=True) - unit_rows * inner)
    return rows, eight_rows(grads * unit_rows), eight_rows(grads)


def eight_rows(values):
    return jnp.sum(values.reshape(-1, 8, values.shape[1]), axis=0)


def picks_hot(picked_ref, first_row, rows):
    spot = lax.broadcasted_iota(jnp.int32, (picked_ref.shape[0], rows), 1) + first_row
    return (picked_ref[...] == spot).astype(jnp.bfloat16)


def enter_kernel(
    length_ref, token_ref, place_ref, vector_ref, weight_ref, embedded_ref, input_ref, low_ref, packed_ref
):
    block, seq = pl.program_id(0), pl.program_id(1)
    rows = token_ref.shape[0]
    vectors = vector_ref[...].astype(jnp.float32).T
    embedded = token_ref[...] + place_ref[...].astype(jnp.float32).T
    embedded_ref[...] = embedded
    inputs = norm_parts(embedded)[0] * vectors[0:1] + vectors[1:2]
    input_ref[...] = inputs
    low = inputs.astype(jnp.bfloat16)
    low_ref[...] = low

    @pl.when(length_ref[seq] > block * rows)
    def _():
        width = low.shape[1]
        for part, bias in enumerate((vectors[2:3], None, vectors[3:4])):
            columns = slice(part * width, (part + 1) * width)
            values = dense(low, weight_ref[:, columns])
            if bias is not None:
                values = values + bias
            packed_ref[:, columns] = values.astype(jnp.bfloat16)


def feed_kernel(
    length_ref,
    true_ref,
    mixed_ref,
    input_ref,
    teacher_ref,
    picked_ref,
    vector_ref,
    bias_ref,
    out_ref,
    up_ref,
    down_ref,
    joined_one_ref,
    normed_ref,
    slope_ref,
    active_ref,
    joined_two_ref,
    grad_ref,
    chosen_ref,
    loss_ref,
    final_ref,
):
    seq, block = pl.program_id(0), pl.program_id(1)
    rows, width = mixed_ref.shape
    alive = length_ref[seq] > block * rows
    final_ref[...] = input_ref[...]

    @pl.when(alive)
    def _():
        vectors = vector_ref[...].astype(jnp.float32).T
        joined = input_ref[...] + (dense(mixed_ref[...], out_ref[...]) + vectors[4:5])
        joined_one_ref[...] = joined
        normed = norm_parts(joined)[0] * vectors[5:6] + vectors[6:7]
        low = normed.astype(jnp.bfloat16)
        normed_ref[...] = low
        fed = None
        for column in range(0, up_ref.shape[1], width):
            columns = slice(column, column + width)
            hidden = dense(low, up_ref[:, columns]) + bias_ref[:, columns]
            share = normal_cdf(hidden)
            density = jnp.exp(-0.5 * hidden * hidden) * (2.0 * jnp.pi) ** -0.5
            slope_ref[:, columns] = (share + hidden * density).astype(jnp.bfloat16)
            active = (hidden * share).astype(jnp.bfloat16)
            active_ref[:, columns] = active
            part = dense(active, down_ref[:, columns])
            fed = part if fed is None else fed + part
        joined = normed + (fed + vectors[7:8])
        joined_two_ref[...] = joined
        final_ref[...] = norm_parts(joined)[0] * vectors[8:9] + vectors[9:10]

    @pl.when(jnp.logical_not(alive))
    def _():
        normed_ref[...] = jnp.zeros_like(normed_ref)
        active_ref[...] = jnp.zeros_like(active_ref)

    final = final_ref[...]
    row = lax.broadcasted_iota(jnp.int32, final.shape, 0) + block * rows
    gap = jnp.where(row < true_ref[seq], final - teacher_ref[...].astype(jnp.float32), 0.0)
    grad_ref[...] = 2.0 * gap
    hot = picks_hot(picked_ref, block * rows, rows)
    chosen = dense(hot, final.astype(jnp.bfloat16)).astype(jnp.bfloat16)

    @pl.when(block == 0)
    def _():
        chosen_ref[...] = chosen

    @pl.when(block > 0)
    def _():
        chosen_ref[...] += chosen

    @pl.when((block == 0) & (seq == 0))
    def _():
        loss_ref[...] = jnp.zeros_like(loss_ref)

    loss_ref[...] += eight_rows(gap * gap)


def unfeed_kernel(
    length_ref,
    grad_ref,
    head_ref,
    picked_ref,
    joined_one_ref,
    slope_ref,
    joined_two_ref,
    vector_ref,
    out_ref,
    up_ref,
    down_ref,
    final_ref,
    joined_out,
    mixed_out,
    attention_out,
    feed_out,
    hidden_out,
    sums_ref,
    hidden_sum_ref,
):
    seq, block = pl.program_id(0), pl.program_id(1)
    rows, width = grad_ref.shape
    alive = length_ref[seq] > block * rows
    head = jnp.sum(head_ref[...].astype(jnp.float32), axis=0)
    high = head.astype(jnp.bfloat16)
    rest = (head - high.astype(jnp.float32)).astype(jnp.bfloat16)
    hot = picks_hot(picked_ref, block * rows, rows)
    grads = grad_ref[...] + dense_tn(hot, high) + dense_tn(hot, rest)
    final_ref[...] = grads

    @pl.when((block == 0) & (seq == 0))
    def _():
        sums_ref[...] = jnp.zeros_like(sums_ref)
        hidden_sum_ref[...] = jnp.zeros_like(hidden_sum_ref)

    @pl.when(alive)
    def _():
        vectors = vector_ref[...].astype(jnp.float32).T
        unit_rows, spread = norm_parts(joined_two_ref[...])
        grad_two, gain_two, shift_two = norm_back(grads, unit_rows, spread, vectors[8:9])
        feed = grad_two.astype(jnp.bfloat16)
        feed_out[...] = feed
        back = grad_two
        for column in range(0, up_ref.shape[1], width):
            columns = slice(column, column + width)
            hidden = dense_nt(feed, down_ref[:, columns])
            hidden = (hidden * slope_ref[:, columns].astype(jnp.float32)).astype(jnp.bfloat16)
            hidden_out[:, columns] = hidden
            hidden_sum_ref[:, columns] += eight_rows(hidden.astype(jnp.float32))
            back = back + dense_nt(hidden, up_ref[:, columns])
        unit_rows, spread = norm_parts(joined_one_ref[...])
        grad_one, gain_one, shift_one = norm_back(back, unit_rows, spread, vectors[5:6])
        joined_out[...] = grad_one
        attention = grad_one.astype(jnp.bfloat16)
        attention_out[...] = attention
        mixed_out[...] = dense_nt(attention, out_ref[...]).astype(jnp.bfloat16)
        sums_ref[0] += eight_rows(attention.astype(jnp.float32))
        sums_ref[1] += gain_one
        sums_ref[2] += shift_one
        sums_ref[3] += eight_rows(feed.astype(jnp.float32))
        sums_ref[4] += gain_two
        sums_ref[5] += shift_two

    @pl.when(jnp.logical_not(alive))
    def _():
        for ref in (joined_out, mixed_out, attention_out, feed_out, hidden_out):
            ref[...] = jnp.zeros_like(ref)


def leave_kernel(
    length_ref,
    keep_ref,
    query_ref,
    key_ref,
    value_ref,
    joined_ref,
    final_ref,
    embedded_ref,
    vector_ref,
    weight_ref,
    rows_ref,
    place_ref,
    sums_ref,
    place_sum,
):
    block, seq = pl.program_id(0), pl.program_id(1)
    rows, width = joined_ref.shape
    alive = length_ref[seq] > block * rows
    vectors = vector_ref[...].astype(jnp.float32).T
    dropped = (keep_ref[seq] == 0).astype(jnp.float32)

    @pl.when((block == 0) & (seq == 0))
    def _():
        sums_ref[...] = jnp.zeros_like(sums_ref)

    @pl.when(seq == 0)
    def _():
        place_sum[...] = jnp.zeros_like(place_sum)

    def finish(grads):
        unit_rows, spread = norm_parts(embedded_ref[...])
        grads, gain, shift = norm_back(grads, unit_rows, spread, vectors[0:1])
        sums_ref[0] += gain
        sums_ref[1] += shift
        rows_ref[...] = grads.astype(jnp.bfloat16)
        place_sum[...] += grads

    @pl.when(alive)
    def _():
        grads = joined_ref[...]
        for part, ref in enumerate((query_ref, key_ref, value_ref)):
            grads = grads + dense_nt(ref[...], weight_ref[:, part * width : (part + 1) * width])
        sums_ref[2] += eight_rows(query_ref[...].astype(jnp.float32))
        sums_ref[3] += eight_rows(value_ref[...].astype(jnp.float32))
        finish(grads)

    @pl.when(jnp.logical_not(alive))
    def _():
        finish(final_ref[...] * dropped)

    @pl.when(seq == pl.num_programs(1) - 1)
    def _():
        place_ref[...] = place_sum[...].T.astype(jnp.bfloat16)


def deal_out(product, member_ref, kept_ref, given_ref, halves):
    halves[...] = product.reshape(halves.shape).astype(halves.dtype)
    member = member_ref[0]
    kept_ref[0] = halves[:, member]
    given_ref[0] = halves[:, 1 - member]


def early_kernel(
    member_ref,
    mixed_ref,
    attention_ref,
    normed_ref,
    hidden_ref,
    active_ref,
    feed_ref,
    kept_ref,
    given_ref,
    halves,
):
    place, blocks = pl.program_id(0), pl.num_programs(0) // 2
    cases = (
        (place == 0, mixed_ref, attention_ref),
        ((place > 0) & (place <= blocks), normed_ref, hidden_ref),
        (place > blocks, active_ref, feed_ref),
    )
    for wanted, left_ref, right_ref in cases:

        @pl.when(wanted)
        def _():
            product = dense_tn(left_ref[...], right_ref[...])
            deal_out(product, member_ref, kept_ref, given_ref, halves)


def late_kernel(
    member_ref,
    low_ref,
    query_ref,
    key_ref,
    value_ref,
    place_ref,
    sums_one_ref,
    sums_two_ref,
    up_ref,
    kept_ref,
    given_ref,
    halves,
    columns,
    vectors,
):
    for part, ref in enumerate((query_ref, key_ref, value_ref)):

        @pl.when(pl.program_id(0) == part)
        def _():
            product = dense_tn(low_ref[...], ref[...])
            deal_out(product, member_ref, kept_ref, given_ref, halves)

    @pl.when(pl.program_id(0) == 3)
    def _():
        vectors[...] = jnp.zeros_like(vectors)
        for row in range(4):
            vectors[row : row + 1, :] = jnp.sum(sums_two_ref[row], axis=0, keepdims=True)
        for row in range(6):
            vectors[4 + row : 5 + row, :] = jnp.sum(sums_one_ref[row], axis=0, keepdims=True)
        vectors[10:14, :] = up_ref[...]
        columns[...] = jnp.zeros_like(columns)
        width = place_ref.shape[1]
        columns[:, :width] = place_ref[...].astype(jnp.float32)
        columns[:, width : width + vectors.shape[0]] = vectors[...].T
        deal_out(columns[...], member_ref, kept_ref, given_ref, halves)


def head_grad_kernel(slope_ref, last_ref, chosen_ref, *grad_refs):
    count = len(grad_refs)
    for place, grad_ref in enumerate(grad_refs):
        source = last_ref if place == count - 2 else slope_ref

        @pl.when(pl.program_id(0) == place)
        def _():
            grad_ref[...] = dense_tn(source[0], chosen_ref[...]).astype(grad_ref.dtype)


def head_first_kernel(slope_ref, chosen_ref, grad_ref):
    grad_ref[...] = dense_tn(slope_ref[0], chosen_ref[...]).astype(grad_ref.dtype)


def row_kernel(kernel, prefetch, operands, outs, grid, scratch=()):
    return pl.pallas_call(
        kernel,
        out_shape=tuple(jax.ShapeDtypeStruct(shape, kind) for shape, kind, _, _ in outs),
        grid_spec=pltpu.PrefetchScalarGridSpec(
            num_scalar_prefetch=len(prefetch),
            grid=grid,
            in_specs=[pl.BlockSpec(block, where) for _, block, where in operands],
            out_specs=tuple(pl.BlockSpec(block, where) for _, _, block, where in outs),
            scratch_shapes=list(scratch),
        ),
        compiler_params=pltpu.CompilerParams(vmem_limit_bytes=VMEM),
        cost_estimate=NO_COST,
    )(*prefetch, *[array for array, _, _ in operands])


def parcel_kernel(own_rows, tiles, wide, source, parcel_ref, slots, sems):
    part, parts = pl.program_id(0), pl.num_programs(0)

    def first_tile(index):
        return jnp.minimum(own_rows * index // 128, tiles - wide)

    def fetch(index):
        lane = pl.multiple_of(first_tile(index) * 128, 128)
        slot = lax.rem(index, 2)
        return pltpu.make_async_copy(
            source.at[:, pl.ds(lane, wide * 128)],
            slots.at[slot, :, pl.ds(0, wide * 128)],
            sems.at[slot],
        )

    @pl.when(part == 0)
    def _():
        fetch(0).start()

    @pl.when(part + 1 < parts)
    def _():
        fetch(part + 1).start()

    fetch(part).wait()
    shift = own_rows * part - 128 * first_tile(part)
    slot, skip, turn = lax.rem(part, 2), shift // 128, lax.rem(128 - lax.rem(shift, 128), 128)
    n_pick, width = parcel_ref.shape[1:]
    lane = lax.broadcasted_iota(jnp.int32, (n_pick, 128), 1)

    def turned(tile):
        start = pl.multiple_of((tile + skip) * 128, 128)
        values = slots[slot, :, pl.ds(start, 128)].astype(jnp.float32)
        return pltpu.roll(values, turn, axis=1)

    low = turned(0)
    for tile in range(width // 128):
        high = turned(tile + 1)
        values = jnp.where(lane < 128 - lax.rem(shift, 128), low, high)
        values = jnp.where(lane + 128 * tile < own_rows, values, 0.0)
        parcel_ref[0, :, 128 * tile : 128 * (tile + 1)] = values.astype(jnp.bfloat16)
        low = high


def parcels_of(flat_teacher, own_rows, lanes, n_dev):
    n_pick, vocab = flat_teacher.shape
    tiles = vocab // 128
    wide = min(tiles, lanes // 128 + 1)
    return pl.pallas_call(
        functools.partial(parcel_kernel, own_rows, tiles, wide),
        out_shape=jax.ShapeDtypeStruct((n_dev, n_pick, lanes), jnp.bfloat16),
        grid=(n_dev,),
        in_specs=[pl.BlockSpec(memory_space=pl.ANY)],
        out_specs=pl.BlockSpec((1, n_pick, lanes), lambda r: (r, 0, 0)),
        scratch_shapes=[
            pltpu.VMEM((2, n_pick, (wide + 2) * 128), jnp.bfloat16),
            pltpu.SemaphoreType.DMA((2,)),
        ],
        compiler_params=pltpu.CompilerParams(vmem_limit_bytes=VMEM),
        cost_estimate=NO_COST,
    )(flat_teacher)


def head_kernel(steps, place_ref, chosen_ref, target_ref, *refs):
    tables = refs[:steps]
    before = refs[steps:-3]
    slope_ref, part_ref, loss_ref = refs[-3:]
    chosen = chosen_ref[...]
    senders, _, n_pick, _ = target_ref.shape
    total, loss = before[0][...] if before else None, None
    for step in range(steps):
        table = tables[step][...]
        width = table.shape[0]
        target = target_ref[:, place_ref[step]].reshape(senders * n_pick, -1)[:, :width]
        gap = dense_nt(chosen, table) - target.astype(jnp.float32)
        square = jnp.sum((gap * gap).reshape(-1, 8, width), axis=0)
        loss = square if loss is None else loss + square
        slope = (2.0 * gap).astype(jnp.bfloat16)
        slope_ref[step] = slope
        part = dense(slope, table)
        total = part if total is None else total + part
    part_ref[...] = total.astype(part_ref.dtype)

    @pl.when(pl.program_id(0) == 0)
    def _():
        loss_ref[...] = jnp.zeros_like(loss_ref)

    loss_ref[...] += loss


def head_products(places, all_chosen, targets, tables, before, part_type):
    n_dp, n_fs, n_pick, lanes = targets.shape
    row_width = all_chosen.shape[1]
    padded = tables[0].shape[0]
    rows, steps = 2 * n_pick, len(tables)
    whole = pl.BlockSpec((padded, row_width), lambda m, _: (0, 0))
    some = pl.BlockSpec((rows, row_width), lambda m, _: (m, 0))
    return pl.pallas_call(
        functools.partial(head_kernel, steps),
        out_shape=(
            jax.ShapeDtypeStruct((steps, n_dp * n_pick, padded), jnp.bfloat16),
            jax.ShapeDtypeStruct((n_dp * n_pick, row_width), part_type),
            jax.ShapeDtypeStruct((8, padded), jnp.float32),
        ),
        grid_spec=pltpu.PrefetchScalarGridSpec(
            num_scalar_prefetch=1,
            grid=(n_dp // 2,),
            in_specs=[
                some,
                pl.BlockSpec((2, n_fs, n_pick, lanes), lambda m, _: (m, 0, 0, 0)),
            ]
            + [whole] * steps
            + [some] * len(before),
            out_specs=(
                pl.BlockSpec((steps, rows, padded), lambda m, _: (0, m, 0)),
                some,
                pl.BlockSpec((8, padded), lambda m, _: (0, 0)),
            ),
        ),
        compiler_params=pltpu.CompilerParams(vmem_limit_bytes=VMEM),
        cost_estimate=NO_COST,
    )(places, all_chosen, targets, *tables, *before)


def sum_over_peers(part, axis):
    size, me = lax.axis_size(axis), lax.axis_index(axis)
    arrived = [lax.dynamic_index_in_dim(part, me, 1, False).astype(jnp.float32)]
    for apart in range(1, size):
        given = lax.dynamic_index_in_dim(part, me ^ apart, 1, False)
        got = lax.ppermute(given, axis, [(peer, peer ^ apart) for peer in range(size)])
        arrived.append(got.astype(jnp.float32))
    return sum(arrived)


def sum_in_pair(kept, given, pieces=1):
    swap = [(0, 1), (1, 0)]
    size = given.shape[0] // pieces
    got = [
        lax.ppermute(given[p * size : (p + 1) * size], "pair", swap) for p in range(pieces)
    ]
    got = got[0] if pieces == 1 else jnp.concatenate(got)
    return (kept.astype(jnp.float32) + got.astype(jnp.float32)).astype(jnp.bfloat16)


def sum_in_plane(part):
    part = sum_over_peers(part, "plane").astype(jnp.bfloat16)
    return part.reshape(part.shape[0], lax.axis_size("fsdp"), -1, part.shape[-1])


def sum_in_line(part):
    return sum_over_peers(part, "fsdp")


def route_plan(ids, live, own_rows, n_dev):
    place = jnp.arange(ids.shape[0])
    owner = ids // own_rows
    same = (ids[:, None] == ids[None, :]) & live[None, :]
    leader = jnp.min(jnp.where(same, place[None, :], ids.shape[0]), axis=1)
    first = live & (leader == place)
    before = (owner[:, None] == owner[None, :]) & (place[None, :] < leader[:, None])
    rank = jnp.sum(before & first[None, :], axis=1, dtype=jnp.int32)
    room = max(16, 1280 // n_dev)
    rounds = jnp.max(jnp.where(first, rank, 0)) // room + 1
    return ids, live, owner, first, rank, room, rounds, own_rows, n_dev


def slots_of(plan, turn):
    ids, live, owner, first, rank, room, rounds, own_rows, n_dev = plan
    here = live & (rank >= turn * room) & (rank < (turn + 1) * room)
    return jnp.where(here, owner * room + rank - turn * room, -1)


def exchange_wanted(plan, turn, axes):
    ids, live, owner, first, rank, room, rounds, own_rows, n_dev = plan
    slots = slots_of(plan, turn)
    local = jnp.where(first, ids - owner * own_rows + 1, 0)
    hit = jnp.arange(n_dev * room)[:, None] == slots[None, :]
    asked = jnp.max(jnp.where(hit, local[None, :], 0), axis=1) - 1
    message = jnp.concatenate(
        [
            asked.reshape(n_dev, room),
            jnp.broadcast_to(rounds, (n_dev, 128 - room)).astype(jnp.int32),
        ],
        axis=1,
    ).reshape(n_dev, 1, 128)
    heard = lax.all_to_all(message, axes, split_axis=0, concat_axis=0).reshape(n_dev, 128)
    return heard[:, :room].reshape(-1), jnp.max(heard[:, room:])


def ask_rows(plan, wanted, table_low, axes):
    room, own_rows, n_dev = plan[5], plan[7], plan[8]
    one_hot = (wanted[:, None] == jnp.arange(own_rows)[None, :]).astype(jnp.bfloat16)
    rows = dense(one_hot, table_low).astype(jnp.bfloat16)
    return lax.all_to_all(rows.reshape(n_dev, room, -1), axes, split_axis=0, concat_axis=0)


def place_rows(plan, turn, rows):
    room, n_dev = plan[5], plan[8]
    back = (slots_of(plan, turn)[:, None] == jnp.arange(n_dev * room)[None, :]).astype(
        jnp.bfloat16
    )
    return dense(back, rows.reshape(n_dev * room, -1))


def more_rows(plan, rounds, token_rows, table_low, axes):
    def body(state):
        turn, total = state
        wanted, _ = exchange_wanted(plan, turn, axes)
        rows = ask_rows(plan, wanted, table_low, axes)
        return turn + 1, total + place_rows(plan, turn, rows)

    return lax.while_loop(lambda state: state[0] < rounds, body, (jnp.int32(1), token_rows))[1]


def rows_to_give(plan, turn, flat_grad):
    room, n_dev = plan[5], plan[8]
    spread = (jnp.arange(n_dev * room)[:, None] == slots_of(plan, turn)[None, :]).astype(
        jnp.bfloat16
    )
    sums = dense(spread, flat_grad).astype(jnp.bfloat16)
    return sums.reshape(n_dev, room, -1)


def give_rows(sums, axes):
    got = lax.all_to_all(sums, axes, split_axis=0, concat_axis=0)
    return got.reshape(-1, sums.shape[-1])


def more_given(plan, rounds, flat_grad, own_rows, own_part, axes):
    def body(state):
        turn, total = state
        wanted, _ = exchange_wanted(plan, turn, axes)
        one_hot = (jnp.arange(own_part.shape[0])[:, None] == wanted[None, :]).astype(jnp.bfloat16)
        got = give_rows(rows_to_give(plan, turn, flat_grad), axes)
        return turn + 1, (total.astype(jnp.float32) + dense(one_hot, got)).astype(total.dtype)

    return lax.while_loop(lambda state: state[0] < rounds, body, (jnp.int32(1), own_part))[1]


def at_lane(tile, lane, value):
    row = lax.broadcasted_iota(jnp.int32, tile.shape, 0)
    column = lax.broadcasted_iota(jnp.int32, tile.shape, 1)
    return tile + jnp.where((row == 0) & (column == lane), value, 0.0)


def total_sum(values):
    return jnp.sum(jnp.sum(values, axis=0, keepdims=True), axis=1, keepdims=True)


def table_kernel(
    own_rows,
    wanted_ref,
    returned_ref,
    moved_ref,
    part_ref,
    tile_ref,
    hidden_loss_ref,
    head_loss_ref,
    last_loss_ref,
    out_ref,
    up_ref,
    down_ref,
    last_ref,
    grad_ref,
    place_ref,
    qkv_ref,
    vector_ref,
    sum_ref,
):
    rows = grad_ref.shape[0]
    first = pl.program_id(0) * rows
    spot = lax.broadcasted_iota(jnp.int32, (rows, wanted_ref.shape[1]), 0) + first
    hot = (spot == wanted_ref[...]).astype(jnp.bfloat16)
    grads = dense(hot, returned_ref[...])
    grads = grads + (moved_ref[...].astype(jnp.float32) + part_ref[...].astype(jnp.float32))
    row = lax.broadcasted_iota(jnp.int32, grads.shape, 0) + first
    grads = jnp.where(row < own_rows, grads, 0.0)
    grad_ref[...] = grads

    @pl.when(pl.program_id(0) == 0)
    def _():
        sum_ref[...] = tile_ref[...]
        for loss_ref in (hidden_loss_ref, head_loss_ref, last_loss_ref):
            sum_ref[...] = at_lane(sum_ref[...], 1, total_sum(loss_ref[...]))
        width, places = last_ref.shape[2], place_ref.shape[1]
        for part in range(3):
            qkv_ref[:, part * width : (part + 1) * width] = last_ref[part]
        place_ref[...] = last_ref[3][:, :places]
        vectors = last_ref[3][:, places : places + 128].T
        vector_ref[...] = vectors[: vector_ref.shape[0], :]
        for other in (out_ref, up_ref, down_ref, place_ref, qkv_ref, vector_ref):
            sum_ref[...] = at_lane(sum_ref[...], 0, total_sum(other[...] * other[...]))

    sum_ref[...] = at_lane(sum_ref[...], 0, total_sum(grads * grads))


def update_kernel(own_rows, steps, every_ref, *refs):
    weights, grads, firsts, seconds = [refs[7 * k : 7 * k + 7] for k in range(4)]
    moments, squares, updates = [refs[7 * k : 7 * k + 7] for k in range(4, 7)]
    total_ref, sum_ref = refs[49:]
    totals = jnp.sum(every_ref[...], axis=0)
    count = totals[0:1, 2:3]
    norm = jnp.sqrt(totals[0:1, 0:1]) / count
    factor = jnp.minimum(1.0, CLIP_NORM / norm) / count

    def step(place, live=None):
        weight = weights[place][...]
        clipped = grads[place][...] * factor
        moment = BETA_ONE * firsts[place][...] + (1.0 - BETA_ONE) * clipped
        square = BETA_TWO * seconds[place][...] + (1.0 - BETA_TWO) * clipped * clipped
        update = (
            moment
            * (1.0 / (1.0 - BETA_ONE**STEP))
            / (jnp.sqrt(square * (1.0 / (1.0 - BETA_TWO**STEP))) + ADAM_EPS)
            + DECAY_RATE * weight
        )
        moments[place][...] = moment
        squares[place][...] = square
        updates[place][...] = update
        if live is not None:
            update = jnp.where(live, update, 0.0)
        sum_ref[...] = at_lane(sum_ref[...], place, total_sum(update * update))

    @pl.when(pl.program_id(0) == 0)
    def _():
        total_ref[...] = at_lane(totals, 127, norm)
        sum_ref[...] = jnp.zeros_like(sum_ref)

    for place in range(1, 7):

        @pl.when(pl.program_id(0) == place % steps)
        def _():
            step(place)

    row = lax.broadcasted_iota(jnp.int32, weights[0].shape, 0)
    step(0, row + pl.program_id(0) * weights[0].shape[0] < own_rows)


def weight_kernel(steps, every_ref, total_ref, *refs):
    weights, updates, outs = refs[:7], refs[7:14], refs[14:21]
    sum_ref = refs[21]
    update_norms = jnp.sqrt(jnp.sum(every_ref[...], axis=0))

    def step(place):
        norm = jnp.sqrt(total_ref[0:1, 3 + place : 4 + place])
        ratio = LEARN_RATE * (norm / update_norms[0:1, place : place + 1])
        outs[place][...] = weights[place][...] - ratio * updates[place][...]

    @pl.when(pl.program_id(0) == 0)
    def _():
        sum_ref[...] = update_norms

    for place in range(1, 7):

        @pl.when(pl.program_id(0) == place % steps)
        def _():
            step(place)

    step(0)


def hidden_order(values, row_width):
    lead = values.shape[:-1]
    return jnp.swapaxes(values.reshape(lead + (row_width, -1)), -1, -2).reshape(lead + (-1,))


def hidden_back(values, row_width):
    lead = values.shape[:-1]
    return jnp.swapaxes(values.reshape(lead + (-1, row_width)), -1, -2).reshape(lead + (-1,))


def column_blocks(values, row_width):
    return [values[:, c : c + row_width] for c in range(0, values.shape[1], row_width)]


def on_device(
    token_ids,
    true_mask,
    keep_layer,
    picked,
    teacher_hidden,
    teacher_logits,
    embed_table,
    pos_table,
    query_key_value_weight,
    output_weight,
    up_weight,
    down_weight,
    gains_biases,
    first_embed,
    first_pos,
    first_qkv,
    first_out,
    first_up,
    first_down,
    first_gains,
    second_embed,
    second_pos,
    second_qkv,
    second_out,
    second_up,
    second_down,
    second_gains,
):
    axes = AXES
    n_dp, n_fs = lax.axis_size(SPLIT), lax.axis_size("fsdp")
    n_dev = n_dp * n_fs
    i_fs = lax.axis_index("fsdp")
    masters = (
        embed_table,
        pos_table,
        query_key_value_weight,
        output_weight,
        up_weight,
        down_weight,
        gains_biases,
    )
    firsts = (first_embed, first_pos, first_qkv, first_out, first_up, first_down, first_gains)
    seconds = (
        second_embed,
        second_pos,
        second_qkv,
        second_out,
        second_up,
        second_down,
        second_gains,
    )
    seq_count, seq_len = token_ids.shape
    own_rows, row_width = embed_table.shape
    ff = up_weight.shape[1]
    in_rows = query_key_value_weight.shape[0]
    n_tok = seq_count * seq_len
    n_pick = picked.shape[0] * picked.shape[1]
    vocab = own_rows * n_dev
    block_rows = own_rows * n_fs

    table_low = embed_table.astype(jnp.bfloat16)
    pack_width = 3 * row_width + row_width + ff + ff + seq_len
    gain_width = -(-14 // 128) * 128
    packed_low = jnp.concatenate(
        [
            query_key_value_weight,
            output_weight,
            hidden_order(up_weight, row_width),
            down_weight.reshape(in_rows, ff),
            pos_table.T,
            jnp.pad(gains_biases.T, ((0, 0), (0, gain_width - 14))),
        ],
        axis=1,
    ).astype(jnp.bfloat16)
    gathered = lax.all_gather(packed_low, axes, axis=0, tiled=True)
    plan = route_plan(token_ids.reshape(-1), true_mask.reshape(-1) > 0, own_rows, n_dev)
    wanted, rounds = exchange_wanted(plan, 0, axes)
    ring = [(z, (z + 1) % n_fs) for z in range(n_fs)]
    padded = -(-own_rows // 16) * 16
    lanes = -(-own_rows // 128) * 128
    first_table = jnp.pad(table_low, ((0, padded - own_rows), (0, 0)))
    arrived = ask_rows(plan, wanted, table_low, axes)

    targets = parcels_of(teacher_logits.reshape(n_pick, vocab), own_rows, lanes, n_dev)
    arrived, targets = lax.optimization_barrier((arrived, targets))
    targets = lax.all_to_all(
        targets.reshape(n_dp, n_fs, n_pick, lanes), SPLIT, split_axis=0, concat_axis=0
    )
    tile = jnp.zeros((8, 128), jnp.float32)
    scalars = [jnp.sum(true_mask.astype(jnp.float32))]
    scalars += [jnp.sum(member * member) for member in masters]
    for place, value in enumerate(scalars):
        tile = at_lane(tile, place + 2, value)
    arrived, first_table, tile = lax.optimization_barrier((arrived, first_table, tile))
    tables = [first_table, lax.ppermute(first_table, "fsdp", ring)]

    i_dp = lax.axis_index(SPLIT)
    token_rows = place_rows(plan, 0, arrived)
    token_rows = more_rows(plan, rounds, token_rows, table_low, axes)

    def pass_table(*later):
        newest, *later = lax.optimization_barrier((tables[-1], *later))
        if len(tables) < n_fs:
            tables.append(lax.ppermute(newest, "fsdp", ring))
        return later

    places = lax.rem(i_fs - jnp.arange(n_fs, dtype=jnp.int32) + n_fs, n_fs)

    rows = seq_len // 2
    n_block = seq_len // rows
    keeps = (keep_layer > 0).astype(jnp.int32)
    trues = jnp.sum(true_mask, axis=1)
    lengths = trues * keeps
    pick_column = picked.reshape(-1, 1)
    bf16, f32 = jnp.bfloat16, jnp.float32

    def by_seq(width, array=None):
        spec = ((rows, width), lambda s, b, *_: (s * n_block + b, 0))
        return spec if array is None else (array, *spec)

    def by_block(width, array=None):
        spec = ((rows, width), lambda b, s, *_: (s * n_block + b, 0))
        return spec if array is None else (array, *spec)

    def whole(shape):
        return (shape, lambda *_: (0,) * len(shape))

    def weight(width, place):
        return (gathered, (row_width, width), lambda *_: (0, place))

    vectors = weight(gain_width, pack_width // gain_width)
    qkv_weight = weight(3 * row_width, 0)
    out_weight = weight(row_width, 3)
    up_weight_low, down_weight_low = weight(ff, 1), weight(ff, 2)
    first_place = (4 * row_width + 2 * ff) // rows
    embedded, flat_in, flat_low, packed = row_kernel(
        enter_kernel,
        (lengths,),
        [
            by_block(row_width, token_rows),
            (gathered, (row_width, rows), lambda b, s, *_: (0, first_place + b)),
            vectors,
            qkv_weight,
        ],
        [
            ((n_tok, row_width), f32, *by_block(row_width)),
            ((n_tok, row_width), f32, *by_block(row_width)),
            ((n_tok, row_width), bf16, *by_block(row_width)),
            ((n_tok, 3 * row_width), bf16, *by_block(3 * row_width)),
        ],
        (n_block, seq_count),
    )
    mixed_output = attend(lengths, packed)
    (mixed_output,) = pass_table(mixed_output)
    up_bias = hidden_order(
        gathered[:, pack_width + 10 : pack_width + 14].astype(f32).T.reshape(1, -1), row_width
    )
    pick_count = picked.shape[1]
    picks = (pick_column, (pick_count, 1), lambda s, b, *_: (s, 0))
    (
        joined_one,
        normed_low,
        gelu_slopes,
        gelu_activated,
        joined_two,
        grad_start,
        chosen,
        hidden_loss,
    ) = row_kernel(
        feed_kernel,
        (lengths, trues),
        [
            by_seq(row_width, mixed_output),
            by_seq(row_width, flat_in),
            by_seq(row_width, teacher_hidden.reshape(n_tok, row_width)),
            picks,
            vectors,
            (up_bias, *whole((1, ff))),
            out_weight,
            up_weight_low,
            down_weight_low,
        ],
        [
            ((n_tok, row_width), f32, *by_seq(row_width)),
            ((n_tok, row_width), bf16, *by_seq(row_width)),
            ((n_tok, ff), bf16, *by_seq(ff)),
            ((n_tok, ff), bf16, *by_seq(ff)),
            ((n_tok, row_width), f32, *by_seq(row_width)),
            ((n_tok, row_width), f32, *by_seq(row_width)),
            ((n_pick, row_width), bf16, (pick_count, row_width), lambda s, b, *_: (s, 0)),
            ((8, row_width), f32, *whole((8, row_width))),
        ],
        (seq_count, n_block),
        [pltpu.VMEM((rows, row_width), f32)],
    )

    if n_fs > 2:
        (chosen,) = pass_table(chosen)
    by_distance = jnp.stack(
        [chosen]
        + [
            lax.ppermute(chosen, SPLIT, [(p, p ^ apart) for p in range(n_dp)])
            for apart in range(1, n_dp)
        ]
    )
    all_chosen = jnp.concatenate(
        [lax.dynamic_index_in_dim(by_distance, i_dp ^ p, 0, False) for p in range(n_dp)]
    )
    while len(tables) < n_fs:
        (all_chosen,) = pass_table(all_chosen)
    slopes, chosen_part, head_loss = head_products(
        places[:-1], all_chosen, targets, tables[:-1], [], jnp.float32
    )
    last_slopes, chosen_part, last_loss = head_products(
        places[-1:], all_chosen, targets, tables[-1:], [chosen_part], jnp.bfloat16
    )
    many = n_dp * n_pick
    all_picked = (all_chosen, (many, row_width), lambda d: (0, 0))
    (head_part,) = row_kernel(
        head_first_kernel,
        (),
        [(slopes, (1, many, padded), lambda d: (1, 0, 0)), all_picked],
        [((padded, row_width), bf16, (padded, row_width), lambda d: (0, 0))],
        (1,),
    )
    head_sums = [lax.ppermute(head_part, "fsdp", ring)]
    last_slopes, grad_chosen = lax.optimization_barrier((last_slopes, chosen_part))
    grad_chosen = lax.all_to_all(
        grad_chosen.reshape(n_dp, n_pick, row_width), SPLIT, split_axis=0, concat_axis=0
    )
    head_parts = row_kernel(
        head_grad_kernel,
        (),
        [
            (
                slopes,
                (1, many, padded),
                lambda d: (jnp.where(d < n_fs - 3, d + 2, 0), 0, 0),
            ),
            (last_slopes, (1, many, padded), lambda d: (0, 0, 0)),
            all_picked,
        ],
        [((padded, row_width), bf16, (padded, row_width), lambda d: (0, 0))] * (n_fs - 1),
        (n_fs - 1,),
    )

    def pass_sum(*later):
        newest, *later = lax.optimization_barrier((head_sums[-1], *later))
        step = len(head_sums)
        if step + 1 < n_fs:
            total = newest.astype(f32) + head_parts[step - 1].astype(f32)
            head_sums.append(lax.ppermute(total.astype(bf16), "fsdp", ring))
        return later

    grad_chosen, *head_parts = pass_sum(grad_chosen, *head_parts)
    for _ in range(n_fs - 4):
        (grad_chosen,) = pass_sum(grad_chosen)

    (
        grad_final,
        grad_joined_one,
        grad_mixed,
        grad_attention,
        grad_feed,
        grad_hidden,
        sums_one,
        hidden_sums,
    ) = row_kernel(
        unfeed_kernel,
        (lengths,),
        [
            by_seq(row_width, grad_start),
            (grad_chosen, (n_dp, pick_count, row_width), lambda s, b, *_: (0, s, 0)),
            picks,
            by_seq(row_width, joined_one),
            by_seq(ff, gelu_slopes),
            by_seq(row_width, joined_two),
            vectors,
            out_weight,
            up_weight_low,
            down_weight_low,
        ],
        [
            ((n_tok, row_width), f32, *by_seq(row_width)),
            ((n_tok, row_width), f32, *by_seq(row_width)),
            ((n_tok, row_width), bf16, *by_seq(row_width)),
            ((n_tok, row_width), bf16, *by_seq(row_width)),
            ((n_tok, row_width), bf16, *by_seq(row_width)),
            ((n_tok, ff), bf16, *by_seq(ff)),
            ((6, 8, row_width), f32, *whole((6, 8, row_width))),
            ((8, ff), f32, *whole((8, ff))),
        ],
        (seq_count, n_block),
    )
    member = lax.axis_index("pair").reshape(1).astype(jnp.int32)
    n_plane = lax.axis_size("plane")
    share = row_width // (2 * n_plane)
    halves = pltpu.VMEM((n_plane, 2, share, row_width), bf16)

    def dealt(columns):
        out = (
            (columns, n_plane, share, row_width),
            bf16,
            (1, n_plane, share, row_width),
            lambda j, *_: (j, 0, 0, 0),
        )
        return [out, out]

    def full(array):
        return (array, *whole(array.shape))

    blocks = ff // row_width
    early_kept, early_given = row_kernel(
        early_kernel,
        (member,),
        [
            full(mixed_output),
            full(grad_attention),
            full(normed_low),
            (
                grad_hidden,
                (n_tok, row_width),
                lambda j, *_: (0, jnp.clip(j - 1, 0, blocks - 1)),
            ),
            (
                gelu_activated,
                (n_tok, row_width),
                lambda j, *_: (0, jnp.clip(j - 1 - blocks, 0, blocks - 1)),
            ),
            full(grad_feed),
        ],
        dealt(1 + 2 * blocks),
        (1 + 2 * blocks,),
        [halves],
    )
    up_rows = hidden_back(jnp.sum(hidden_sums, axis=0, keepdims=True), row_width)
    early_kept, early_given = pass_sum(early_kept, early_given)
    early = sum_in_pair(early_kept, early_given)
    grad_mixed, early, up_rows = lax.optimization_barrier((grad_mixed, early, up_rows))
    early = sum_in_plane(early)
    *grad_parts, head_sums[-1] = lax.optimization_barrier(
        (*attend(lengths, packed, grad_mixed), head_sums[-1])
    )
    flat_grad, place_grad, sums_two = row_kernel(
        leave_kernel,
        (lengths, keeps),
        [by_block(row_width, part) for part in grad_parts]
        + [
            by_block(row_width, grad_joined_one),
            by_block(row_width, grad_final),
            by_block(row_width, embedded),
            vectors,
            qkv_weight,
        ],
        [
            ((n_tok, row_width), bf16, *by_block(row_width)),
            ((row_width, seq_len), bf16, (row_width, rows), lambda b, s, *_: (0, b)),
            ((4, 8, row_width), f32, *whole((4, 8, row_width))),
        ],
        (n_block, seq_count),
        [pltpu.VMEM((rows, row_width), f32)],
    )
    flat_grad, early = lax.optimization_barrier((flat_grad, early))
    early = lax.psum_scatter(
        early.reshape(early.shape[0], -1, row_width), "fsdp", scatter_dimension=1, tiled=True
    ).astype(f32)
    given_rows = rows_to_give(plan, 0, flat_grad)
    given_rows, *grad_parts = lax.optimization_barrier((given_rows, *grad_parts))
    returned = give_rows(given_rows, axes)
    own_part = more_given(plan, rounds, flat_grad, own_rows, head_parts[n_fs - 2], axes)
    late_kept, late_given = row_kernel(
        late_kernel,
        (member,),
        [full(flat_low)]
        + [full(part) for part in grad_parts]
        + [
            full(place_grad),
            full(sums_one),
            full(sums_two),
            full(up_rows.reshape(4, row_width)),
        ],
        dealt(4),
        (4,),
        [
            halves,
            pltpu.VMEM((row_width, row_width), f32),
            pltpu.VMEM((gain_width, row_width), f32),
        ],
    )
    late_kept, late_given, own_part = lax.optimization_barrier(
        (late_kept, late_given, own_part)
    )
    last = sum_in_plane(sum_in_pair(late_kept, late_given, 4))
    returned, last = lax.optimization_barrier((returned, last))
    last = sum_in_line(last)
    early_grads = (
        early[0],
        jnp.transpose(early[1 : 1 + blocks], (1, 2, 0)).reshape(in_rows, ff),
        jnp.swapaxes(early[1 + blocks :], 0, 1).reshape(-1, row_width),
    )
    rows = 208
    steps = -(-own_rows // rows)

    def by_row(array=None, width=row_width):
        spec = ((rows, width), lambda r, *_: (r, 0))
        return spec if array is None else (array, *spec)

    table_grad, place_sums, qkv_sums, vector_sums, tile = row_kernel(
        functools.partial(table_kernel, own_rows),
        (),
        [
            full(wanted.reshape(1, -1)),
            full(returned),
            by_row(head_sums[-1]),
            by_row(own_part),
            full(tile),
            full(hidden_loss),
            full(head_loss),
            full(last_loss),
        ]
        + [full(grad) for grad in early_grads]
        + [full(last)],
        [
            ((own_rows, row_width), f32, *by_row()),
            ((in_rows, seq_len), f32, *whole((in_rows, seq_len))),
            ((in_rows, 3 * row_width), f32, *whole((in_rows, 3 * row_width))),
            (gains_biases.shape, f32, *whole(gains_biases.shape)),
            ((8, 128), f32, *whole((8, 128))),
        ],
        (steps,),
    )

    def exchange(tile):
        return lax.all_to_all(
            jnp.broadcast_to(tile[None], (n_dev, 8, 128)), axes, split_axis=0, concat_axis=0
        )

    def turned(arrays):
        return [array.T if place == 1 else array for place, array in enumerate(arrays)]

    def specs(arrays):
        return [by_row(arrays[0])] + [full(array) for array in arrays[1:]]

    weights = turned(masters)
    like = [
        (array.shape, f32, *(whole(array.shape) if place else by_row()))
        for place, array in enumerate(weights)
    ]
    tile_out = ((8, 128), f32, *whole((8, 128)))
    *results, totals, tile = row_kernel(
        functools.partial(update_kernel, own_rows, steps),
        (),
        [full(exchange(tile))]
        + specs(weights)
        + specs([table_grad, place_sums, qkv_sums, *early_grads, vector_sums])
        + specs(turned(firsts))
        + specs(turned(seconds)),
        like * 3 + [tile_out, tile_out],
        (steps,),
    )
    new_moments, new_squares = turned(results[:7]), turned(results[7:14])
    *new_weights, update_norms = row_kernel(
        functools.partial(weight_kernel, steps),
        (),
        [full(exchange(tile)), full(totals)] + specs(weights) + specs(results[14:]),
        like + [tile_out],
        (steps,),
    )
    new_weights = turned(new_weights)
    loss_sum, token_count, grad_norm = totals[0, 1], totals[0, 2], totals[0, 127]
    matrix_norms = jnp.stack([jnp.sqrt(totals[0, 3:10]), update_norms[0, :7]])
    return (
        loss_sum,
        token_count,
        grad_norm,
        new_weights[0],
        new_weights[1],
        new_weights[2],
        new_weights[3],
        new_weights[4],
        new_weights[5],
        new_weights[6],
        new_moments[0],
        new_moments[1],
        new_moments[2],
        new_moments[3],
        new_moments[4],
        new_moments[5],
        new_moments[6],
        new_squares[0],
        new_squares[1],
        new_squares[2],
        new_squares[3],
        new_squares[4],
        new_squares[5],
        new_squares[6],
        matrix_norms,
    )


def solution(mesh):
    split = Mesh(
        mesh.devices.reshape(mesh.shape["dp"] // 2, 2, mesh.shape["fsdp"]), AXES
    )
    placed = (
        P(AXES, None),
        P(AXES, None),
        P(AXES),
        P(AXES, None),
        P(AXES, None, None),
        P(AXES, None, None),
        P(AXES, None),
        P(None, AXES),
        P(AXES, None),
        P(AXES, None),
        P(AXES, None),
        P(AXES, None),
        P(None, AXES),
        P(AXES, None),
        P(None, AXES),
        P(AXES, None),
        P(AXES, None),
        P(AXES, None),
        P(AXES, None),
        P(None, AXES),
        P(AXES, None),
        P(None, AXES),
        P(AXES, None),
        P(AXES, None),
        P(AXES, None),
        P(AXES, None),
        P(None, AXES),
    )
    return jax.shard_map(
        on_device,
        mesh=split,
        in_specs=placed,
        out_specs=(
            P(),
            P(),
            P(),
            P(AXES, None),
            P(None, AXES),
            P(AXES, None),
            P(AXES, None),
            P(AXES, None),
            P(AXES, None),
            P(None, AXES),
            P(AXES, None),
            P(None, AXES),
            P(AXES, None),
            P(AXES, None),
            P(AXES, None),
            P(AXES, None),
            P(None, AXES),
            P(AXES, None),
            P(None, AXES),
            P(AXES, None),
            P(AXES, None),
            P(AXES, None),
            P(AXES, None),
            P(None, AXES),
            P(),
        ),
        check_vma=False,
    )
```

```python
import functools

import jax
import jax.numpy as jnp
from jax import lax
from jax.experimental import pallas as pl
from jax.experimental.pallas import tpu as pltpu
from jax.sharding import Mesh
from jax.sharding import PartitionSpec as P

H = 12
HD = 64
STEP = 10


NORM_EPS = 1e-05
CLIP_NORM = 0.5
BETA_ONE = 0.9
BETA_TWO = 0.999
ADAM_EPS = 1e-06
DECAY_RATE = 0.01
LEARN_RATE = 0.3
MASKED_SCORE = -1e30

SPLIT = ("plane", "pair")
AXES = ("plane", "pair", "fsdp")
VMEM = 60 * 2**20
NO_COST = pl.CostEstimate(flops=0, bytes_accessed=0, transcendentals=0)


def normal_cdf(values):
    return 0.5 + 0.5 * lax.erf(values * 0.5**0.5)


def dense(left_op, right_op):
    return jnp.dot(left_op, right_op, preferred_element_type=jnp.float32)


def dense_tn(left_op, right_op):
    return lax.dot_general(
        left_op, right_op, (((0,), (0,)), ((), ())), preferred_element_type=jnp.float32
    )


def dense_nt(left_op, right_op):
    return lax.dot_general(
        left_op, right_op, (((1,), (1,)), ((), ())), preferred_element_type=jnp.float32
    )


def pair_lanes(shape, member):
    lane = lax.broadcasted_iota(jnp.int32, shape, 1)
    return (lane >= HD) if member else (lane < HD)


def softmax_rows(query_rows, key_rows, length):
    scores = dense_nt(query_rows, key_rows)
    spot = lax.broadcasted_iota(jnp.int32, (1, scores.shape[1]), 1)
    scores = scores + jnp.where(spot < length, 0.0, MASKED_SCORE)
    exponent = jnp.exp(scores - jnp.max(scores, axis=1, keepdims=True))
    return exponent * (1.0 / jnp.sum(exponent, axis=1, keepdims=True))


def softmax_columns(key_rows, query_rows, length):
    scores = dense_nt(key_rows, query_rows)
    spot = lax.broadcasted_iota(jnp.int32, (scores.shape[0], 1), 0)
    scores = scores + jnp.where(spot < length, 0.0, MASKED_SCORE)
    exponent = jnp.exp(scores - jnp.max(scores, axis=0, keepdims=True))
    return exponent * (1.0 / jnp.sum(exponent, axis=0, keepdims=True))


def row_spans(seq_len):
    half = seq_len // 2
    return ((0, half), (half, seq_len))


def mix_kernel(length_ref, query_ref, key_ref, value_ref, mixed_ref):
    seq_len = query_ref.shape[0]
    length = length_ref[pl.program_id(0)]

    for low, high in row_spans(seq_len):

        @pl.when((length > low) & (length <= high))
        def _():
            step = high
            keys, values = key_ref[0:high, :], value_ref[0:high, :]
            for row in range(0, high, step):
                queries = query_ref[row : row + step, :] * 0.125
                parts = []
                for member in (0, 1):
                    lanes = pair_lanes(queries.shape, member)
                    chance = softmax_rows(
                        jnp.where(lanes, queries, jnp.zeros_like(queries)), keys, length
                    )
                    parts.append(dense(chance.astype(jnp.bfloat16), values))
                mixed_ref[row : row + step, :] = jnp.where(
                    pair_lanes(parts[0].shape, 1), parts[1], parts[0]
                ).astype(jnp.bfloat16)
            if high < seq_len:
                mixed_ref[high:, :] = jnp.zeros((seq_len - high, 2 * HD), jnp.bfloat16)

    @pl.when(length == 0)
    def _():
        mixed_ref[...] = jnp.zeros_like(mixed_ref)


def unmix_kernel(
    length_ref, query_ref, key_ref, value_ref, grad_ref, query_out, key_out, value_out
):
    seq_len = query_ref.shape[0]
    length = length_ref[pl.program_id(0)]
    outs = (query_out, key_out, value_out)

    for low, high in row_spans(seq_len):

        @pl.when((length > low) & (length <= high))
        def _():
            step = high
            keys, values = key_ref[0:high, :], value_ref[0:high, :]
            key_total, value_total = None, None
            for row in range(0, high, step):
                plain = query_ref[row : row + step, :]
                queries = plain * 0.125
                grads = grad_ref[row : row + step, :]
                parts = []
                for member in (0, 1):
                    lanes = pair_lanes(queries.shape, member)
                    zero = jnp.zeros_like(queries)
                    chance = softmax_columns(keys, jnp.where(lanes, queries, zero), length)
                    slope = dense_nt(values, jnp.where(lanes, grads, zero))
                    slope = chance * (slope - jnp.sum(slope * chance, axis=0, keepdims=True))
                    slope = slope.astype(jnp.bfloat16)
                    parts.append(
                        (
                            dense_tn(slope, keys),
                            dense(slope, plain),
                            dense(chance.astype(jnp.bfloat16), grads),
                        )
                    )
                query_part, key_part, value_part = [
                    jnp.where(pair_lanes(first.shape, 1), second, first)
                    for first, second in zip(*parts)
                ]
                query_out[row : row + step, :] = (query_part * 0.125).astype(jnp.bfloat16)
                key_total = key_part if key_total is None else key_total + key_part
                value_total = value_part if value_total is None else value_total + value_part
            key_out[0:high, :] = (key_total * 0.125).astype(jnp.bfloat16)
            value_out[0:high, :] = value_total.astype(jnp.bfloat16)
            if high < seq_len:
                for ref in outs:
                    ref[high:, :] = jnp.zeros((seq_len - high, 2 * HD), jnp.bfloat16)

    @pl.when(length == 0)
    def _():
        for ref in outs:
            ref[...] = jnp.zeros_like(ref)


def attend(lengths, packed, grad_mixed=None):
    seq_count = lengths.shape[0]
    seq_len = packed.shape[0] // seq_count
    pairs = H // 2

    def block(first):
        return pl.BlockSpec((seq_len, 2 * HD), lambda s, h, _: (s, first + h))

    out = jax.ShapeDtypeStruct((packed.shape[0], H * HD), jnp.bfloat16)
    forward = grad_mixed is None
    operands = (packed, packed, packed) + (() if forward else (grad_mixed,))
    return pl.pallas_call(
        mix_kernel if forward else unmix_kernel,
        out_shape=out if forward else (out, out, out),
        grid_spec=pltpu.PrefetchScalarGridSpec(
            num_scalar_prefetch=1,
            grid=(seq_count, pairs),
            in_specs=[block(0), block(pairs), block(2 * pairs)] + ([] if forward else [block(0)]),
            out_specs=block(0) if forward else (block(0),) * 3,
        ),
        compiler_params=pltpu.CompilerParams(vmem_limit_bytes=VMEM),
        cost_estimate=NO_COST,
    )(lengths, *operands)


def norm_parts(values):
    centered = values - jnp.mean(values, axis=1, keepdims=True)
    spread = lax.rsqrt(jnp.mean(centered * centered, axis=1, keepdims=True) + NORM_EPS)
    return centered * spread, spread


def norm_back(grads, unit_rows, spread, gain_row):
    scaled = grads * gain_row
    inner = jnp.mean(scaled * unit_rows, axis=1, keepdims=True)
    rows = spread * (scaled - jnp.mean(scaled, axis=1, keepdims=True) - unit_rows * inner)
    return rows, eight_rows(grads * unit_rows), eight_rows(grads)


def eight_rows(values):
    return jnp.sum(values.reshape(-1, 8, values.shape[1]), axis=0)


def picks_hot(picked_ref, first_row, rows):
    spot = lax.broadcasted_iota(jnp.int32, (picked_ref.shape[0], rows), 1) + first_row
    return (picked_ref[...] == spot).astype(jnp.bfloat16)


def enter_kernel(
    length_ref, token_ref, place_ref, vector_ref, weight_ref, embedded_ref, input_ref, low_ref, packed_ref
):
    block, seq = pl.program_id(0), pl.program_id(1)
    rows = token_ref.shape[0]
    vectors = vector_ref[...].astype(jnp.float32).T
    embedded = token_ref[...] + place_ref[...].astype(jnp.float32).T
    embedded_ref[...] = embedded
    inputs = norm_parts(embedded)[0] * vectors[0:1] + vectors[1:2]
    input_ref[...] = inputs
    low = inputs.astype(jnp.bfloat16)
    low_ref[...] = low

    @pl.when(length_ref[seq] > block * rows)
    def _():
        width = low.shape[1]
        for part, bias in enumerate((vectors[2:3], None, vectors[3:4])):
            columns = slice(part * width, (part + 1) * width)
            values = dense(low, weight_ref[:, columns])
            if bias is not None:
                values = values + bias
            packed_ref[:, columns] = values.astype(jnp.bfloat16)


def feed_kernel(
    length_ref,
    true_ref,
    mixed_ref,
    input_ref,
    teacher_ref,
    picked_ref,
    vector_ref,
    bias_ref,
    out_ref,
    up_ref,
    down_ref,
    joined_one_ref,
    normed_ref,
    slope_ref,
    active_ref,
    joined_two_ref,
    grad_ref,
    chosen_ref,
    loss_ref,
    final_ref,
):
    seq, block = pl.program_id(0), pl.program_id(1)
    rows, width = mixed_ref.shape
    alive = length_ref[seq] > block * rows
    final_ref[...] = input_ref[...]

    @pl.when(alive)
    def _():
        vectors = vector_ref[...].astype(jnp.float32).T
        joined = input_ref[...] + (dense(mixed_ref[...], out_ref[...]) + vectors[4:5])
        joined_one_ref[...] = joined
        normed = norm_parts(joined)[0] * vectors[5:6] + vectors[6:7]
        low = normed.astype(jnp.bfloat16)
        normed_ref[...] = low
        fed = None
        for column in range(0, up_ref.shape[1], width):
            columns = slice(column, column + width)
            hidden = dense(low, up_ref[:, columns]) + bias_ref[:, columns]
            share = normal_cdf(hidden)
            density = jnp.exp(-0.5 * hidden * hidden) * (2.0 * jnp.pi) ** -0.5
            slope_ref[:, columns] = (share + hidden * density).astype(jnp.bfloat16)
            active = (hidden * share).astype(jnp.bfloat16)
            active_ref[:, columns] = active
            part = dense(active, down_ref[:, columns])
            fed = part if fed is None else fed + part
        joined = normed + (fed + vectors[7:8])
        joined_two_ref[...] = joined
        final_ref[...] = norm_parts(joined)[0] * vectors[8:9] + vectors[9:10]

    @pl.when(jnp.logical_not(alive))
    def _():
        normed_ref[...] = jnp.zeros_like(normed_ref)
        active_ref[...] = jnp.zeros_like(active_ref)

    final = final_ref[...]
    row = lax.broadcasted_iota(jnp.int32, final.shape, 0) + block * rows
    gap = jnp.where(row < true_ref[seq], final - teacher_ref[...].astype(jnp.float32), 0.0)
    grad_ref[...] = 2.0 * gap
    hot = picks_hot(picked_ref, block * rows, rows)
    chosen = dense(hot, final.astype(jnp.bfloat16)).astype(jnp.bfloat16)

    @pl.when(block == 0)
    def _():
        chosen_ref[...] = chosen

    @pl.when(block > 0)
    def _():
        chosen_ref[...] += chosen

    @pl.when((block == 0) & (seq == 0))
    def _():
        loss_ref[...] = jnp.zeros_like(loss_ref)

    loss_ref[...] += eight_rows(gap * gap)


def unfeed_kernel(
    length_ref,
    grad_ref,
    head_ref,
    picked_ref,
    joined_one_ref,
    slope_ref,
    joined_two_ref,
    vector_ref,
    out_ref,
    up_ref,
    down_ref,
    final_ref,
    joined_out,
    mixed_out,
    attention_out,
    feed_out,
    hidden_out,
    sums_ref,
    hidden_sum_ref,
):
    seq, block = pl.program_id(0), pl.program_id(1)
    rows, width = grad_ref.shape
    alive = length_ref[seq] > block * rows
    head = jnp.sum(head_ref[...].astype(jnp.float32), axis=0)
    high = head.astype(jnp.bfloat16)
    rest = (head - high.astype(jnp.float32)).astype(jnp.bfloat16)
    hot = picks_hot(picked_ref, block * rows, rows)
    grads = grad_ref[...] + dense_tn(hot, high) + dense_tn(hot, rest)
    final_ref[...] = grads

    @pl.when((block == 0) & (seq == 0))
    def _():
        sums_ref[...] = jnp.zeros_like(sums_ref)
        hidden_sum_ref[...] = jnp.zeros_like(hidden_sum_ref)

    @pl.when(alive)
    def _():
        vectors = vector_ref[...].astype(jnp.float32).T
        unit_rows, spread = norm_parts(joined_two_ref[...])
        grad_two, gain_two, shift_two = norm_back(grads, unit_rows, spread, vectors[8:9])
        feed = grad_two.astype(jnp.bfloat16)
        feed_out[...] = feed
        back = grad_two
        for column in range(0, up_ref.shape[1], width):
            columns = slice(column, column + width)
            hidden = dense_nt(feed, down_ref[:, columns])
            hidden = (hidden * slope_ref[:, columns].astype(jnp.float32)).astype(jnp.bfloat16)
            hidden_out[:, columns] = hidden
            hidden_sum_ref[:, columns] += eight_rows(hidden.astype(jnp.float32))
            back = back + dense_nt(hidden, up_ref[:, columns])
        unit_rows, spread = norm_parts(joined_one_ref[...])
        grad_one, gain_one, shift_one = norm_back(back, unit_rows, spread, vectors[5:6])
        joined_out[...] = grad_one
        attention = grad_one.astype(jnp.bfloat16)
        attention_out[...] = attention
        mixed_out[...] = dense_nt(attention, out_ref[...]).astype(jnp.bfloat16)
        sums_ref[0] += eight_rows(attention.astype(jnp.float32))
        sums_ref[1] += gain_one
        sums_ref[2] += shift_one
        sums_ref[3] += eight_rows(feed.astype(jnp.float32))
        sums_ref[4] += gain_two
        sums_ref[5] += shift_two

    @pl.when(jnp.logical_not(alive))
    def _():
        for ref in (joined_out, mixed_out, attention_out, feed_out, hidden_out):
            ref[...] = jnp.zeros_like(ref)


def leave_kernel(
    length_ref,
    keep_ref,
    query_ref,
    key_ref,
    value_ref,
    joined_ref,
    final_ref,
    embedded_ref,
    vector_ref,
    weight_ref,
    rows_ref,
    place_ref,
    sums_ref,
    place_sum,
):
    block, seq = pl.program_id(0), pl.program_id(1)
    rows, width = joined_ref.shape
    alive = length_ref[seq] > block * rows
    vectors = vector_ref[...].astype(jnp.float32).T
    dropped = (keep_ref[seq] == 0).astype(jnp.float32)

    @pl.when((block == 0) & (seq == 0))
    def _():
        sums_ref[...] = jnp.zeros_like(sums_ref)

    @pl.when(seq == 0)
    def _():
        place_sum[...] = jnp.zeros_like(place_sum)

    def finish(grads):
        unit_rows, spread = norm_parts(embedded_ref[...])
        grads, gain, shift = norm_back(grads, unit_rows, spread, vectors[0:1])
        sums_ref[0] += gain
        sums_ref[1] += shift
        rows_ref[...] = grads.astype(jnp.bfloat16)
        place_sum[...] += grads

    @pl.when(alive)
    def _():
        grads = joined_ref[...]
        for part, ref in enumerate((query_ref, key_ref, value_ref)):
            grads = grads + dense_nt(ref[...], weight_ref[:, part * width : (part + 1) * width])
        sums_ref[2] += eight_rows(query_ref[...].astype(jnp.float32))
        sums_ref[3] += eight_rows(value_ref[...].astype(jnp.float32))
        finish(grads)

    @pl.when(jnp.logical_not(alive))
    def _():
        finish(final_ref[...] * dropped)

    @pl.when(seq == pl.num_programs(1) - 1)
    def _():
        place_ref[...] = place_sum[...].T.astype(jnp.bfloat16)


def deal_out(product, member_ref, kept_ref, given_ref, halves):
    halves[...] = product.reshape(halves.shape).astype(halves.dtype)
    member = member_ref[0]
    kept_ref[0] = halves[:, member]
    given_ref[0] = halves[:, 1 - member]


def early_kernel(
    member_ref,
    mixed_ref,
    attention_ref,
    normed_ref,
    hidden_ref,
    active_ref,
    feed_ref,
    kept_ref,
    given_ref,
    halves,
):
    place, blocks = pl.program_id(0), pl.num_programs(0) // 2
    cases = (
        (place == 0, mixed_ref, attention_ref),
        ((place > 0) & (place <= blocks), normed_ref, hidden_ref),
        (place > blocks, active_ref, feed_ref),
    )
    for wanted, left_ref, right_ref in cases:

        @pl.when(wanted)
        def _():
            product = dense_tn(left_ref[...], right_ref[...])
            deal_out(product, member_ref, kept_ref, given_ref, halves)


def late_kernel(
    member_ref,
    low_ref,
    query_ref,
    key_ref,
    value_ref,
    place_ref,
    sums_one_ref,
    sums_two_ref,
    up_ref,
    kept_ref,
    given_ref,
    halves,
    columns,
    vectors,
):
    for part, ref in enumerate((query_ref, key_ref, value_ref)):

        @pl.when(pl.program_id(0) == part)
        def _():
            product = dense_tn(low_ref[...], ref[...])
            deal_out(product, member_ref, kept_ref, given_ref, halves)

    @pl.when(pl.program_id(0) == 3)
    def _():
        vectors[...] = jnp.zeros_like(vectors)
        for row in range(4):
            vectors[row : row + 1, :] = jnp.sum(sums_two_ref[row], axis=0, keepdims=True)
        for row in range(6):
            vectors[4 + row : 5 + row, :] = jnp.sum(sums_one_ref[row], axis=0, keepdims=True)
        vectors[10:14, :] = up_ref[...]
        columns[...] = jnp.zeros_like(columns)
        width = place_ref.shape[1]
        columns[:, :width] = place_ref[...].astype(jnp.float32)
        columns[:, width : width + vectors.shape[0]] = vectors[...].T
        deal_out(columns[...], member_ref, kept_ref, given_ref, halves)


def head_grad_kernel(slope_ref, last_ref, chosen_ref, *grad_refs):
    count = len(grad_refs)
    for place, grad_ref in enumerate(grad_refs):
        source = last_ref if place == count - 2 else slope_ref

        @pl.when(pl.program_id(0) == place)
        def _():
            grad_ref[...] = dense_tn(source[0], chosen_ref[...]).astype(grad_ref.dtype)


def head_first_kernel(slope_ref, chosen_ref, grad_ref):
    grad_ref[...] = dense_tn(slope_ref[0], chosen_ref[...]).astype(grad_ref.dtype)


def row_kernel(kernel, prefetch, operands, outs, grid, scratch=()):
    return pl.pallas_call(
        kernel,
        out_shape=tuple(jax.ShapeDtypeStruct(shape, kind) for shape, kind, _, _ in outs),
        grid_spec=pltpu.PrefetchScalarGridSpec(
            num_scalar_prefetch=len(prefetch),
            grid=grid,
            in_specs=[pl.BlockSpec(block, where) for _, block, where in operands],
            out_specs=tuple(pl.BlockSpec(block, where) for _, _, block, where in outs),
            scratch_shapes=list(scratch),
        ),
        compiler_params=pltpu.CompilerParams(vmem_limit_bytes=VMEM),
        cost_estimate=NO_COST,
    )(*prefetch, *[array for array, _, _ in operands])


def parcel_kernel(own_rows, tiles, wide, source, parcel_ref, slots, sems):
    part, parts = pl.program_id(0), pl.num_programs(0)

    def first_tile(index):
        return jnp.minimum(own_rows * index // 128, tiles - wide)

    def fetch(index):
        lane = pl.multiple_of(first_tile(index) * 128, 128)
        slot = lax.rem(index, 2)
        return pltpu.make_async_copy(
            source.at[:, pl.ds(lane, wide * 128)],
            slots.at[slot, :, pl.ds(0, wide * 128)],
            sems.at[slot],
        )

    @pl.when(part == 0)
    def _():
        fetch(0).start()

    @pl.when(part + 1 < parts)
    def _():
        fetch(part + 1).start()

    fetch(part).wait()
    shift = own_rows * part - 128 * first_tile(part)
    slot, skip, turn = lax.rem(part, 2), shift // 128, lax.rem(128 - lax.rem(shift, 128), 128)
    n_pick, width = parcel_ref.shape[1:]
    lane = lax.broadcasted_iota(jnp.int32, (n_pick, 128), 1)

    def turned(tile):
        start = pl.multiple_of((tile + skip) * 128, 128)
        values = slots[slot, :, pl.ds(start, 128)].astype(jnp.float32)
        return pltpu.roll(values, turn, axis=1)

    low = turned(0)
    for tile in range(width // 128):
        high = turned(tile + 1)
        values = jnp.where(lane < 128 - lax.rem(shift, 128), low, high)
        values = jnp.where(lane + 128 * tile < own_rows, values, 0.0)
        parcel_ref[0, :, 128 * tile : 128 * (tile + 1)] = values.astype(jnp.bfloat16)
        low = high


def parcels_of(flat_teacher, own_rows, lanes, n_dev):
    n_pick, vocab = flat_teacher.shape
    tiles = vocab // 128
    wide = min(tiles, lanes // 128 + 1)
    return pl.pallas_call(
        functools.partial(parcel_kernel, own_rows, tiles, wide),
        out_shape=jax.ShapeDtypeStruct((n_dev, n_pick, lanes), jnp.bfloat16),
        grid=(n_dev,),
        in_specs=[pl.BlockSpec(memory_space=pl.ANY)],
        out_specs=pl.BlockSpec((1, n_pick, lanes), lambda r: (r, 0, 0)),
        scratch_shapes=[
            pltpu.VMEM((2, n_pick, (wide + 2) * 128), jnp.bfloat16),
            pltpu.SemaphoreType.DMA((2,)),
        ],
        compiler_params=pltpu.CompilerParams(vmem_limit_bytes=VMEM),
        cost_estimate=NO_COST,
    )(flat_teacher)


def head_kernel(steps, place_ref, chosen_ref, target_ref, *refs):
    tables = refs[:steps]
    before = refs[steps:-3]
    slope_ref, part_ref, loss_ref = refs[-3:]
    chosen = chosen_ref[...]
    senders, _, n_pick, _ = target_ref.shape
    total, loss = before[0][...] if before else None, None
    for step in range(steps):
        table = tables[step][...]
        width = table.shape[0]
        target = target_ref[:, place_ref[step]].reshape(senders * n_pick, -1)[:, :width]
        gap = dense_nt(chosen, table) - target.astype(jnp.float32)
        square = jnp.sum((gap * gap).reshape(-1, 8, width), axis=0)
        loss = square if loss is None else loss + square
        slope = (2.0 * gap).astype(jnp.bfloat16)
        slope_ref[step] = slope
        part = dense(slope, table)
        total = part if total is None else total + part
    part_ref[...] = total.astype(part_ref.dtype)

    @pl.when(pl.program_id(0) == 0)
    def _():
        loss_ref[...] = jnp.zeros_like(loss_ref)

    loss_ref[...] += loss


def head_products(places, all_chosen, targets, tables, before, part_type):
    n_dp, n_fs, n_pick, lanes = targets.shape
    row_width = all_chosen.shape[1]
    padded = tables[0].shape[0]
    rows, steps = 2 * n_pick, len(tables)
    whole = pl.BlockSpec((padded, row_width), lambda m, _: (0, 0))
    some = pl.BlockSpec((rows, row_width), lambda m, _: (m, 0))
    return pl.pallas_call(
        functools.partial(head_kernel, steps),
        out_shape=(
            jax.ShapeDtypeStruct((steps, n_dp * n_pick, padded), jnp.bfloat16),
            jax.ShapeDtypeStruct((n_dp * n_pick, row_width), part_type),
            jax.ShapeDtypeStruct((8, padded), jnp.float32),
        ),
        grid_spec=pltpu.PrefetchScalarGridSpec(
            num_scalar_prefetch=1,
            grid=(n_dp // 2,),
            in_specs=[
                some,
                pl.BlockSpec((2, n_fs, n_pick, lanes), lambda m, _: (m, 0, 0, 0)),
            ]
            + [whole] * steps
            + [some] * len(before),
            out_specs=(
                pl.BlockSpec((steps, rows, padded), lambda m, _: (0, m, 0)),
                some,
                pl.BlockSpec((8, padded), lambda m, _: (0, 0)),
            ),
        ),
        compiler_params=pltpu.CompilerParams(vmem_limit_bytes=VMEM),
        cost_estimate=NO_COST,
    )(places, all_chosen, targets, *tables, *before)


def sum_over_peers(part, axis):
    size, me = lax.axis_size(axis), lax.axis_index(axis)
    arrived = [lax.dynamic_index_in_dim(part, me, 1, False).astype(jnp.float32)]
    for apart in range(1, size):
        given = lax.dynamic_index_in_dim(part, me ^ apart, 1, False)
        got = lax.ppermute(given, axis, [(peer, peer ^ apart) for peer in range(size)])
        arrived.append(got.astype(jnp.float32))
    return sum(arrived)


def sum_in_pair(kept, given, pieces=1):
    swap = [(0, 1), (1, 0)]
    size = given.shape[0] // pieces
    got = [
        lax.ppermute(given[p * size : (p + 1) * size], "pair", swap) for p in range(pieces)
    ]
    got = got[0] if pieces == 1 else jnp.concatenate(got)
    return (kept.astype(jnp.float32) + got.astype(jnp.float32)).astype(jnp.bfloat16)


def sum_in_plane(part):
    part = sum_over_peers(part, "plane").astype(jnp.bfloat16)
    return part.reshape(part.shape[0], lax.axis_size("fsdp"), -1, part.shape[-1])


def sum_in_line(part):
    return sum_over_peers(part, "fsdp")


def route_plan(ids, live, own_rows, n_dev):
    place = jnp.arange(ids.shape[0])
    owner = ids // own_rows
    same = (ids[:, None] == ids[None, :]) & live[None, :]
    leader = jnp.min(jnp.where(same, place[None, :], ids.shape[0]), axis=1)
    first = live & (leader == place)
    before = (owner[:, None] == owner[None, :]) & (place[None, :] < leader[:, None])
    rank = jnp.sum(before & first[None, :], axis=1, dtype=jnp.int32)
    room = max(16, 1280 // n_dev)
    rounds = jnp.max(jnp.where(first, rank, 0)) // room + 1
    return ids, live, owner, first, rank, room, rounds, own_rows, n_dev


def slots_of(plan, turn):
    ids, live, owner, first, rank, room, rounds, own_rows, n_dev = plan
    here = live & (rank >= turn * room) & (rank < (turn + 1) * room)
    return jnp.where(here, owner * room + rank - turn * room, -1)


def exchange_wanted(plan, turn, axes):
    ids, live, owner, first, rank, room, rounds, own_rows, n_dev = plan
    slots = slots_of(plan, turn)
    local = jnp.where(first, ids - owner * own_rows + 1, 0)
    hit = jnp.arange(n_dev * room)[:, None] == slots[None, :]
    asked = jnp.max(jnp.where(hit, local[None, :], 0), axis=1) - 1
    message = jnp.concatenate(
        [
            asked.reshape(n_dev, room),
            jnp.broadcast_to(rounds, (n_dev, 128 - room)).astype(jnp.int32),
        ],
        axis=1,
    ).reshape(n_dev, 1, 128)
    heard = lax.all_to_all(message, axes, split_axis=0, concat_axis=0).reshape(n_dev, 128)
    return heard[:, :room].reshape(-1), jnp.max(heard[:, room:])


def ask_rows(plan, wanted, table_low, axes):
    room, own_rows, n_dev = plan[5], plan[7], plan[8]
    one_hot = (wanted[:, None] == jnp.arange(own_rows)[None, :]).astype(jnp.bfloat16)
    rows = dense(one_hot, table_low).astype(jnp.bfloat16)
    return lax.all_to_all(rows.reshape(n_dev, room, -1), axes, split_axis=0, concat_axis=0)


def place_rows(plan, turn, rows):
    room, n_dev = plan[5], plan[8]
    back = (slots_of(plan, turn)[:, None] == jnp.arange(n_dev * room)[None, :]).astype(
        jnp.bfloat16
    )
    return dense(back, rows.reshape(n_dev * room, -1))


def more_rows(plan, rounds, token_rows, table_low, axes):
    def body(state):
        turn, total = state
        wanted, _ = exchange_wanted(plan, turn, axes)
        rows = ask_rows(plan, wanted, table_low, axes)
        return turn + 1, total + place_rows(plan, turn, rows)

    return lax.while_loop(lambda state: state[0] < rounds, body, (jnp.int32(1), token_rows))[1]


def rows_to_give(plan, turn, flat_grad):
    room, n_dev = plan[5], plan[8]
    spread = (jnp.arange(n_dev * room)[:, None] == slots_of(plan, turn)[None, :]).astype(
        jnp.bfloat16
    )
    sums = dense(spread, flat_grad).astype(jnp.bfloat16)
    return sums.reshape(n_dev, room, -1)


def give_rows(sums, axes):
    got = lax.all_to_all(sums, axes, split_axis=0, concat_axis=0)
    return got.reshape(-1, sums.shape[-1])


def more_given(plan, rounds, flat_grad, own_rows, own_part, axes):
    def body(state):
        turn, total = state
        wanted, _ = exchange_wanted(plan, turn, axes)
        one_hot = (jnp.arange(own_part.shape[0])[:, None] == wanted[None, :]).astype(jnp.bfloat16)
        got = give_rows(rows_to_give(plan, turn, flat_grad), axes)
        return turn + 1, (total.astype(jnp.float32) + dense(one_hot, got)).astype(total.dtype)

    return lax.while_loop(lambda state: state[0] < rounds, body, (jnp.int32(1), own_part))[1]


def at_lane(tile, lane, value):
    row = lax.broadcasted_iota(jnp.int32, tile.shape, 0)
    column = lax.broadcasted_iota(jnp.int32, tile.shape, 1)
    return tile + jnp.where((row == 0) & (column == lane), value, 0.0)


def total_sum(values):
    return jnp.sum(jnp.sum(values, axis=0, keepdims=True), axis=1, keepdims=True)


def table_kernel(
    own_rows,
    wanted_ref,
    returned_ref,
    moved_ref,
    part_ref,
    tile_ref,
    hidden_loss_ref,
    head_loss_ref,
    last_loss_ref,
    out_ref,
    up_ref,
    down_ref,
    last_ref,
    grad_ref,
    place_ref,
    qkv_ref,
    vector_ref,
    sum_ref,
):
    rows = grad_ref.shape[0]
    first = pl.program_id(0) * rows
    spot = lax.broadcasted_iota(jnp.int32, (rows, wanted_ref.shape[1]), 0) + first
    hot = (spot == wanted_ref[...]).astype(jnp.bfloat16)
    grads = dense(hot, returned_ref[...])
    grads = grads + (moved_ref[...].astype(jnp.float32) + part_ref[...].astype(jnp.float32))
    row = lax.broadcasted_iota(jnp.int32, grads.shape, 0) + first
    grads = jnp.where(row < own_rows, grads, 0.0)
    grad_ref[...] = grads

    @pl.when(pl.program_id(0) == 0)
    def _():
        sum_ref[...] = tile_ref[...]
        for loss_ref in (hidden_loss_ref, head_loss_ref, last_loss_ref):
            sum_ref[...] = at_lane(sum_ref[...], 1, total_sum(loss_ref[...]))
        width, places = last_ref.shape[2], place_ref.shape[1]
        for part in range(3):
            qkv_ref[:, part * width : (part + 1) * width] = last_ref[part]
        place_ref[...] = last_ref[3][:, :places]
        vectors = last_ref[3][:, places : places + 128].T
        vector_ref[...] = vectors[: vector_ref.shape[0], :]
        for other in (out_ref, up_ref, down_ref, place_ref, qkv_ref, vector_ref):
            sum_ref[...] = at_lane(sum_ref[...], 0, total_sum(other[...] * other[...]))

    sum_ref[...] = at_lane(sum_ref[...], 0, total_sum(grads * grads))


def update_kernel(own_rows, steps, every_ref, *refs):
    weights, grads, firsts, seconds = [refs[7 * k : 7 * k + 7] for k in range(4)]
    moments, squares, updates = [refs[7 * k : 7 * k + 7] for k in range(4, 7)]
    total_ref, sum_ref = refs[49:]
    totals = jnp.sum(every_ref[...], axis=0)
    count = totals[0:1, 2:3]
    norm = jnp.sqrt(totals[0:1, 0:1]) / count
    factor = jnp.minimum(1.0, CLIP_NORM / norm) / count

    def step(place, live=None):
        weight = weights[place][...]
        clipped = grads[place][...] * factor
        moment = BETA_ONE * firsts[place][...] + (1.0 - BETA_ONE) * clipped
        square = BETA_TWO * seconds[place][...] + (1.0 - BETA_TWO) * clipped * clipped
        update = (
            moment
            * (1.0 / (1.0 - BETA_ONE**STEP))
            / (jnp.sqrt(square * (1.0 / (1.0 - BETA_TWO**STEP))) + ADAM_EPS)
            + DECAY_RATE * weight
        )
        moments[place][...] = moment
        squares[place][...] = square
        updates[place][...] = update
        if live is not None:
            update = jnp.where(live, update, 0.0)
        sum_ref[...] = at_lane(sum_ref[...], place, total_sum(update * update))

    @pl.when(pl.program_id(0) == 0)
    def _():
        total_ref[...] = at_lane(totals, 127, norm)
        sum_ref[...] = jnp.zeros_like(sum_ref)

    for place in range(1, 7):

        @pl.when(pl.program_id(0) == place % steps)
        def _():
            step(place)

    row = lax.broadcasted_iota(jnp.int32, weights[0].shape, 0)
    step(0, row + pl.program_id(0) * weights[0].shape[0] < own_rows)


def weight_kernel(steps, every_ref, total_ref, *refs):
    weights, updates, outs = refs[:7], refs[7:14], refs[14:21]
    sum_ref = refs[21]
    update_norms = jnp.sqrt(jnp.sum(every_ref[...], axis=0))

    def step(place):
        norm = jnp.sqrt(total_ref[0:1, 3 + place : 4 + place])
        ratio = LEARN_RATE * (norm / update_norms[0:1, place : place + 1])
        outs[place][...] = weights[place][...] - ratio * updates[place][...]

    @pl.when(pl.program_id(0) == 0)
    def _():
        sum_ref[...] = update_norms

    for place in range(1, 7):

        @pl.when(pl.program_id(0) == place % steps)
        def _():
            step(place)

    step(0)


def hidden_order(values, row_width):
    lead = values.shape[:-1]
    return jnp.swapaxes(values.reshape(lead + (row_width, -1)), -1, -2).reshape(lead + (-1,))


def hidden_back(values, row_width):
    lead = values.shape[:-1]
    return jnp.swapaxes(values.reshape(lead + (-1, row_width)), -1, -2).reshape(lead + (-1,))


def column_blocks(values, row_width):
    return [values[:, c : c + row_width] for c in range(0, values.shape[1], row_width)]


def on_device(
    token_ids,
    true_mask,
    keep_layer,
    picked,
    teacher_hidden,
    teacher_logits,
    embed_table,
    pos_table,
    query_key_value_weight,
    output_weight,
    up_weight,
    down_weight,
    gains_biases,
    first_embed,
    first_pos,
    first_qkv,
    first_out,
    first_up,
    first_down,
    first_gains,
    second_embed,
    second_pos,
    second_qkv,
    second_out,
    second_up,
    second_down,
    second_gains,
):
    axes = AXES
    n_dp, n_fs = lax.axis_size(SPLIT), lax.axis_size("fsdp")
    n_dev = n_dp * n_fs
    i_fs = lax.axis_index("fsdp")
    masters = (
        embed_table,
        pos_table,
        query_key_value_weight,
        output_weight,
        up_weight,
        down_weight,
        gains_biases,
    )
    firsts = (first_embed, first_pos, first_qkv, first_out, first_up, first_down, first_gains)
    seconds = (
        second_embed,
        second_pos,
        second_qkv,
        second_out,
        second_up,
        second_down,
        second_gains,
    )
    seq_count, seq_len = token_ids.shape
    own_rows, row_width = embed_table.shape
    ff = up_weight.shape[1]
    in_rows = query_key_value_weight.shape[0]
    n_tok = seq_count * seq_len
    n_pick = picked.shape[0] * picked.shape[1]
    vocab = own_rows * n_dev
    block_rows = own_rows * n_fs

    table_low = embed_table.astype(jnp.bfloat16)
    pack_width = 3 * row_width + row_width + ff + ff + seq_len
    gain_width = -(-14 // 128) * 128
    packed_low = jnp.concatenate(
        [
            query_key_value_weight,
            output_weight,
            hidden_order(up_weight, row_width),
            down_weight.reshape(in_rows, ff),
            pos_table.T,
            jnp.pad(gains_biases.T, ((0, 0), (0, gain_width - 14))),
        ],
        axis=1,
    ).astype(jnp.bfloat16)
    gathered = lax.all_gather(packed_low, axes, axis=0, tiled=True)
    plan = route_plan(token_ids.reshape(-1), true_mask.reshape(-1) > 0, own_rows, n_dev)
    wanted, rounds = exchange_wanted(plan, 0, axes)
    ring = [(z, (z + 1) % n_fs) for z in range(n_fs)]
    padded = -(-own_rows // 16) * 16
    lanes = -(-own_rows // 128) * 128
    first_table = jnp.pad(table_low, ((0, padded - own_rows), (0, 0)))
    arrived = ask_rows(plan, wanted, table_low, axes)

    targets = parcels_of(teacher_logits.reshape(n_pick, vocab), own_rows, lanes, n_dev)
    arrived, targets = lax.optimization_barrier((arrived, targets))
    targets = lax.all_to_all(
        targets.reshape(n_dp, n_fs, n_pick, lanes), SPLIT, split_axis=0, concat_axis=0
    )
    tile = jnp.zeros((8, 128), jnp.float32)
    scalars = [jnp.sum(true_mask.astype(jnp.float32))]
    scalars += [jnp.sum(member * member) for member in masters]
    for place, value in enumerate(scalars):
        tile = at_lane(tile, place + 2, value)
    arrived, first_table, tile = lax.optimization_barrier((arrived, first_table, tile))
    tables = [first_table, lax.ppermute(first_table, "fsdp", ring)]

    i_dp = lax.axis_index(SPLIT)
    token_rows = place_rows(plan, 0, arrived)
    token_rows = more_rows(plan, rounds, token_rows, table_low, axes)

    def pass_table(*later):
        newest, *later = lax.optimization_barrier((tables[-1], *later))
        if len(tables) < n_fs:
            tables.append(lax.ppermute(newest, "fsdp", ring))
        return later

    places = lax.rem(i_fs - jnp.arange(n_fs, dtype=jnp.int32) + n_fs, n_fs)

    rows = seq_len // 2
    n_block = seq_len // rows
    keeps = (keep_layer > 0).astype(jnp.int32)
    trues = jnp.sum(true_mask, axis=1)
    lengths = trues * keeps
    pick_column = picked.reshape(-1, 1)
    bf16, f32 = jnp.bfloat16, jnp.float32

    def by_seq(width, array=None):
        spec = ((rows, width), lambda s, b, *_: (s * n_block + b, 0))
        return spec if array is None else (array, *spec)

    def by_block(width, array=None):
        spec = ((rows, width), lambda b, s, *_: (s * n_block + b, 0))
        return spec if array is None else (array, *spec)

    def whole(shape):
        return (shape, lambda *_: (0,) * len(shape))

    def weight(width, place):
        return (gathered, (row_width, width), lambda *_: (0, place))

    (gathered,) = pass_table(gathered)
    vectors = weight(gain_width, pack_width // gain_width)
    qkv_weight = weight(3 * row_width, 0)
    out_weight = weight(row_width, 3)
    up_weight_low, down_weight_low = weight(ff, 1), weight(ff, 2)
    first_place = (4 * row_width + 2 * ff) // rows
    embedded, flat_in, flat_low, packed = row_kernel(
        enter_kernel,
        (lengths,),
        [
            by_block(row_width, token_rows),
            (gathered, (row_width, rows), lambda b, s, *_: (0, first_place + b)),
            vectors,
            qkv_weight,
        ],
        [
            ((n_tok, row_width), f32, *by_block(row_width)),
            ((n_tok, row_width), f32, *by_block(row_width)),
            ((n_tok, row_width), bf16, *by_block(row_width)),
            ((n_tok, 3 * row_width), bf16, *by_block(3 * row_width)),
        ],
        (n_block, seq_count),
    )
    mixed_output = attend(lengths, packed)
    up_bias = hidden_order(
        gathered[:, pack_width + 10 : pack_width + 14].astype(f32).T.reshape(1, -1), row_width
    )
    pick_count = picked.shape[1]
    picks = (pick_column, (pick_count, 1), lambda s, b, *_: (s, 0))
    (
        joined_one,
        normed_low,
        gelu_slopes,
        gelu_activated,
        joined_two,
        grad_start,
        chosen,
        hidden_loss,
    ) = row_kernel(
        feed_kernel,
        (lengths, trues),
        [
            by_seq(row_width, mixed_output),
            by_seq(row_width, flat_in),
            by_seq(row_width, teacher_hidden.reshape(n_tok, row_width)),
            picks,
            vectors,
            (up_bias, *whole((1, ff))),
            out_weight,
            up_weight_low,
            down_weight_low,
        ],
        [
            ((n_tok, row_width), f32, *by_seq(row_width)),
            ((n_tok, row_width), bf16, *by_seq(row_width)),
            ((n_tok, ff), bf16, *by_seq(ff)),
            ((n_tok, ff), bf16, *by_seq(ff)),
            ((n_tok, row_width), f32, *by_seq(row_width)),
            ((n_tok, row_width), f32, *by_seq(row_width)),
            ((n_pick, row_width), bf16, (pick_count, row_width), lambda s, b, *_: (s, 0)),
            ((8, row_width), f32, *whole((8, row_width))),
        ],
        (seq_count, n_block),
        [pltpu.VMEM((rows, row_width), f32)],
    )

    if n_fs > 2:
        (chosen,) = pass_table(chosen)
    all_chosen = lax.all_gather(chosen, SPLIT, axis=0, tiled=True)
    while len(tables) < n_fs:
        (all_chosen,) = pass_table(all_chosen)
    slopes, chosen_part, head_loss = head_products(
        places[:-1], all_chosen, targets, tables[:-1], [], jnp.float32
    )
    last_slopes, chosen_part, last_loss = head_products(
        places[-1:], all_chosen, targets, tables[-1:], [chosen_part], jnp.bfloat16
    )
    many = n_dp * n_pick
    all_picked = (all_chosen, (many, row_width), lambda d: (0, 0))
    (head_part,) = row_kernel(
        head_first_kernel,
        (),
        [(slopes, (1, many, padded), lambda d: (1, 0, 0)), all_picked],
        [((padded, row_width), bf16, (padded, row_width), lambda d: (0, 0))],
        (1,),
    )
    head_sums = [lax.ppermute(head_part, "fsdp", ring)]
    last_slopes, grad_chosen = lax.optimization_barrier((last_slopes, chosen_part))
    grad_chosen = lax.all_to_all(
        grad_chosen.reshape(n_dp, n_pick, row_width), SPLIT, split_axis=0, concat_axis=0
    )
    head_parts = row_kernel(
        head_grad_kernel,
        (),
        [
            (
                slopes,
                (1, many, padded),
                lambda d: (jnp.where(d < n_fs - 3, d + 2, 0), 0, 0),
            ),
            (last_slopes, (1, many, padded), lambda d: (0, 0, 0)),
            all_picked,
        ],
        [((padded, row_width), bf16, (padded, row_width), lambda d: (0, 0))] * (n_fs - 1),
        (n_fs - 1,),
    )

    def pass_sum(*later):
        newest, *later = lax.optimization_barrier((head_sums[-1], *later))
        step = len(head_sums)
        if step + 1 < n_fs:
            total = newest.astype(f32) + head_parts[step - 1].astype(f32)
            head_sums.append(lax.ppermute(total.astype(bf16), "fsdp", ring))
        return later

    grad_chosen, *head_parts = pass_sum(grad_chosen, *head_parts)
    for _ in range(n_fs - 4):
        (grad_chosen,) = pass_sum(grad_chosen)

    (
        grad_final,
        grad_joined_one,
        grad_mixed,
        grad_attention,
        grad_feed,
        grad_hidden,
        sums_one,
        hidden_sums,
    ) = row_kernel(
        unfeed_kernel,
        (lengths,),
        [
            by_seq(row_width, grad_start),
            (grad_chosen, (n_dp, pick_count, row_width), lambda s, b, *_: (0, s, 0)),
            picks,
            by_seq(row_width, joined_one),
            by_seq(ff, gelu_slopes),
            by_seq(row_width, joined_two),
            vectors,
            out_weight,
            up_weight_low,
            down_weight_low,
        ],
        [
            ((n_tok, row_width), f32, *by_seq(row_width)),
            ((n_tok, row_width), f32, *by_seq(row_width)),
            ((n_tok, row_width), bf16, *by_seq(row_width)),
            ((n_tok, row_width), bf16, *by_seq(row_width)),
            ((n_tok, row_width), bf16, *by_seq(row_width)),
            ((n_tok, ff), bf16, *by_seq(ff)),
            ((6, 8, row_width), f32, *whole((6, 8, row_width))),
            ((8, ff), f32, *whole((8, ff))),
        ],
        (seq_count, n_block),
    )
    member = lax.axis_index("pair").reshape(1).astype(jnp.int32)
    n_plane = lax.axis_size("plane")
    share = row_width // (2 * n_plane)
    halves = pltpu.VMEM((n_plane, 2, share, row_width), bf16)

    def dealt(columns):
        out = (
            (columns, n_plane, share, row_width),
            bf16,
            (1, n_plane, share, row_width),
            lambda j, *_: (j, 0, 0, 0),
        )
        return [out, out]

    def full(array):
        return (array, *whole(array.shape))

    blocks = ff // row_width
    early_kept, early_given = row_kernel(
        early_kernel,
        (member,),
        [
            full(mixed_output),
            full(grad_attention),
            full(normed_low),
            (
                grad_hidden,
                (n_tok, row_width),
                lambda j, *_: (0, jnp.clip(j - 1, 0, blocks - 1)),
            ),
            (
                gelu_activated,
                (n_tok, row_width),
                lambda j, *_: (0, jnp.clip(j - 1 - blocks, 0, blocks - 1)),
            ),
            full(grad_feed),
        ],
        dealt(1 + 2 * blocks),
        (1 + 2 * blocks,),
        [halves],
    )
    up_rows = hidden_back(jnp.sum(hidden_sums, axis=0, keepdims=True), row_width)
    early_kept, early_given = pass_sum(early_kept, early_given)
    early = sum_in_pair(early_kept, early_given)
    grad_mixed, early, up_rows = lax.optimization_barrier((grad_mixed, early, up_rows))
    early = sum_in_plane(early)
    *grad_parts, head_sums[-1] = lax.optimization_barrier(
        (*attend(lengths, packed, grad_mixed), head_sums[-1])
    )
    flat_grad, place_grad, sums_two = row_kernel(
        leave_kernel,
        (lengths, keeps),
        [by_block(row_width, part) for part in grad_parts]
        + [
            by_block(row_width, grad_joined_one),
            by_block(row_width, grad_final),
            by_block(row_width, embedded),
            vectors,
            qkv_weight,
        ],
        [
            ((n_tok, row_width), bf16, *by_block(row_width)),
            ((row_width, seq_len), bf16, (row_width, rows), lambda b, s, *_: (0, b)),
            ((4, 8, row_width), f32, *whole((4, 8, row_width))),
        ],
        (n_block, seq_count),
        [pltpu.VMEM((rows, row_width), f32)],
    )
    flat_grad, early = lax.optimization_barrier((flat_grad, early))
    early = lax.psum_scatter(
        early.reshape(early.shape[0], -1, row_width), "fsdp", scatter_dimension=1, tiled=True
    ).astype(f32)
    given_rows = rows_to_give(plan, 0, flat_grad)
    given_rows, *grad_parts = lax.optimization_barrier((given_rows, *grad_parts))
    returned = give_rows(given_rows, axes)
    own_part = more_given(plan, rounds, flat_grad, own_rows, head_parts[n_fs - 2], axes)
    late_kept, late_given = row_kernel(
        late_kernel,
        (member,),
        [full(flat_low)]
        + [full(part) for part in grad_parts]
        + [
            full(place_grad),
            full(sums_one),
            full(sums_two),
            full(up_rows.reshape(4, row_width)),
        ],
        dealt(4),
        (4,),
        [
            halves,
            pltpu.VMEM((row_width, row_width), f32),
            pltpu.VMEM((gain_width, row_width), f32),
        ],
    )
    late_kept, late_given, own_part = lax.optimization_barrier(
        (late_kept, late_given, own_part)
    )
    last = sum_in_plane(sum_in_pair(late_kept, late_given, 4))
    early, last = lax.optimization_barrier((early, last))
    last = sum_in_line(last)
    early_grads = (
        early[0],
        jnp.transpose(early[1 : 1 + blocks], (1, 2, 0)).reshape(in_rows, ff),
        jnp.swapaxes(early[1 + blocks :], 0, 1).reshape(-1, row_width),
    )
    rows = 208
    steps = -(-own_rows // rows)

    def by_row(array=None, width=row_width):
        spec = ((rows, width), lambda r, *_: (r, 0))
        return spec if array is None else (array, *spec)

    table_grad, place_sums, qkv_sums, vector_sums, tile = row_kernel(
        functools.partial(table_kernel, own_rows),
        (),
        [
            full(wanted.reshape(1, -1)),
            full(returned),
            by_row(head_sums[-1]),
            by_row(own_part),
            full(tile),
            full(hidden_loss),
            full(head_loss),
            full(last_loss),
        ]
        + [full(grad) for grad in early_grads]
        + [full(last)],
        [
            ((own_rows, row_width), f32, *by_row()),
            ((in_rows, seq_len), f32, *whole((in_rows, seq_len))),
            ((in_rows, 3 * row_width), f32, *whole((in_rows, 3 * row_width))),
            (gains_biases.shape, f32, *whole(gains_biases.shape)),
            ((8, 128), f32, *whole((8, 128))),
        ],
        (steps,),
    )

    def exchange(tile):
        return lax.all_to_all(
            jnp.broadcast_to(tile[None], (n_dev, 8, 128)), axes, split_axis=0, concat_axis=0
        )

    def turned(arrays):
        return [array.T if place == 1 else array for place, array in enumerate(arrays)]

    def specs(arrays):
        return [by_row(arrays[0])] + [full(array) for array in arrays[1:]]

    weights = turned(masters)
    like = [
        (array.shape, f32, *(whole(array.shape) if place else by_row()))
        for place, array in enumerate(weights)
    ]
    tile_out = ((8, 128), f32, *whole((8, 128)))
    *results, totals, tile = row_kernel(
        functools.partial(update_kernel, own_rows, steps),
        (),
        [full(exchange(tile))]
        + specs(weights)
        + specs([table_grad, place_sums, qkv_sums, *early_grads, vector_sums])
        + specs(turned(firsts))
        + specs(turned(seconds)),
        like * 3 + [tile_out, tile_out],
        (steps,),
    )
    new_moments, new_squares = turned(results[:7]), turned(results[7:14])
    *new_weights, update_norms = row_kernel(
        functools.partial(weight_kernel, steps),
        (),
        [full(exchange(tile)), full(totals)] + specs(weights) + specs(results[14:]),
        like + [tile_out],
        (steps,),
    )
    new_weights = turned(new_weights)
    loss_sum, token_count, grad_norm = totals[0, 1], totals[0, 2], totals[0, 127]
    matrix_norms = jnp.stack([jnp.sqrt(totals[0, 3:10]), update_norms[0, :7]])
    return (
        loss_sum,
        token_count,
        grad_norm,
        new_weights[0],
        new_weights[1],
        new_weights[2],
        new_weights[3],
        new_weights[4],
        new_weights[5],
        new_weights[6],
        new_moments[0],
        new_moments[1],
        new_moments[2],
        new_moments[3],
        new_moments[4],
        new_moments[5],
        new_moments[6],
        new_squares[0],
        new_squares[1],
        new_squares[2],
        new_squares[3],
        new_squares[4],
        new_squares[5],
        new_squares[6],
        matrix_norms,
    )


def solution(mesh):
    split = Mesh(
        mesh.devices.reshape(mesh.shape["dp"] // 2, 2, mesh.shape["fsdp"]), AXES
    )
    placed = (
        P(AXES, None),
        P(AXES, None),
        P(AXES),
        P(AXES, None),
        P(AXES, None, None),
        P(AXES, None, None),
        P(AXES, None),
        P(None, AXES),
        P(AXES, None),
        P(AXES, None),
        P(AXES, None),
        P(AXES, None),
        P(None, AXES),
        P(AXES, None),
        P(None, AXES),
        P(AXES, None),
        P(AXES, None),
        P(AXES, None),
        P(AXES, None),
        P(None, AXES),
        P(AXES, None),
        P(None, AXES),
        P(AXES, None),
        P(AXES, None),
        P(AXES, None),
        P(AXES, None),
        P(None, AXES),
    )
    return jax.shard_map(
        on_device,
        mesh=split,
        in_specs=placed,
        out_specs=(
            P(),
            P(),
            P(),
            P(AXES, None),
            P(None, AXES),
            P(AXES, None),
            P(AXES, None),
            P(AXES, None),
            P(AXES, None),
            P(None, AXES),
            P(AXES, None),
            P(None, AXES),
            P(AXES, None),
            P(AXES, None),
            P(AXES, None),
            P(AXES, None),
            P(None, AXES),
            P(AXES, None),
            P(None, AXES),
            P(AXES, None),
            P(AXES, None),
            P(AXES, None),
            P(AXES, None),
            P(None, AXES),
            P(),
        ),
        check_vma=False,
    )
```

```python
import functools

import jax
import jax.numpy as jnp
from jax import lax
from jax.experimental import pallas as pl
from jax.experimental.pallas import tpu as pltpu
from jax.sharding import Mesh
from jax.sharding import PartitionSpec as P

H = 12
HD = 64
STEP = 10


NORM_EPS = 1e-05
CLIP_NORM = 0.5
BETA_ONE = 0.9
BETA_TWO = 0.999
ADAM_EPS = 1e-06
DECAY_RATE = 0.01
LEARN_RATE = 0.3
MASKED_SCORE = -1e30

SPLIT = ("plane", "pair")
AXES = ("plane", "pair", "fsdp")
VMEM = 60 * 2**20
NO_COST = pl.CostEstimate(flops=0, bytes_accessed=0, transcendentals=0)


def normal_cdf(values):
    return 0.5 + 0.5 * lax.erf(values * 0.5**0.5)


def dense(left_op, right_op):
    return jnp.dot(left_op, right_op, preferred_element_type=jnp.float32)


def dense_tn(left_op, right_op):
    return lax.dot_general(
        left_op, right_op, (((0,), (0,)), ((), ())), preferred_element_type=jnp.float32
    )


def dense_nt(left_op, right_op):
    return lax.dot_general(
        left_op, right_op, (((1,), (1,)), ((), ())), preferred_element_type=jnp.float32
    )


def pair_lanes(shape, member):
    lane = lax.broadcasted_iota(jnp.int32, shape, 1)
    return (lane >= HD) if member else (lane < HD)


def softmax_rows(query_rows, key_rows, length):
    scores = dense_nt(query_rows, key_rows)
    spot = lax.broadcasted_iota(jnp.int32, (1, scores.shape[1]), 1)
    scores = scores + jnp.where(spot < length, 0.0, MASKED_SCORE)
    exponent = jnp.exp(scores - jnp.max(scores, axis=1, keepdims=True))
    return exponent * (1.0 / jnp.sum(exponent, axis=1, keepdims=True))


def softmax_columns(key_rows, query_rows, length):
    scores = dense_nt(key_rows, query_rows)
    spot = lax.broadcasted_iota(jnp.int32, (scores.shape[0], 1), 0)
    scores = scores + jnp.where(spot < length, 0.0, MASKED_SCORE)
    exponent = jnp.exp(scores - jnp.max(scores, axis=0, keepdims=True))
    return exponent * (1.0 / jnp.sum(exponent, axis=0, keepdims=True))


def row_spans(seq_len):
    half = seq_len // 2
    return ((0, half), (half, seq_len))


def mix_kernel(length_ref, query_ref, key_ref, value_ref, mixed_ref):
    seq_len = query_ref.shape[0]
    length = length_ref[pl.program_id(0)]

    for low, high in row_spans(seq_len):

        @pl.when((length > low) & (length <= high))
        def _():
            step = high
            keys, values = key_ref[0:high, :], value_ref[0:high, :]
            for row in range(0, high, step):
                queries = query_ref[row : row + step, :] * 0.125
                parts = []
                for member in (0, 1):
                    lanes = pair_lanes(queries.shape, member)
                    chance = softmax_rows(
                        jnp.where(lanes, queries, jnp.zeros_like(queries)), keys, length
                    )
                    parts.append(dense(chance.astype(jnp.bfloat16), values))
                mixed_ref[row : row + step, :] = jnp.where(
                    pair_lanes(parts[0].shape, 1), parts[1], parts[0]
                ).astype(jnp.bfloat16)
            if high < seq_len:
                mixed_ref[high:, :] = jnp.zeros((seq_len - high, 2 * HD), jnp.bfloat16)

    @pl.when(length == 0)
    def _():
        mixed_ref[...] = jnp.zeros_like(mixed_ref)


def unmix_kernel(
    length_ref, query_ref, key_ref, value_ref, grad_ref, query_out, key_out, value_out
):
    seq_len = query_ref.shape[0]
    length = length_ref[pl.program_id(0)]
    outs = (query_out, key_out, value_out)

    for low, high in row_spans(seq_len):

        @pl.when((length > low) & (length <= high))
        def _():
            step = high
            keys, values = key_ref[0:high, :], value_ref[0:high, :]
            key_total, value_total = None, None
            for row in range(0, high, step):
                plain = query_ref[row : row + step, :]
                queries = plain * 0.125
                grads = grad_ref[row : row + step, :]
                parts = []
                for member in (0, 1):
                    lanes = pair_lanes(queries.shape, member)
                    zero = jnp.zeros_like(queries)
                    chance = softmax_columns(keys, jnp.where(lanes, queries, zero), length)
                    slope = dense_nt(values, jnp.where(lanes, grads, zero))
                    slope = chance * (slope - jnp.sum(slope * chance, axis=0, keepdims=True))
                    slope = slope.astype(jnp.bfloat16)
                    parts.append(
                        (
                            dense_tn(slope, keys),
                            dense(slope, plain),
                            dense(chance.astype(jnp.bfloat16), grads),
                        )
                    )
                query_part, key_part, value_part = [
                    jnp.where(pair_lanes(first.shape, 1), second, first)
                    for first, second in zip(*parts)
                ]
                query_out[row : row + step, :] = (query_part * 0.125).astype(jnp.bfloat16)
                key_total = key_part if key_total is None else key_total + key_part
                value_total = value_part if value_total is None else value_total + value_part
            key_out[0:high, :] = (key_total * 0.125).astype(jnp.bfloat16)
            value_out[0:high, :] = value_total.astype(jnp.bfloat16)
            if high < seq_len:
                for ref in outs:
                    ref[high:, :] = jnp.zeros((seq_len - high, 2 * HD), jnp.bfloat16)

    @pl.when(length == 0)
    def _():
        for ref in outs:
            ref[...] = jnp.zeros_like(ref)


def attend(lengths, packed, grad_mixed=None):
    seq_count = lengths.shape[0]
    seq_len = packed.shape[0] // seq_count
    pairs = H // 2

    def block(first):
        return pl.BlockSpec((seq_len, 2 * HD), lambda s, h, _: (s, first + h))

    out = jax.ShapeDtypeStruct((packed.shape[0], H * HD), jnp.bfloat16)
    forward = grad_mixed is None
    operands = (packed, packed, packed) + (() if forward else (grad_mixed,))
    return pl.pallas_call(
        mix_kernel if forward else unmix_kernel,
        out_shape=out if forward else (out, out, out),
        grid_spec=pltpu.PrefetchScalarGridSpec(
            num_scalar_prefetch=1,
            grid=(seq_count, pairs),
            in_specs=[block(0), block(pairs), block(2 * pairs)] + ([] if forward else [block(0)]),
            out_specs=block(0) if forward else (block(0),) * 3,
        ),
        compiler_params=pltpu.CompilerParams(vmem_limit_bytes=VMEM),
        cost_estimate=NO_COST,
    )(lengths, *operands)


def norm_parts(values):
    centered = values - jnp.mean(values, axis=1, keepdims=True)
    spread = lax.rsqrt(jnp.mean(centered * centered, axis=1, keepdims=True) + NORM_EPS)
    return centered * spread, spread


def norm_back(grads, unit_rows, spread, gain_row):
    scaled = grads * gain_row
    inner = jnp.mean(scaled * unit_rows, axis=1, keepdims=True)
    rows = spread * (scaled - jnp.mean(scaled, axis=1, keepdims=True) - unit_rows * inner)
    return rows, eight_rows(grads * unit_rows), eight_rows(grads)


def eight_rows(values):
    return jnp.sum(values.reshape(-1, 8, values.shape[1]), axis=0)


def picks_hot(picked_ref, first_row, rows):
    spot = lax.broadcasted_iota(jnp.int32, (picked_ref.shape[0], rows), 1) + first_row
    return (picked_ref[...] == spot).astype(jnp.bfloat16)


def enter_kernel(
    length_ref, token_ref, place_ref, vector_ref, weight_ref, embedded_ref, input_ref, low_ref, packed_ref
):
    block, seq = pl.program_id(0), pl.program_id(1)
    rows = token_ref.shape[0]
    vectors = vector_ref[...].astype(jnp.float32).T
    embedded = token_ref[...] + place_ref[...].astype(jnp.float32).T
    embedded_ref[...] = embedded
    inputs = norm_parts(embedded)[0] * vectors[0:1] + vectors[1:2]
    input_ref[...] = inputs
    low = inputs.astype(jnp.bfloat16)
    low_ref[...] = low

    @pl.when(length_ref[seq] > block * rows)
    def _():
        width = low.shape[1]
        for part, bias in enumerate((vectors[2:3], None, vectors[3:4])):
            columns = slice(part * width, (part + 1) * width)
            values = dense(low, weight_ref[:, columns])
            if bias is not None:
                values = values + bias
            packed_ref[:, columns] = values.astype(jnp.bfloat16)


def feed_kernel(
    length_ref,
    true_ref,
    mixed_ref,
    input_ref,
    teacher_ref,
    picked_ref,
    vector_ref,
    bias_ref,
    out_ref,
    up_ref,
    down_ref,
    joined_one_ref,
    normed_ref,
    slope_ref,
    active_ref,
    joined_two_ref,
    grad_ref,
    chosen_ref,
    loss_ref,
    final_ref,
):
    seq, block = pl.program_id(0), pl.program_id(1)
    rows, width = mixed_ref.shape
    alive = length_ref[seq] > block * rows
    final_ref[...] = input_ref[...]

    @pl.when(alive)
    def _():
        vectors = vector_ref[...].astype(jnp.float32).T
        joined = input_ref[...] + (dense(mixed_ref[...], out_ref[...]) + vectors[4:5])
        joined_one_ref[...] = joined
        normed = norm_parts(joined)[0] * vectors[5:6] + vectors[6:7]
        low = normed.astype(jnp.bfloat16)
        normed_ref[...] = low
        fed = None
        for column in range(0, up_ref.shape[1], width):
            columns = slice(column, column + width)
            hidden = dense(low, up_ref[:, columns]) + bias_ref[:, columns]
            share = normal_cdf(hidden)
            density = jnp.exp(-0.5 * hidden * hidden) * (2.0 * jnp.pi) ** -0.5
            slope_ref[:, columns] = (share + hidden * density).astype(jnp.bfloat16)
            active = (hidden * share).astype(jnp.bfloat16)
            active_ref[:, columns] = active
            part = dense(active, down_ref[:, columns])
            fed = part if fed is None else fed + part
        joined = normed + (fed + vectors[7:8])
        joined_two_ref[...] = joined
        final_ref[...] = norm_parts(joined)[0] * vectors[8:9] + vectors[9:10]

    @pl.when(jnp.logical_not(alive))
    def _():
        normed_ref[...] = jnp.zeros_like(normed_ref)
        active_ref[...] = jnp.zeros_like(active_ref)

    final = final_ref[...]
    row = lax.broadcasted_iota(jnp.int32, final.shape, 0) + block * rows
    gap = jnp.where(row < true_ref[seq], final - teacher_ref[...].astype(jnp.float32), 0.0)
    grad_ref[...] = 2.0 * gap
    hot = picks_hot(picked_ref, block * rows, rows)
    chosen = dense(hot, final.astype(jnp.bfloat16)).astype(jnp.bfloat16)

    @pl.when(block == 0)
    def _():
        chosen_ref[...] = chosen

    @pl.when(block > 0)
    def _():
        chosen_ref[...] += chosen

    @pl.when((block == 0) & (seq == 0))
    def _():
        loss_ref[...] = jnp.zeros_like(loss_ref)

    loss_ref[...] += eight_rows(gap * gap)


def unfeed_kernel(
    length_ref,
    grad_ref,
    head_ref,
    picked_ref,
    joined_one_ref,
    slope_ref,
    joined_two_ref,
    vector_ref,
    out_ref,
    up_ref,
    down_ref,
    final_ref,
    joined_out,
    mixed_out,
    attention_out,
    feed_out,
    hidden_out,
    sums_ref,
    hidden_sum_ref,
):
    seq, block = pl.program_id(0), pl.program_id(1)
    rows, width = grad_ref.shape
    alive = length_ref[seq] > block * rows
    head = jnp.sum(head_ref[...].astype(jnp.float32), axis=0)
    high = head.astype(jnp.bfloat16)
    rest = (head - high.astype(jnp.float32)).astype(jnp.bfloat16)
    hot = picks_hot(picked_ref, block * rows, rows)
    grads = grad_ref[...] + dense_tn(hot, high) + dense_tn(hot, rest)
    final_ref[...] = grads

    @pl.when((block == 0) & (seq == 0))
    def _():
        sums_ref[...] = jnp.zeros_like(sums_ref)
        hidden_sum_ref[...] = jnp.zeros_like(hidden_sum_ref)

    @pl.when(alive)
    def _():
        vectors = vector_ref[...].astype(jnp.float32).T
        unit_rows, spread = norm_parts(joined_two_ref[...])
        grad_two, gain_two, shift_two = norm_back(grads, unit_rows, spread, vectors[8:9])
        feed = grad_two.astype(jnp.bfloat16)
        feed_out[...] = feed
        back = grad_two
        for column in range(0, up_ref.shape[1], width):
            columns = slice(column, column + width)
            hidden = dense_nt(feed, down_ref[:, columns])
            hidden = (hidden * slope_ref[:, columns].astype(jnp.float32)).astype(jnp.bfloat16)
            hidden_out[:, columns] = hidden
            hidden_sum_ref[:, columns] += eight_rows(hidden.astype(jnp.float32))
            back = back + dense_nt(hidden, up_ref[:, columns])
        unit_rows, spread = norm_parts(joined_one_ref[...])
        grad_one, gain_one, shift_one = norm_back(back, unit_rows, spread, vectors[5:6])
        joined_out[...] = grad_one
        attention = grad_one.astype(jnp.bfloat16)
        attention_out[...] = attention
        mixed_out[...] = dense_nt(attention, out_ref[...]).astype(jnp.bfloat16)
        sums_ref[0] += eight_rows(attention.astype(jnp.float32))
        sums_ref[1] += gain_one
        sums_ref[2] += shift_one
        sums_ref[3] += eight_rows(feed.astype(jnp.float32))
        sums_ref[4] += gain_two
        sums_ref[5] += shift_two

    @pl.when(jnp.logical_not(alive))
    def _():
        for ref in (joined_out, mixed_out, attention_out, feed_out, hidden_out):
            ref[...] = jnp.zeros_like(ref)


def leave_kernel(
    length_ref,
    keep_ref,
    query_ref,
    key_ref,
    value_ref,
    joined_ref,
    final_ref,
    embedded_ref,
    vector_ref,
    weight_ref,
    rows_ref,
    place_ref,
    sums_ref,
    place_sum,
):
    block, seq = pl.program_id(0), pl.program_id(1)
    rows, width = joined_ref.shape
    alive = length_ref[seq] > block * rows
    vectors = vector_ref[...].astype(jnp.float32).T
    dropped = (keep_ref[seq] == 0).astype(jnp.float32)

    @pl.when((block == 0) & (seq == 0))
    def _():
        sums_ref[...] = jnp.zeros_like(sums_ref)

    @pl.when(seq == 0)
    def _():
        place_sum[...] = jnp.zeros_like(place_sum)

    def finish(grads):
        unit_rows, spread = norm_parts(embedded_ref[...])
        grads, gain, shift = norm_back(grads, unit_rows, spread, vectors[0:1])
        sums_ref[0] += gain
        sums_ref[1] += shift
        rows_ref[...] = grads.astype(jnp.bfloat16)
        place_sum[...] += grads

    @pl.when(alive)
    def _():
        grads = joined_ref[...]
        for part, ref in enumerate((query_ref, key_ref, value_ref)):
            grads = grads + dense_nt(ref[...], weight_ref[:, part * width : (part + 1) * width])
        sums_ref[2] += eight_rows(query_ref[...].astype(jnp.float32))
        sums_ref[3] += eight_rows(value_ref[...].astype(jnp.float32))
        finish(grads)

    @pl.when(jnp.logical_not(alive))
    def _():
        finish(final_ref[...] * dropped)

    @pl.when(seq == pl.num_programs(1) - 1)
    def _():
        place_ref[...] = place_sum[...].T.astype(jnp.bfloat16)


def deal_out(product, member_ref, kept_ref, given_ref, halves):
    halves[...] = product.reshape(halves.shape).astype(halves.dtype)
    member = member_ref[0]
    kept_ref[0] = halves[:, member]
    given_ref[0] = halves[:, 1 - member]


def early_kernel(
    member_ref,
    mixed_ref,
    attention_ref,
    normed_ref,
    hidden_ref,
    active_ref,
    feed_ref,
    kept_ref,
    given_ref,
    halves,
):
    place, blocks = pl.program_id(0), pl.num_programs(0) // 2
    cases = (
        (place == 0, mixed_ref, attention_ref),
        ((place > 0) & (place <= blocks), normed_ref, hidden_ref),
        (place > blocks, active_ref, feed_ref),
    )
    for wanted, left_ref, right_ref in cases:

        @pl.when(wanted)
        def _():
            product = dense_tn(left_ref[...], right_ref[...])
            deal_out(product, member_ref, kept_ref, given_ref, halves)


def late_kernel(
    member_ref,
    low_ref,
    query_ref,
    key_ref,
    value_ref,
    place_ref,
    sums_one_ref,
    sums_two_ref,
    up_ref,
    kept_ref,
    given_ref,
    halves,
    columns,
    vectors,
):
    for part, ref in enumerate((query_ref, key_ref, value_ref)):

        @pl.when(pl.program_id(0) == part)
        def _():
            product = dense_tn(low_ref[...], ref[...])
            deal_out(product, member_ref, kept_ref, given_ref, halves)

    @pl.when(pl.program_id(0) == 3)
    def _():
        vectors[...] = jnp.zeros_like(vectors)
        for row in range(4):
            vectors[row : row + 1, :] = jnp.sum(sums_two_ref[row], axis=0, keepdims=True)
        for row in range(6):
            vectors[4 + row : 5 + row, :] = jnp.sum(sums_one_ref[row], axis=0, keepdims=True)
        vectors[10:14, :] = up_ref[...]
        columns[...] = jnp.zeros_like(columns)
        width = place_ref.shape[1]
        columns[:, :width] = place_ref[...].astype(jnp.float32)
        columns[:, width : width + vectors.shape[0]] = vectors[...].T
        deal_out(columns[...], member_ref, kept_ref, given_ref, halves)


def head_grad_kernel(slope_ref, last_ref, chosen_ref, *grad_refs):
    count = len(grad_refs)
    for place, grad_ref in enumerate(grad_refs):
        source = last_ref if place == count - 2 else slope_ref

        @pl.when(pl.program_id(0) == place)
        def _():
            grad_ref[...] = dense_tn(source[0], chosen_ref[...]).astype(grad_ref.dtype)


def head_first_kernel(slope_ref, chosen_ref, grad_ref):
    grad_ref[...] = dense_tn(slope_ref[0], chosen_ref[...]).astype(grad_ref.dtype)


def row_kernel(kernel, prefetch, operands, outs, grid, scratch=()):
    return pl.pallas_call(
        kernel,
        out_shape=tuple(jax.ShapeDtypeStruct(shape, kind) for shape, kind, _, _ in outs),
        grid_spec=pltpu.PrefetchScalarGridSpec(
            num_scalar_prefetch=len(prefetch),
            grid=grid,
            in_specs=[pl.BlockSpec(block, where) for _, block, where in operands],
            out_specs=tuple(pl.BlockSpec(block, where) for _, _, block, where in outs),
            scratch_shapes=list(scratch),
        ),
        compiler_params=pltpu.CompilerParams(vmem_limit_bytes=VMEM),
        cost_estimate=NO_COST,
    )(*prefetch, *[array for array, _, _ in operands])


def parcel_kernel(own_rows, tiles, wide, source, parcel_ref, slots, sems):
    part, parts = pl.program_id(0), pl.num_programs(0)

    def first_tile(index):
        return jnp.minimum(own_rows * index // 128, tiles - wide)

    def fetch(index):
        lane = pl.multiple_of(first_tile(index) * 128, 128)
        slot = lax.rem(index, 2)
        return pltpu.make_async_copy(
            source.at[:, pl.ds(lane, wide * 128)],
            slots.at[slot, :, pl.ds(0, wide * 128)],
            sems.at[slot],
        )

    @pl.when(part == 0)
    def _():
        fetch(0).start()

    @pl.when(part + 1 < parts)
    def _():
        fetch(part + 1).start()

    fetch(part).wait()
    shift = own_rows * part - 128 * first_tile(part)
    slot, skip, turn = lax.rem(part, 2), shift // 128, lax.rem(128 - lax.rem(shift, 128), 128)
    n_pick, width = parcel_ref.shape[1:]
    lane = lax.broadcasted_iota(jnp.int32, (n_pick, 128), 1)

    def turned(tile):
        start = pl.multiple_of((tile + skip) * 128, 128)
        values = slots[slot, :, pl.ds(start, 128)].astype(jnp.float32)
        return pltpu.roll(values, turn, axis=1)

    low = turned(0)
    for tile in range(width // 128):
        high = turned(tile + 1)
        values = jnp.where(lane < 128 - lax.rem(shift, 128), low, high)
        values = jnp.where(lane + 128 * tile < own_rows, values, 0.0)
        parcel_ref[0, :, 128 * tile : 128 * (tile + 1)] = values.astype(jnp.bfloat16)
        low = high


def parcels_of(flat_teacher, own_rows, lanes, n_dev):
    n_pick, vocab = flat_teacher.shape
    tiles = vocab // 128
    wide = min(tiles, lanes // 128 + 1)
    return pl.pallas_call(
        functools.partial(parcel_kernel, own_rows, tiles, wide),
        out_shape=jax.ShapeDtypeStruct((n_dev, n_pick, lanes), jnp.bfloat16),
        grid=(n_dev,),
        in_specs=[pl.BlockSpec(memory_space=pl.ANY)],
        out_specs=pl.BlockSpec((1, n_pick, lanes), lambda r: (r, 0, 0)),
        scratch_shapes=[
            pltpu.VMEM((2, n_pick, (wide + 2) * 128), jnp.bfloat16),
            pltpu.SemaphoreType.DMA((2,)),
        ],
        compiler_params=pltpu.CompilerParams(vmem_limit_bytes=VMEM),
        cost_estimate=NO_COST,
    )(flat_teacher)


def head_kernel(steps, place_ref, chosen_ref, target_ref, *refs):
    tables = refs[:steps]
    before = refs[steps:-3]
    slope_ref, part_ref, loss_ref = refs[-3:]
    chosen = chosen_ref[...]
    senders, _, n_pick, _ = target_ref.shape
    total, loss = before[0][...] if before else None, None
    for step in range(steps):
        table = tables[step][...]
        width = table.shape[0]
        target = target_ref[:, place_ref[step]].reshape(senders * n_pick, -1)[:, :width]
        gap = dense_nt(chosen, table) - target.astype(jnp.float32)
        square = jnp.sum((gap * gap).reshape(-1, 8, width), axis=0)
        loss = square if loss is None else loss + square
        slope = (2.0 * gap).astype(jnp.bfloat16)
        slope_ref[step] = slope
        part = dense(slope, table)
        total = part if total is None else total + part
    part_ref[...] = total.astype(part_ref.dtype)

    @pl.when(pl.program_id(0) == 0)
    def _():
        loss_ref[...] = jnp.zeros_like(loss_ref)

    loss_ref[...] += loss


def head_products(places, all_chosen, targets, tables, before, part_type):
    n_dp, n_fs, n_pick, lanes = targets.shape
    row_width = all_chosen.shape[1]
    padded = tables[0].shape[0]
    rows, steps = 2 * n_pick, len(tables)
    whole = pl.BlockSpec((padded, row_width), lambda m, _: (0, 0))
    some = pl.BlockSpec((rows, row_width), lambda m, _: (m, 0))
    return pl.pallas_call(
        functools.partial(head_kernel, steps),
        out_shape=(
            jax.ShapeDtypeStruct((steps, n_dp * n_pick, padded), jnp.bfloat16),
            jax.ShapeDtypeStruct((n_dp * n_pick, row_width), part_type),
            jax.ShapeDtypeStruct((8, padded), jnp.float32),
        ),
        grid_spec=pltpu.PrefetchScalarGridSpec(
            num_scalar_prefetch=1,
            grid=(n_dp // 2,),
            in_specs=[
                some,
                pl.BlockSpec((2, n_fs, n_pick, lanes), lambda m, _: (m, 0, 0, 0)),
            ]
            + [whole] * steps
            + [some] * len(before),
            out_specs=(
                pl.BlockSpec((steps, rows, padded), lambda m, _: (0, m, 0)),
                some,
                pl.BlockSpec((8, padded), lambda m, _: (0, 0)),
            ),
        ),
        compiler_params=pltpu.CompilerParams(vmem_limit_bytes=VMEM),
        cost_estimate=NO_COST,
    )(places, all_chosen, targets, *tables, *before)


def sum_over_peers(part, axis):
    size, me = lax.axis_size(axis), lax.axis_index(axis)
    arrived = [lax.dynamic_index_in_dim(part, me, 1, False).astype(jnp.float32)]
    for apart in range(1, size):
        given = lax.dynamic_index_in_dim(part, me ^ apart, 1, False)
        got = lax.ppermute(given, axis, [(peer, peer ^ apart) for peer in range(size)])
        arrived.append(got.astype(jnp.float32))
    return sum(arrived)


def sum_in_pair(kept, given, pieces=1):
    swap = [(0, 1), (1, 0)]
    size = given.shape[0] // pieces
    got = [
        lax.ppermute(given[p * size : (p + 1) * size], "pair", swap) for p in range(pieces)
    ]
    got = got[0] if pieces == 1 else jnp.concatenate(got)
    return (kept.astype(jnp.float32) + got.astype(jnp.float32)).astype(jnp.bfloat16)


def sum_in_plane(part):
    part = sum_over_peers(part, "plane").astype(jnp.bfloat16)
    return part.reshape(part.shape[0], lax.axis_size("fsdp"), -1, part.shape[-1])


def sum_in_line(part):
    return sum_over_peers(part, "fsdp")


def route_plan(ids, live, own_rows, n_dev):
    place = jnp.arange(ids.shape[0])
    owner = ids // own_rows
    same = (ids[:, None] == ids[None, :]) & live[None, :]
    leader = jnp.min(jnp.where(same, place[None, :], ids.shape[0]), axis=1)
    first = live & (leader == place)
    before = (owner[:, None] == owner[None, :]) & (place[None, :] < leader[:, None])
    rank = jnp.sum(before & first[None, :], axis=1, dtype=jnp.int32)
    room = max(16, 1280 // n_dev)
    rounds = jnp.max(jnp.where(first, rank, 0)) // room + 1
    return ids, live, owner, first, rank, room, rounds, own_rows, n_dev


def slots_of(plan, turn):
    ids, live, owner, first, rank, room, rounds, own_rows, n_dev = plan
    here = live & (rank >= turn * room) & (rank < (turn + 1) * room)
    return jnp.where(here, owner * room + rank - turn * room, -1)


def exchange_wanted(plan, turn, axes):
    ids, live, owner, first, rank, room, rounds, own_rows, n_dev = plan
    slots = slots_of(plan, turn)
    local = jnp.where(first, ids - owner * own_rows + 1, 0)
    hit = jnp.arange(n_dev * room)[:, None] == slots[None, :]
    asked = jnp.max(jnp.where(hit, local[None, :], 0), axis=1) - 1
    message = jnp.concatenate(
        [
            asked.reshape(n_dev, room),
            jnp.broadcast_to(rounds, (n_dev, 128 - room)).astype(jnp.int32),
        ],
        axis=1,
    ).reshape(n_dev, 1, 128)
    heard = lax.all_to_all(message, axes, split_axis=0, concat_axis=0).reshape(n_dev, 128)
    return heard[:, :room].reshape(-1), jnp.max(heard[:, room:])


def ask_rows(plan, wanted, table_low, axes):
    room, own_rows, n_dev = plan[5], plan[7], plan[8]
    one_hot = (wanted[:, None] == jnp.arange(own_rows)[None, :]).astype(jnp.bfloat16)
    rows = dense(one_hot, table_low).astype(jnp.bfloat16)
    return lax.all_to_all(rows.reshape(n_dev, room, -1), axes, split_axis=0, concat_axis=0)


def place_rows(plan, turn, rows):
    room, n_dev = plan[5], plan[8]
    back = (slots_of(plan, turn)[:, None] == jnp.arange(n_dev * room)[None, :]).astype(
        jnp.bfloat16
    )
    return dense(back, rows.reshape(n_dev * room, -1))


def more_rows(plan, rounds, token_rows, table_low, axes):
    def body(state):
        turn, total = state
        wanted, _ = exchange_wanted(plan, turn, axes)
        rows = ask_rows(plan, wanted, table_low, axes)
        return turn + 1, total + place_rows(plan, turn, rows)

    return lax.while_loop(lambda state: state[0] < rounds, body, (jnp.int32(1), token_rows))[1]


def rows_to_give(plan, turn, flat_grad):
    room, n_dev = plan[5], plan[8]
    spread = (jnp.arange(n_dev * room)[:, None] == slots_of(plan, turn)[None, :]).astype(
        jnp.bfloat16
    )
    sums = dense(spread, flat_grad).astype(jnp.bfloat16)
    return sums.reshape(n_dev, room, -1)


def give_rows(sums, axes):
    got = lax.all_to_all(sums, axes, split_axis=0, concat_axis=0)
    return got.reshape(-1, sums.shape[-1])


def more_given(plan, rounds, flat_grad, own_rows, own_part, axes):
    def body(state):
        turn, total = state
        wanted, _ = exchange_wanted(plan, turn, axes)
        one_hot = (jnp.arange(own_part.shape[0])[:, None] == wanted[None, :]).astype(jnp.bfloat16)
        got = give_rows(rows_to_give(plan, turn, flat_grad), axes)
        return turn + 1, (total.astype(jnp.float32) + dense(one_hot, got)).astype(total.dtype)

    return lax.while_loop(lambda state: state[0] < rounds, body, (jnp.int32(1), own_part))[1]


def at_lane(tile, lane, value):
    row = lax.broadcasted_iota(jnp.int32, tile.shape, 0)
    column = lax.broadcasted_iota(jnp.int32, tile.shape, 1)
    return tile + jnp.where((row == 0) & (column == lane), value, 0.0)


def total_sum(values):
    return jnp.sum(jnp.sum(values, axis=0, keepdims=True), axis=1, keepdims=True)


def table_kernel(
    own_rows,
    wanted_ref,
    returned_ref,
    moved_ref,
    part_ref,
    tile_ref,
    hidden_loss_ref,
    head_loss_ref,
    last_loss_ref,
    out_ref,
    up_ref,
    down_ref,
    last_ref,
    grad_ref,
    place_ref,
    qkv_ref,
    vector_ref,
    sum_ref,
):
    rows = grad_ref.shape[0]
    first = pl.program_id(0) * rows
    spot = lax.broadcasted_iota(jnp.int32, (rows, wanted_ref.shape[1]), 0) + first
    hot = (spot == wanted_ref[...]).astype(jnp.bfloat16)
    grads = dense(hot, returned_ref[...])
    grads = grads + (moved_ref[...].astype(jnp.float32) + part_ref[...].astype(jnp.float32))
    row = lax.broadcasted_iota(jnp.int32, grads.shape, 0) + first
    grads = jnp.where(row < own_rows, grads, 0.0)
    grad_ref[...] = grads

    @pl.when(pl.program_id(0) == 0)
    def _():
        sum_ref[...] = tile_ref[...]
        for loss_ref in (hidden_loss_ref, head_loss_ref, last_loss_ref):
            sum_ref[...] = at_lane(sum_ref[...], 1, total_sum(loss_ref[...]))
        width, places = last_ref.shape[2], place_ref.shape[1]
        for part in range(3):
            qkv_ref[:, part * width : (part + 1) * width] = last_ref[part]
        place_ref[...] = last_ref[3][:, :places]
        vectors = last_ref[3][:, places : places + 128].T
        vector_ref[...] = vectors[: vector_ref.shape[0], :]
        for other in (out_ref, up_ref, down_ref, place_ref, qkv_ref, vector_ref):
            sum_ref[...] = at_lane(sum_ref[...], 0, total_sum(other[...] * other[...]))

    sum_ref[...] = at_lane(sum_ref[...], 0, total_sum(grads * grads))


def update_kernel(own_rows, steps, every_ref, *refs):
    weights, grads, firsts, seconds = [refs[7 * k : 7 * k + 7] for k in range(4)]
    moments, squares, updates = [refs[7 * k : 7 * k + 7] for k in range(4, 7)]
    total_ref, sum_ref = refs[49:]
    totals = jnp.sum(every_ref[...], axis=0)
    count = totals[0:1, 2:3]
    norm = jnp.sqrt(totals[0:1, 0:1]) / count
    factor = jnp.minimum(1.0, CLIP_NORM / norm) / count

    def step(place, live=None):
        weight = weights[place][...]
        clipped = grads[place][...] * factor
        moment = BETA_ONE * firsts[place][...] + (1.0 - BETA_ONE) * clipped
        square = BETA_TWO * seconds[place][...] + (1.0 - BETA_TWO) * clipped * clipped
        update = (
            moment
            * (1.0 / (1.0 - BETA_ONE**STEP))
            / (jnp.sqrt(square * (1.0 / (1.0 - BETA_TWO**STEP))) + ADAM_EPS)
            + DECAY_RATE * weight
        )
        moments[place][...] = moment
        squares[place][...] = square
        updates[place][...] = update
        if live is not None:
            update = jnp.where(live, update, 0.0)
        sum_ref[...] = at_lane(sum_ref[...], place, total_sum(update * update))

    @pl.when(pl.program_id(0) == 0)
    def _():
        total_ref[...] = at_lane(totals, 127, norm)
        sum_ref[...] = jnp.zeros_like(sum_ref)

    for place in range(1, 7):

        @pl.when(pl.program_id(0) == place % steps)
        def _():
            step(place)

    row = lax.broadcasted_iota(jnp.int32, weights[0].shape, 0)
    step(0, row + pl.program_id(0) * weights[0].shape[0] < own_rows)


def weight_kernel(steps, every_ref, total_ref, *refs):
    weights, updates, outs = refs[:7], refs[7:14], refs[14:21]
    sum_ref = refs[21]
    update_norms = jnp.sqrt(jnp.sum(every_ref[...], axis=0))

    def step(place):
        norm = jnp.sqrt(total_ref[0:1, 3 + place : 4 + place])
        ratio = LEARN_RATE * (norm / update_norms[0:1, place : place + 1])
        outs[place][...] = weights[place][...] - ratio * updates[place][...]

    @pl.when(pl.program_id(0) == 0)
    def _():
        sum_ref[...] = update_norms

    for place in range(1, 7):

        @pl.when(pl.program_id(0) == place % steps)
        def _():
            step(place)

    step(0)


def hidden_order(values, row_width):
    lead = values.shape[:-1]
    return jnp.swapaxes(values.reshape(lead + (row_width, -1)), -1, -2).reshape(lead + (-1,))


def hidden_back(values, row_width):
    lead = values.shape[:-1]
    return jnp.swapaxes(values.reshape(lead + (-1, row_width)), -1, -2).reshape(lead + (-1,))


def column_blocks(values, row_width):
    return [values[:, c : c + row_width] for c in range(0, values.shape[1], row_width)]


def on_device(
    token_ids,
    true_mask,
    keep_layer,
    picked,
    teacher_hidden,
    teacher_logits,
    embed_table,
    pos_table,
    query_key_value_weight,
    output_weight,
    up_weight,
    down_weight,
    gains_biases,
    first_embed,
    first_pos,
    first_qkv,
    first_out,
    first_up,
    first_down,
    first_gains,
    second_embed,
    second_pos,
    second_qkv,
    second_out,
    second_up,
    second_down,
    second_gains,
):
    axes = AXES
    n_dp, n_fs = lax.axis_size(SPLIT), lax.axis_size("fsdp")
    n_dev = n_dp * n_fs
    i_fs = lax.axis_index("fsdp")
    masters = (
        embed_table,
        pos_table,
        query_key_value_weight,
        output_weight,
        up_weight,
        down_weight,
        gains_biases,
    )
    firsts = (first_embed, first_pos, first_qkv, first_out, first_up, first_down, first_gains)
    seconds = (
        second_embed,
        second_pos,
        second_qkv,
        second_out,
        second_up,
        second_down,
        second_gains,
    )
    seq_count, seq_len = token_ids.shape
    own_rows, row_width = embed_table.shape
    ff = up_weight.shape[1]
    in_rows = query_key_value_weight.shape[0]
    n_tok = seq_count * seq_len
    n_pick = picked.shape[0] * picked.shape[1]
    vocab = own_rows * n_dev
    block_rows = own_rows * n_fs

    table_low = embed_table.astype(jnp.bfloat16)
    pack_width = 3 * row_width + row_width + ff + ff + seq_len
    gain_width = -(-14 // 128) * 128
    packed_low = jnp.concatenate(
        [
            query_key_value_weight,
            output_weight,
            hidden_order(up_weight, row_width),
            down_weight.reshape(in_rows, ff),
            pos_table.T,
            jnp.pad(gains_biases.T, ((0, 0), (0, gain_width - 14))),
        ],
        axis=1,
    ).astype(jnp.bfloat16)
    gathered = lax.all_gather(packed_low, axes, axis=0, tiled=True)
    plan = route_plan(token_ids.reshape(-1), true_mask.reshape(-1) > 0, own_rows, n_dev)
    wanted, rounds = exchange_wanted(plan, 0, axes)
    ring = [(z, (z + 1) % n_fs) for z in range(n_fs)]
    padded = -(-own_rows // 16) * 16
    lanes = -(-own_rows // 128) * 128
    first_table = jnp.pad(table_low, ((0, padded - own_rows), (0, 0)))
    arrived = ask_rows(plan, wanted, table_low, axes)

    targets = parcels_of(teacher_logits.reshape(n_pick, vocab), own_rows, lanes, n_dev)
    arrived, targets = lax.optimization_barrier((arrived, targets))
    targets = lax.all_to_all(
        targets.reshape(n_dp, n_fs, n_pick, lanes), SPLIT, split_axis=0, concat_axis=0
    )
    tile = jnp.zeros((8, 128), jnp.float32)
    scalars = [jnp.sum(true_mask.astype(jnp.float32))]
    scalars += [jnp.sum(member * member) for member in masters]
    for place, value in enumerate(scalars):
        tile = at_lane(tile, place + 2, value)
    arrived, first_table, tile = lax.optimization_barrier((arrived, first_table, tile))
    tables = [first_table, lax.ppermute(first_table, "fsdp", ring)]

    i_dp = lax.axis_index(SPLIT)
    token_rows = place_rows(plan, 0, arrived)
    token_rows = more_rows(plan, rounds, token_rows, table_low, axes)

    def pass_table(*later):
        newest, *later = lax.optimization_barrier((tables[-1], *later))
        if len(tables) < n_fs:
            tables.append(lax.ppermute(newest, "fsdp", ring))
        return later

    places = lax.rem(i_fs - jnp.arange(n_fs, dtype=jnp.int32) + n_fs, n_fs)

    rows = seq_len // 2
    n_block = seq_len // rows
    keeps = (keep_layer > 0).astype(jnp.int32)
    trues = jnp.sum(true_mask, axis=1)
    lengths = trues * keeps
    pick_column = picked.reshape(-1, 1)
    bf16, f32 = jnp.bfloat16, jnp.float32

    def by_seq(width, array=None):
        spec = ((rows, width), lambda s, b, *_: (s * n_block + b, 0))
        return spec if array is None else (array, *spec)

    def by_block(width, array=None):
        spec = ((rows, width), lambda b, s, *_: (s * n_block + b, 0))
        return spec if array is None else (array, *spec)

    def whole(shape):
        return (shape, lambda *_: (0,) * len(shape))

    def weight(width, place):
        return (gathered, (row_width, width), lambda *_: (0, place))

    (gathered,) = pass_table(gathered)
    vectors = weight(gain_width, pack_width // gain_width)
    qkv_weight = weight(3 * row_width, 0)
    out_weight = weight(row_width, 3)
    up_weight_low, down_weight_low = weight(ff, 1), weight(ff, 2)
    first_place = (4 * row_width + 2 * ff) // rows
    embedded, flat_in, flat_low, packed = row_kernel(
        enter_kernel,
        (lengths,),
        [
            by_block(row_width, token_rows),
            (gathered, (row_width, rows), lambda b, s, *_: (0, first_place + b)),
            vectors,
            qkv_weight,
        ],
        [
            ((n_tok, row_width), f32, *by_block(row_width)),
            ((n_tok, row_width), f32, *by_block(row_width)),
            ((n_tok, row_width), bf16, *by_block(row_width)),
            ((n_tok, 3 * row_width), bf16, *by_block(3 * row_width)),
        ],
        (n_block, seq_count),
    )
    mixed_output = attend(lengths, packed)
    up_bias = hidden_order(
        gathered[:, pack_width + 10 : pack_width + 14].astype(f32).T.reshape(1, -1), row_width
    )
    pick_count = picked.shape[1]
    picks = (pick_column, (pick_count, 1), lambda s, b, *_: (s, 0))
    (
        joined_one,
        normed_low,
        gelu_slopes,
        gelu_activated,
        joined_two,
        grad_start,
        chosen,
        hidden_loss,
    ) = row_kernel(
        feed_kernel,
        (lengths, trues),
        [
            by_seq(row_width, mixed_output),
            by_seq(row_width, flat_in),
            by_seq(row_width, teacher_hidden.reshape(n_tok, row_width)),
            picks,
            vectors,
            (up_bias, *whole((1, ff))),
            out_weight,
            up_weight_low,
            down_weight_low,
        ],
        [
            ((n_tok, row_width), f32, *by_seq(row_width)),
            ((n_tok, row_width), bf16, *by_seq(row_width)),
            ((n_tok, ff), bf16, *by_seq(ff)),
            ((n_tok, ff), bf16, *by_seq(ff)),
            ((n_tok, row_width), f32, *by_seq(row_width)),
            ((n_tok, row_width), f32, *by_seq(row_width)),
            ((n_pick, row_width), bf16, (pick_count, row_width), lambda s, b, *_: (s, 0)),
            ((8, row_width), f32, *whole((8, row_width))),
        ],
        (seq_count, n_block),
        [pltpu.VMEM((rows, row_width), f32)],
    )

    if n_fs > 2:
        (chosen,) = pass_table(chosen)
    all_chosen = lax.all_gather(chosen, SPLIT, axis=0, tiled=True)
    while len(tables) < n_fs:
        (all_chosen,) = pass_table(all_chosen)
    slopes, chosen_part, head_loss = head_products(
        places[:-1], all_chosen, targets, tables[:-1], [], jnp.float32
    )
    last_slopes, chosen_part, last_loss = head_products(
        places[-1:], all_chosen, targets, tables[-1:], [chosen_part], jnp.bfloat16
    )
    many = n_dp * n_pick
    all_picked = (all_chosen, (many, row_width), lambda d: (0, 0))
    (head_part,) = row_kernel(
        head_first_kernel,
        (),
        [(slopes, (1, many, padded), lambda d: (1, 0, 0)), all_picked],
        [((padded, row_width), bf16, (padded, row_width), lambda d: (0, 0))],
        (1,),
    )
    head_sums = [lax.ppermute(head_part, "fsdp", ring)]
    last_slopes, grad_chosen = lax.optimization_barrier((last_slopes, chosen_part))
    grad_chosen = lax.all_to_all(
        grad_chosen.reshape(n_dp, n_pick, row_width), SPLIT, split_axis=0, concat_axis=0
    )
    head_parts = row_kernel(
        head_grad_kernel,
        (),
        [
            (
                slopes,
                (1, many, padded),
                lambda d: (jnp.where(d < n_fs - 3, d + 2, 0), 0, 0),
            ),
            (last_slopes, (1, many, padded), lambda d: (0, 0, 0)),
            all_picked,
        ],
        [((padded, row_width), bf16, (padded, row_width), lambda d: (0, 0))] * (n_fs - 1),
        (n_fs - 1,),
    )

    def pass_sum(*later):
        newest, *later = lax.optimization_barrier((head_sums[-1], *later))
        step = len(head_sums)
        if step + 1 < n_fs:
            total = newest.astype(f32) + head_parts[step - 1].astype(f32)
            head_sums.append(lax.ppermute(total.astype(bf16), "fsdp", ring))
        return later

    grad_chosen, *head_parts = pass_sum(grad_chosen, *head_parts)
    for _ in range(n_fs - 4):
        (grad_chosen,) = pass_sum(grad_chosen)

    (
        grad_final,
        grad_joined_one,
        grad_mixed,
        grad_attention,
        grad_feed,
        grad_hidden,
        sums_one,
        hidden_sums,
    ) = row_kernel(
        unfeed_kernel,
        (lengths,),
        [
            by_seq(row_width, grad_start),
            (grad_chosen, (n_dp, pick_count, row_width), lambda s, b, *_: (0, s, 0)),
            picks,
            by_seq(row_width, joined_one),
            by_seq(ff, gelu_slopes),
            by_seq(row_width, joined_two),
            vectors,
            out_weight,
            up_weight_low,
            down_weight_low,
        ],
        [
            ((n_tok, row_width), f32, *by_seq(row_width)),
            ((n_tok, row_width), f32, *by_seq(row_width)),
            ((n_tok, row_width), bf16, *by_seq(row_width)),
            ((n_tok, row_width), bf16, *by_seq(row_width)),
            ((n_tok, row_width), bf16, *by_seq(row_width)),
            ((n_tok, ff), bf16, *by_seq(ff)),
            ((6, 8, row_width), f32, *whole((6, 8, row_width))),
            ((8, ff), f32, *whole((8, ff))),
        ],
        (seq_count, n_block),
    )
    member = lax.axis_index("pair").reshape(1).astype(jnp.int32)
    n_plane = lax.axis_size("plane")
    share = row_width // (2 * n_plane)
    halves = pltpu.VMEM((n_plane, 2, share, row_width), bf16)

    def dealt(columns):
        out = (
            (columns, n_plane, share, row_width),
            bf16,
            (1, n_plane, share, row_width),
            lambda j, *_: (j, 0, 0, 0),
        )
        return [out, out]

    def full(array):
        return (array, *whole(array.shape))

    blocks = ff // row_width
    early_kept, early_given = row_kernel(
        early_kernel,
        (member,),
        [
            full(mixed_output),
            full(grad_attention),
            full(normed_low),
            (
                grad_hidden,
                (n_tok, row_width),
                lambda j, *_: (0, jnp.clip(j - 1, 0, blocks - 1)),
            ),
            (
                gelu_activated,
                (n_tok, row_width),
                lambda j, *_: (0, jnp.clip(j - 1 - blocks, 0, blocks - 1)),
            ),
            full(grad_feed),
        ],
        dealt(1 + 2 * blocks),
        (1 + 2 * blocks,),
        [halves],
    )
    up_rows = hidden_back(jnp.sum(hidden_sums, axis=0, keepdims=True), row_width)
    early_kept, early_given = pass_sum(early_kept, early_given)
    early = sum_in_pair(early_kept, early_given)
    grad_mixed, early, up_rows = lax.optimization_barrier((grad_mixed, early, up_rows))
    early = sum_in_plane(early)
    *grad_parts, head_sums[-1] = lax.optimization_barrier(
        (*attend(lengths, packed, grad_mixed), head_sums[-1])
    )
    flat_grad, place_grad, sums_two = row_kernel(
        leave_kernel,
        (lengths, keeps),
        [by_block(row_width, part) for part in grad_parts]
        + [
            by_block(row_width, grad_joined_one),
            by_block(row_width, grad_final),
            by_block(row_width, embedded),
            vectors,
            qkv_weight,
        ],
        [
            ((n_tok, row_width), bf16, *by_block(row_width)),
            ((row_width, seq_len), bf16, (row_width, rows), lambda b, s, *_: (0, b)),
            ((4, 8, row_width), f32, *whole((4, 8, row_width))),
        ],
        (n_block, seq_count),
        [pltpu.VMEM((rows, row_width), f32)],
    )
    flat_grad, early = lax.optimization_barrier((flat_grad, early))
    early = lax.psum_scatter(
        early.reshape(early.shape[0], -1, row_width), "fsdp", scatter_dimension=1, tiled=True
    ).astype(f32)
    given_rows = rows_to_give(plan, 0, flat_grad)
    given_rows, *grad_parts = lax.optimization_barrier((given_rows, *grad_parts))
    returned = give_rows(given_rows, axes)
    own_part = more_given(plan, rounds, flat_grad, own_rows, head_parts[n_fs - 2], axes)
    late_kept, late_given = row_kernel(
        late_kernel,
        (member,),
        [full(flat_low)]
        + [full(part) for part in grad_parts]
        + [
            full(place_grad),
            full(sums_one),
            full(sums_two),
            full(up_rows.reshape(4, row_width)),
        ],
        dealt(4),
        (4,),
        [
            halves,
            pltpu.VMEM((row_width, row_width), f32),
            pltpu.VMEM((gain_width, row_width), f32),
        ],
    )
    late_kept, late_given, own_part = lax.optimization_barrier(
        (late_kept, late_given, own_part)
    )
    last = sum_in_plane(sum_in_pair(late_kept, late_given, 4))
    early, last = lax.optimization_barrier((early, last))
    last = sum_in_line(last)
    early_grads = (
        early[0],
        jnp.transpose(early[1 : 1 + blocks], (1, 2, 0)).reshape(in_rows, ff),
        jnp.swapaxes(early[1 + blocks :], 0, 1).reshape(-1, row_width),
    )
    rows = 400 if own_rows > 400 else 208
    steps = -(-own_rows // rows)

    def by_row(array=None, width=row_width):
        spec = ((rows, width), lambda r, *_: (r, 0))
        return spec if array is None else (array, *spec)

    table_grad, place_sums, qkv_sums, vector_sums, tile = row_kernel(
        functools.partial(table_kernel, own_rows),
        (),
        [
            full(wanted.reshape(1, -1)),
            full(returned),
            by_row(head_sums[-1]),
            by_row(own_part),
            full(tile),
            full(hidden_loss),
            full(head_loss),
            full(last_loss),
        ]
        + [full(grad) for grad in early_grads]
        + [full(last)],
        [
            ((own_rows, row_width), f32, *by_row()),
            ((in_rows, seq_len), f32, *whole((in_rows, seq_len))),
            ((in_rows, 3 * row_width), f32, *whole((in_rows, 3 * row_width))),
            (gains_biases.shape, f32, *whole(gains_biases.shape)),
            ((8, 128), f32, *whole((8, 128))),
        ],
        (steps,),
    )

    def exchange(tile):
        return lax.all_to_all(
            jnp.broadcast_to(tile[None], (n_dev, 8, 128)), axes, split_axis=0, concat_axis=0
        )

    def turned(arrays):
        return [array.T if place == 1 else array for place, array in enumerate(arrays)]

    def specs(arrays):
        return [by_row(arrays[0])] + [full(array) for array in arrays[1:]]

    weights = turned(masters)
    like = [
        (array.shape, f32, *(whole(array.shape) if place else by_row()))
        for place, array in enumerate(weights)
    ]
    tile_out = ((8, 128), f32, *whole((8, 128)))
    *results, totals, tile = row_kernel(
        functools.partial(update_kernel, own_rows, steps),
        (),
        [full(exchange(tile))]
        + specs(weights)
        + specs([table_grad, place_sums, qkv_sums, *early_grads, vector_sums])
        + specs(turned(firsts))
        + specs(turned(seconds)),
        like * 3 + [tile_out, tile_out],
        (steps,),
    )
    new_moments, new_squares = turned(results[:7]), turned(results[7:14])
    *new_weights, update_norms = row_kernel(
        functools.partial(weight_kernel, steps),
        (),
        [full(exchange(tile)), full(totals)] + specs(weights) + specs(results[14:]),
        like + [tile_out],
        (steps,),
    )
    new_weights = turned(new_weights)
    loss_sum, token_count, grad_norm = totals[0, 1], totals[0, 2], totals[0, 127]
    matrix_norms = jnp.stack([jnp.sqrt(totals[0, 3:10]), update_norms[0, :7]])
    return (
        loss_sum,
        token_count,
        grad_norm,
        new_weights[0],
        new_weights[1],
        new_weights[2],
        new_weights[3],
        new_weights[4],
        new_weights[5],
        new_weights[6],
        new_moments[0],
        new_moments[1],
        new_moments[2],
        new_moments[3],
        new_moments[4],
        new_moments[5],
        new_moments[6],
        new_squares[0],
        new_squares[1],
        new_squares[2],
        new_squares[3],
        new_squares[4],
        new_squares[5],
        new_squares[6],
        matrix_norms,
    )


def solution(mesh):
    split = Mesh(
        mesh.devices.reshape(mesh.shape["dp"] // 2, 2, mesh.shape["fsdp"]), AXES
    )
    placed = (
        P(AXES, None),
        P(AXES, None),
        P(AXES),
        P(AXES, None),
        P(AXES, None, None),
        P(AXES, None, None),
        P(AXES, None),
        P(None, AXES),
        P(AXES, None),
        P(AXES, None),
        P(AXES, None),
        P(AXES, None),
        P(None, AXES),
        P(AXES, None),
        P(None, AXES),
        P(AXES, None),
        P(AXES, None),
        P(AXES, None),
        P(AXES, None),
        P(None, AXES),
        P(AXES, None),
        P(None, AXES),
        P(AXES, None),
        P(AXES, None),
        P(AXES, None),
        P(AXES, None),
        P(None, AXES),
    )
    return jax.shard_map(
        on_device,
        mesh=split,
        in_specs=placed,
        out_specs=(
            P(),
            P(),
            P(),
            P(AXES, None),
            P(None, AXES),
            P(AXES, None),
            P(AXES, None),
            P(AXES, None),
            P(AXES, None),
            P(None, AXES),
            P(AXES, None),
            P(None, AXES),
            P(AXES, None),
            P(AXES, None),
            P(AXES, None),
            P(AXES, None),
            P(None, AXES),
            P(AXES, None),
            P(None, AXES),
            P(AXES, None),
            P(AXES, None),
            P(AXES, None),
            P(AXES, None),
            P(None, AXES),
            P(),
        ),
        check_vma=False,
    )
```

```python
import functools

import jax
import jax.numpy as jnp
from jax import lax
from jax.experimental import pallas as pl
from jax.experimental.pallas import tpu as pltpu
from jax.sharding import Mesh
from jax.sharding import PartitionSpec as P

H = 12
HD = 64
STEP = 10


NORM_EPS = 1e-05
CLIP_NORM = 0.5
BETA_ONE = 0.9
BETA_TWO = 0.999
ADAM_EPS = 1e-06
DECAY_RATE = 0.01
LEARN_RATE = 0.3
MASKED_SCORE = -1e30

SPLIT = ("plane", "pair")
AXES = ("plane", "pair", "fsdp")
VMEM = 60 * 2**20
NO_COST = pl.CostEstimate(flops=0, bytes_accessed=0, transcendentals=0)


def normal_cdf(values):
    return 0.5 + 0.5 * lax.erf(values * 0.5**0.5)


def dense(left_op, right_op):
    return jnp.dot(left_op, right_op, preferred_element_type=jnp.float32)


def dense_tn(left_op, right_op):
    return lax.dot_general(
        left_op, right_op, (((0,), (0,)), ((), ())), preferred_element_type=jnp.float32
    )


def dense_nt(left_op, right_op):
    return lax.dot_general(
        left_op, right_op, (((1,), (1,)), ((), ())), preferred_element_type=jnp.float32
    )


def pair_lanes(shape, member):
    lane = lax.broadcasted_iota(jnp.int32, shape, 1)
    return (lane >= HD) if member else (lane < HD)


def softmax_rows(query_rows, key_rows, length):
    scores = dense_nt(query_rows, key_rows)
    spot = lax.broadcasted_iota(jnp.int32, (1, scores.shape[1]), 1)
    scores = scores + jnp.where(spot < length, 0.0, MASKED_SCORE)
    exponent = jnp.exp(scores - jnp.max(scores, axis=1, keepdims=True))
    return exponent * (1.0 / jnp.sum(exponent, axis=1, keepdims=True))


def softmax_columns(key_rows, query_rows, length):
    scores = dense_nt(key_rows, query_rows)
    spot = lax.broadcasted_iota(jnp.int32, (scores.shape[0], 1), 0)
    scores = scores + jnp.where(spot < length, 0.0, MASKED_SCORE)
    exponent = jnp.exp(scores - jnp.max(scores, axis=0, keepdims=True))
    return exponent * (1.0 / jnp.sum(exponent, axis=0, keepdims=True))


def row_spans(seq_len):
    half = seq_len // 2
    return ((0, half), (half, seq_len))


def mix_kernel(length_ref, query_ref, key_ref, value_ref, mixed_ref):
    seq_len = query_ref.shape[0]
    length = length_ref[pl.program_id(0)]

    for low, high in row_spans(seq_len):

        @pl.when((length > low) & (length <= high))
        def _():
            step = high
            keys, values = key_ref[0:high, :], value_ref[0:high, :]
            for row in range(0, high, step):
                queries = query_ref[row : row + step, :] * 0.125
                parts = []
                for member in (0, 1):
                    lanes = pair_lanes(queries.shape, member)
                    chance = softmax_rows(
                        jnp.where(lanes, queries, jnp.zeros_like(queries)), keys, length
                    )
                    parts.append(dense(chance.astype(jnp.bfloat16), values))
                mixed_ref[row : row + step, :] = jnp.where(
                    pair_lanes(parts[0].shape, 1), parts[1], parts[0]
                ).astype(jnp.bfloat16)
            if high < seq_len:
                mixed_ref[high:, :] = jnp.zeros((seq_len - high, 2 * HD), jnp.bfloat16)

    @pl.when(length == 0)
    def _():
        mixed_ref[...] = jnp.zeros_like(mixed_ref)


def unmix_kernel(
    length_ref, query_ref, key_ref, value_ref, grad_ref, query_out, key_out, value_out
):
    seq_len = query_ref.shape[0]
    length = length_ref[pl.program_id(0)]
    outs = (query_out, key_out, value_out)

    for low, high in row_spans(seq_len):

        @pl.when((length > low) & (length <= high))
        def _():
            step = high
            keys, values = key_ref[0:high, :], value_ref[0:high, :]
            key_total, value_total = None, None
            for row in range(0, high, step):
                plain = query_ref[row : row + step, :]
                queries = plain * 0.125
                grads = grad_ref[row : row + step, :]
                parts = []
                for member in (0, 1):
                    lanes = pair_lanes(queries.shape, member)
                    zero = jnp.zeros_like(queries)
                    chance = softmax_columns(keys, jnp.where(lanes, queries, zero), length)
                    slope = dense_nt(values, jnp.where(lanes, grads, zero))
                    slope = chance * (slope - jnp.sum(slope * chance, axis=0, keepdims=True))
                    slope = slope.astype(jnp.bfloat16)
                    parts.append(
                        (
                            dense_tn(slope, keys),
                            dense(slope, plain),
                            dense(chance.astype(jnp.bfloat16), grads),
                        )
                    )
                query_part, key_part, value_part = [
                    jnp.where(pair_lanes(first.shape, 1), second, first)
                    for first, second in zip(*parts)
                ]
                query_out[row : row + step, :] = (query_part * 0.125).astype(jnp.bfloat16)
                key_total = key_part if key_total is None else key_total + key_part
                value_total = value_part if value_total is None else value_total + value_part
            key_out[0:high, :] = (key_total * 0.125).astype(jnp.bfloat16)
            value_out[0:high, :] = value_total.astype(jnp.bfloat16)
            if high < seq_len:
                for ref in outs:
                    ref[high:, :] = jnp.zeros((seq_len - high, 2 * HD), jnp.bfloat16)

    @pl.when(length == 0)
    def _():
        for ref in outs:
            ref[...] = jnp.zeros_like(ref)


def attend(lengths, packed, grad_mixed=None):
    seq_count = lengths.shape[0]
    seq_len = packed.shape[0] // seq_count
    pairs = H // 2

    def block(first):
        return pl.BlockSpec((seq_len, 2 * HD), lambda s, h, _: (s, first + h))

    out = jax.ShapeDtypeStruct((packed.shape[0], H * HD), jnp.bfloat16)
    forward = grad_mixed is None
    operands = (packed, packed, packed) + (() if forward else (grad_mixed,))
    return pl.pallas_call(
        mix_kernel if forward else unmix_kernel,
        out_shape=out if forward else (out, out, out),
        grid_spec=pltpu.PrefetchScalarGridSpec(
            num_scalar_prefetch=1,
            grid=(seq_count, pairs),
            in_specs=[block(0), block(pairs), block(2 * pairs)] + ([] if forward else [block(0)]),
            out_specs=block(0) if forward else (block(0),) * 3,
        ),
        compiler_params=pltpu.CompilerParams(vmem_limit_bytes=VMEM),
        cost_estimate=NO_COST,
    )(lengths, *operands)


def norm_parts(values):
    centered = values - jnp.mean(values, axis=1, keepdims=True)
    spread = lax.rsqrt(jnp.mean(centered * centered, axis=1, keepdims=True) + NORM_EPS)
    return centered * spread, spread


def norm_back(grads, unit_rows, spread, gain_row):
    scaled = grads * gain_row
    inner = jnp.mean(scaled * unit_rows, axis=1, keepdims=True)
    rows = spread * (scaled - jnp.mean(scaled, axis=1, keepdims=True) - unit_rows * inner)
    return rows, eight_rows(grads * unit_rows), eight_rows(grads)


def eight_rows(values):
    return jnp.sum(values.reshape(-1, 8, values.shape[1]), axis=0)


def picks_hot(picked_ref, first_row, rows):
    spot = lax.broadcasted_iota(jnp.int32, (picked_ref.shape[0], rows), 1) + first_row
    return (picked_ref[...] == spot).astype(jnp.bfloat16)


def enter_kernel(
    length_ref, token_ref, place_ref, vector_ref, weight_ref, embedded_ref, input_ref, low_ref, packed_ref
):
    block, seq = pl.program_id(0), pl.program_id(1)
    rows = token_ref.shape[0]
    vectors = vector_ref[...].astype(jnp.float32).T
    embedded = token_ref[...] + place_ref[...].astype(jnp.float32).T
    embedded_ref[...] = embedded
    inputs = norm_parts(embedded)[0] * vectors[0:1] + vectors[1:2]
    input_ref[...] = inputs
    low = inputs.astype(jnp.bfloat16)
    low_ref[...] = low

    @pl.when(length_ref[seq] > block * rows)
    def _():
        width = low.shape[1]
        for part, bias in enumerate((vectors[2:3], None, vectors[3:4])):
            columns = slice(part * width, (part + 1) * width)
            values = dense(low, weight_ref[:, columns])
            if bias is not None:
                values = values + bias
            packed_ref[:, columns] = values.astype(jnp.bfloat16)


def feed_kernel(
    length_ref,
    true_ref,
    mixed_ref,
    input_ref,
    teacher_ref,
    picked_ref,
    vector_ref,
    bias_ref,
    out_ref,
    up_ref,
    down_ref,
    joined_one_ref,
    normed_ref,
    slope_ref,
    active_ref,
    joined_two_ref,
    grad_ref,
    chosen_ref,
    loss_ref,
    final_ref,
):
    seq, block = pl.program_id(0), pl.program_id(1)
    rows, width = mixed_ref.shape
    alive = length_ref[seq] > block * rows
    final_ref[...] = input_ref[...]

    @pl.when(alive)
    def _():
        vectors = vector_ref[...].astype(jnp.float32).T
        joined = input_ref[...] + (dense(mixed_ref[...], out_ref[...]) + vectors[4:5])
        joined_one_ref[...] = joined
        normed = norm_parts(joined)[0] * vectors[5:6] + vectors[6:7]
        low = normed.astype(jnp.bfloat16)
        normed_ref[...] = low
        fed = None
        for column in range(0, up_ref.shape[1], width):
            columns = slice(column, column + width)
            hidden = dense(low, up_ref[:, columns]) + bias_ref[:, columns]
            share = normal_cdf(hidden)
            density = jnp.exp(-0.5 * hidden * hidden) * (2.0 * jnp.pi) ** -0.5
            slope_ref[:, columns] = (share + hidden * density).astype(jnp.bfloat16)
            active = (hidden * share).astype(jnp.bfloat16)
            active_ref[:, columns] = active
            part = dense(active, down_ref[:, columns])
            fed = part if fed is None else fed + part
        joined = normed + (fed + vectors[7:8])
        joined_two_ref[...] = joined
        final_ref[...] = norm_parts(joined)[0] * vectors[8:9] + vectors[9:10]

    @pl.when(jnp.logical_not(alive))
    def _():
        normed_ref[...] = jnp.zeros_like(normed_ref)
        active_ref[...] = jnp.zeros_like(active_ref)

    final = final_ref[...]
    row = lax.broadcasted_iota(jnp.int32, final.shape, 0) + block * rows
    gap = jnp.where(row < true_ref[seq], final - teacher_ref[...].astype(jnp.float32), 0.0)
    grad_ref[...] = 2.0 * gap
    hot = picks_hot(picked_ref, block * rows, rows)
    chosen = dense(hot, final.astype(jnp.bfloat16)).astype(jnp.bfloat16)

    @pl.when(block == 0)
    def _():
        chosen_ref[...] = chosen

    @pl.when(block > 0)
    def _():
        chosen_ref[...] += chosen

    @pl.when((block == 0) & (seq == 0))
    def _():
        loss_ref[...] = jnp.zeros_like(loss_ref)

    loss_ref[...] += eight_rows(gap * gap)


def unfeed_kernel(
    length_ref,
    grad_ref,
    head_ref,
    picked_ref,
    joined_one_ref,
    slope_ref,
    joined_two_ref,
    vector_ref,
    out_ref,
    up_ref,
    down_ref,
    final_ref,
    joined_out,
    mixed_out,
    attention_out,
    feed_out,
    hidden_out,
    sums_ref,
    hidden_sum_ref,
):
    seq, block = pl.program_id(0), pl.program_id(1)
    rows, width = grad_ref.shape
    alive = length_ref[seq] > block * rows
    head = jnp.sum(head_ref[...].astype(jnp.float32), axis=0)
    high = head.astype(jnp.bfloat16)
    rest = (head - high.astype(jnp.float32)).astype(jnp.bfloat16)
    hot = picks_hot(picked_ref, block * rows, rows)
    grads = grad_ref[...] + dense_tn(hot, high) + dense_tn(hot, rest)
    final_ref[...] = grads

    @pl.when((block == 0) & (seq == 0))
    def _():
        sums_ref[...] = jnp.zeros_like(sums_ref)
        hidden_sum_ref[...] = jnp.zeros_like(hidden_sum_ref)

    @pl.when(alive)
    def _():
        vectors = vector_ref[...].astype(jnp.float32).T
        unit_rows, spread = norm_parts(joined_two_ref[...])
        grad_two, gain_two, shift_two = norm_back(grads, unit_rows, spread, vectors[8:9])
        feed = grad_two.astype(jnp.bfloat16)
        feed_out[...] = feed
        back = grad_two
        for column in range(0, up_ref.shape[1], width):
            columns = slice(column, column + width)
            hidden = dense_nt(feed, down_ref[:, columns])
            hidden = (hidden * slope_ref[:, columns].astype(jnp.float32)).astype(jnp.bfloat16)
            hidden_out[:, columns] = hidden
            hidden_sum_ref[:, columns] += eight_rows(hidden.astype(jnp.float32))
            back = back + dense_nt(hidden, up_ref[:, columns])
        unit_rows, spread = norm_parts(joined_one_ref[...])
        grad_one, gain_one, shift_one = norm_back(back, unit_rows, spread, vectors[5:6])
        joined_out[...] = grad_one
        attention = grad_one.astype(jnp.bfloat16)
        attention_out[...] = attention
        mixed_out[...] = dense_nt(attention, out_ref[...]).astype(jnp.bfloat16)
        sums_ref[0] += eight_rows(attention.astype(jnp.float32))
        sums_ref[1] += gain_one
        sums_ref[2] += shift_one
        sums_ref[3] += eight_rows(feed.astype(jnp.float32))
        sums_ref[4] += gain_two
        sums_ref[5] += shift_two

    @pl.when(jnp.logical_not(alive))
    def _():
        for ref in (joined_out, mixed_out, attention_out, feed_out, hidden_out):
            ref[...] = jnp.zeros_like(ref)


def leave_kernel(
    length_ref,
    keep_ref,
    query_ref,
    key_ref,
    value_ref,
    joined_ref,
    final_ref,
    embedded_ref,
    vector_ref,
    weight_ref,
    rows_ref,
    place_ref,
    sums_ref,
    place_sum,
):
    block, seq = pl.program_id(0), pl.program_id(1)
    rows, width = joined_ref.shape
    alive = length_ref[seq] > block * rows
    vectors = vector_ref[...].astype(jnp.float32).T
    dropped = (keep_ref[seq] == 0).astype(jnp.float32)

    @pl.when((block == 0) & (seq == 0))
    def _():
        sums_ref[...] = jnp.zeros_like(sums_ref)

    @pl.when(seq == 0)
    def _():
        place_sum[...] = jnp.zeros_like(place_sum)

    def finish(grads):
        unit_rows, spread = norm_parts(embedded_ref[...])
        grads, gain, shift = norm_back(grads, unit_rows, spread, vectors[0:1])
        sums_ref[0] += gain
        sums_ref[1] += shift
        rows_ref[...] = grads.astype(jnp.bfloat16)
        place_sum[...] += grads

    @pl.when(alive)
    def _():
        grads = joined_ref[...]
        for part, ref in enumerate((query_ref, key_ref, value_ref)):
            grads = grads + dense_nt(ref[...], weight_ref[:, part * width : (part + 1) * width])
        sums_ref[2] += eight_rows(query_ref[...].astype(jnp.float32))
        sums_ref[3] += eight_rows(value_ref[...].astype(jnp.float32))
        finish(grads)

    @pl.when(jnp.logical_not(alive))
    def _():
        finish(final_ref[...] * dropped)

    @pl.when(seq == pl.num_programs(1) - 1)
    def _():
        place_ref[...] = place_sum[...].T.astype(jnp.bfloat16)


def deal_out(product, member_ref, kept_ref, given_ref, halves):
    halves[...] = product.reshape(halves.shape).astype(halves.dtype)
    member = member_ref[0]
    kept_ref[0] = halves[:, member]
    given_ref[0] = halves[:, 1 - member]


def early_kernel(
    member_ref,
    mixed_ref,
    attention_ref,
    normed_ref,
    hidden_ref,
    active_ref,
    feed_ref,
    kept_ref,
    given_ref,
    halves,
):
    place, blocks = pl.program_id(0), pl.num_programs(0) // 2
    cases = (
        (place == 0, mixed_ref, attention_ref),
        ((place > 0) & (place <= blocks), normed_ref, hidden_ref),
        (place > blocks, active_ref, feed_ref),
    )
    for wanted, left_ref, right_ref in cases:

        @pl.when(wanted)
        def _():
            product = dense_tn(left_ref[...], right_ref[...])
            deal_out(product, member_ref, kept_ref, given_ref, halves)


def late_kernel(
    member_ref,
    low_ref,
    query_ref,
    key_ref,
    value_ref,
    place_ref,
    sums_one_ref,
    sums_two_ref,
    up_ref,
    kept_ref,
    given_ref,
    halves,
    columns,
    vectors,
):
    for part, ref in enumerate((query_ref, key_ref, value_ref)):

        @pl.when(pl.program_id(0) == part)
        def _():
            product = dense_tn(low_ref[...], ref[...])
            deal_out(product, member_ref, kept_ref, given_ref, halves)

    @pl.when(pl.program_id(0) == 3)
    def _():
        vectors[...] = jnp.zeros_like(vectors)
        for row in range(4):
            vectors[row : row + 1, :] = jnp.sum(sums_two_ref[row], axis=0, keepdims=True)
        for row in range(6):
            vectors[4 + row : 5 + row, :] = jnp.sum(sums_one_ref[row], axis=0, keepdims=True)
        vectors[10:14, :] = up_ref[...]
        columns[...] = jnp.zeros_like(columns)
        width = place_ref.shape[1]
        columns[:, :width] = place_ref[...].astype(jnp.float32)
        columns[:, width : width + vectors.shape[0]] = vectors[...].T
        deal_out(columns[...], member_ref, kept_ref, given_ref, halves)


def head_grad_kernel(slope_ref, last_ref, chosen_ref, *grad_refs):
    count = len(grad_refs)
    for place, grad_ref in enumerate(grad_refs):
        source = last_ref if place == count - 2 else slope_ref

        @pl.when(pl.program_id(0) == place)
        def _():
            grad_ref[...] = dense_tn(source[0], chosen_ref[...]).astype(grad_ref.dtype)


def head_first_kernel(slope_ref, chosen_ref, grad_ref):
    grad_ref[...] = dense_tn(slope_ref[0], chosen_ref[...]).astype(grad_ref.dtype)


def row_kernel(kernel, prefetch, operands, outs, grid, scratch=()):
    return pl.pallas_call(
        kernel,
        out_shape=tuple(jax.ShapeDtypeStruct(shape, kind) for shape, kind, _, _ in outs),
        grid_spec=pltpu.PrefetchScalarGridSpec(
            num_scalar_prefetch=len(prefetch),
            grid=grid,
            in_specs=[pl.BlockSpec(block, where) for _, block, where in operands],
            out_specs=tuple(pl.BlockSpec(block, where) for _, _, block, where in outs),
            scratch_shapes=list(scratch),
        ),
        compiler_params=pltpu.CompilerParams(vmem_limit_bytes=VMEM),
        cost_estimate=NO_COST,
    )(*prefetch, *[array for array, _, _ in operands])


def parcel_kernel(own_rows, tiles, wide, source, parcel_ref, slots, sems):
    part, parts = pl.program_id(0), pl.num_programs(0)

    def first_tile(index):
        return jnp.minimum(own_rows * index // 128, tiles - wide)

    def fetch(index):
        lane = pl.multiple_of(first_tile(index) * 128, 128)
        slot = lax.rem(index, 2)
        return pltpu.make_async_copy(
            source.at[:, pl.ds(lane, wide * 128)],
            slots.at[slot, :, pl.ds(0, wide * 128)],
            sems.at[slot],
        )

    @pl.when(part == 0)
    def _():
        fetch(0).start()

    @pl.when(part + 1 < parts)
    def _():
        fetch(part + 1).start()

    fetch(part).wait()
    shift = own_rows * part - 128 * first_tile(part)
    slot, skip, turn = lax.rem(part, 2), shift // 128, lax.rem(128 - lax.rem(shift, 128), 128)
    n_pick, width = parcel_ref.shape[1:]
    lane = lax.broadcasted_iota(jnp.int32, (n_pick, 128), 1)

    def turned(tile):
        start = pl.multiple_of((tile + skip) * 128, 128)
        values = slots[slot, :, pl.ds(start, 128)].astype(jnp.float32)
        return pltpu.roll(values, turn, axis=1)

    low = turned(0)
    for tile in range(width // 128):
        high = turned(tile + 1)
        values = jnp.where(lane < 128 - lax.rem(shift, 128), low, high)
        values = jnp.where(lane + 128 * tile < own_rows, values, 0.0)
        parcel_ref[0, :, 128 * tile : 128 * (tile + 1)] = values.astype(jnp.bfloat16)
        low = high


def parcels_of(flat_teacher, own_rows, lanes, n_dev):
    n_pick, vocab = flat_teacher.shape
    tiles = vocab // 128
    wide = min(tiles, lanes // 128 + 1)
    return pl.pallas_call(
        functools.partial(parcel_kernel, own_rows, tiles, wide),
        out_shape=jax.ShapeDtypeStruct((n_dev, n_pick, lanes), jnp.bfloat16),
        grid=(n_dev,),
        in_specs=[pl.BlockSpec(memory_space=pl.ANY)],
        out_specs=pl.BlockSpec((1, n_pick, lanes), lambda r: (r, 0, 0)),
        scratch_shapes=[
            pltpu.VMEM((2, n_pick, (wide + 2) * 128), jnp.bfloat16),
            pltpu.SemaphoreType.DMA((2,)),
        ],
        compiler_params=pltpu.CompilerParams(vmem_limit_bytes=VMEM),
        cost_estimate=NO_COST,
    )(flat_teacher)


def head_kernel(steps, place_ref, chosen_ref, target_ref, *refs):
    tables = refs[:steps]
    before = refs[steps:-3]
    slope_ref, part_ref, loss_ref = refs[-3:]
    chosen = chosen_ref[...]
    senders, _, n_pick, _ = target_ref.shape
    total, loss = before[0][...] if before else None, None
    for step in range(steps):
        table = tables[step][...]
        width = table.shape[0]
        target = target_ref[:, place_ref[step]].reshape(senders * n_pick, -1)[:, :width]
        gap = dense_nt(chosen, table) - target.astype(jnp.float32)
        square = jnp.sum((gap * gap).reshape(-1, 8, width), axis=0)
        loss = square if loss is None else loss + square
        slope = (2.0 * gap).astype(jnp.bfloat16)
        slope_ref[step] = slope
        part = dense(slope, table)
        total = part if total is None else total + part
    part_ref[...] = total.astype(part_ref.dtype)

    @pl.when(pl.program_id(0) == 0)
    def _():
        loss_ref[...] = jnp.zeros_like(loss_ref)

    loss_ref[...] += loss


def head_products(places, all_chosen, targets, tables, before, part_type):
    n_dp, n_fs, n_pick, lanes = targets.shape
    row_width = all_chosen.shape[1]
    padded = tables[0].shape[0]
    rows, steps = 2 * n_pick, len(tables)
    whole = pl.BlockSpec((padded, row_width), lambda m, _: (0, 0))
    some = pl.BlockSpec((rows, row_width), lambda m, _: (m, 0))
    return pl.pallas_call(
        functools.partial(head_kernel, steps),
        out_shape=(
            jax.ShapeDtypeStruct((steps, n_dp * n_pick, padded), jnp.bfloat16),
            jax.ShapeDtypeStruct((n_dp * n_pick, row_width), part_type),
            jax.ShapeDtypeStruct((8, padded), jnp.float32),
        ),
        grid_spec=pltpu.PrefetchScalarGridSpec(
            num_scalar_prefetch=1,
            grid=(n_dp // 2,),
            in_specs=[
                some,
                pl.BlockSpec((2, n_fs, n_pick, lanes), lambda m, _: (m, 0, 0, 0)),
            ]
            + [whole] * steps
            + [some] * len(before),
            out_specs=(
                pl.BlockSpec((steps, rows, padded), lambda m, _: (0, m, 0)),
                some,
                pl.BlockSpec((8, padded), lambda m, _: (0, 0)),
            ),
        ),
        compiler_params=pltpu.CompilerParams(vmem_limit_bytes=VMEM),
        cost_estimate=NO_COST,
    )(places, all_chosen, targets, *tables, *before)


def sum_over_peers(part, axis):
    size, me = lax.axis_size(axis), lax.axis_index(axis)
    arrived = [lax.dynamic_index_in_dim(part, me, 1, False).astype(jnp.float32)]
    for apart in range(1, size):
        given = lax.dynamic_index_in_dim(part, me ^ apart, 1, False)
        got = lax.ppermute(given, axis, [(peer, peer ^ apart) for peer in range(size)])
        arrived.append(got.astype(jnp.float32))
    return sum(arrived)


def sum_in_pair(kept, given, pieces=1):
    swap = [(0, 1), (1, 0)]
    size = given.shape[0] // pieces
    got = [
        lax.ppermute(given[p * size : (p + 1) * size], "pair", swap) for p in range(pieces)
    ]
    got = got[0] if pieces == 1 else jnp.concatenate(got)
    return (kept.astype(jnp.float32) + got.astype(jnp.float32)).astype(jnp.bfloat16)


def sum_in_plane(part):
    part = sum_over_peers(part, "plane").astype(jnp.bfloat16)
    return part.reshape(part.shape[0], lax.axis_size("fsdp"), -1, part.shape[-1])


def sum_in_line(part):
    return sum_over_peers(part, "fsdp")


def route_plan(ids, live, own_rows, n_dev):
    place = jnp.arange(ids.shape[0])
    owner = ids // own_rows
    same = (ids[:, None] == ids[None, :]) & live[None, :]
    leader = jnp.min(jnp.where(same, place[None, :], ids.shape[0]), axis=1)
    first = live & (leader == place)
    before = (owner[:, None] == owner[None, :]) & (place[None, :] < leader[:, None])
    rank = jnp.sum(before & first[None, :], axis=1, dtype=jnp.int32)
    room = max(16, 1280 // n_dev)
    rounds = jnp.max(jnp.where(first, rank, 0)) // room + 1
    return ids, live, owner, first, rank, room, rounds, own_rows, n_dev


def slots_of(plan, turn):
    ids, live, owner, first, rank, room, rounds, own_rows, n_dev = plan
    here = live & (rank >= turn * room) & (rank < (turn + 1) * room)
    return jnp.where(here, owner * room + rank - turn * room, -1)


def exchange_wanted(plan, turn, axes):
    ids, live, owner, first, rank, room, rounds, own_rows, n_dev = plan
    slots = slots_of(plan, turn)
    local = jnp.where(first, ids - owner * own_rows + 1, 0)
    hit = jnp.arange(n_dev * room)[:, None] == slots[None, :]
    asked = jnp.max(jnp.where(hit, local[None, :], 0), axis=1) - 1
    message = jnp.concatenate(
        [
            asked.reshape(n_dev, room),
            jnp.broadcast_to(rounds, (n_dev, 128 - room)).astype(jnp.int32),
        ],
        axis=1,
    ).reshape(n_dev, 1, 128)
    heard = lax.all_to_all(message, axes, split_axis=0, concat_axis=0).reshape(n_dev, 128)
    return heard[:, :room].reshape(-1), jnp.max(heard[:, room:])


def ask_rows(plan, wanted, table_low, axes):
    room, own_rows, n_dev = plan[5], plan[7], plan[8]
    one_hot = (wanted[:, None] == jnp.arange(own_rows)[None, :]).astype(jnp.bfloat16)
    rows = dense(one_hot, table_low).astype(jnp.bfloat16)
    return lax.all_to_all(rows.reshape(n_dev, room, -1), axes, split_axis=0, concat_axis=0)


def place_rows(plan, turn, rows):
    room, n_dev = plan[5], plan[8]
    back = (slots_of(plan, turn)[:, None] == jnp.arange(n_dev * room)[None, :]).astype(
        jnp.bfloat16
    )
    return dense(back, rows.reshape(n_dev * room, -1))


def more_rows(plan, rounds, token_rows, table_low, axes):
    def body(state):
        turn, total = state
        wanted, _ = exchange_wanted(plan, turn, axes)
        rows = ask_rows(plan, wanted, table_low, axes)
        return turn + 1, total + place_rows(plan, turn, rows)

    return lax.while_loop(lambda state: state[0] < rounds, body, (jnp.int32(1), token_rows))[1]


def rows_to_give(plan, turn, flat_grad):
    room, n_dev = plan[5], plan[8]
    spread = (jnp.arange(n_dev * room)[:, None] == slots_of(plan, turn)[None, :]).astype(
        jnp.bfloat16
    )
    sums = dense(spread, flat_grad).astype(jnp.bfloat16)
    return sums.reshape(n_dev, room, -1)


def give_rows(sums, axes):
    got = lax.all_to_all(sums, axes, split_axis=0, concat_axis=0)
    return got.reshape(-1, sums.shape[-1])


def more_given(plan, rounds, flat_grad, own_rows, own_part, axes):
    def body(state):
        turn, total = state
        wanted, _ = exchange_wanted(plan, turn, axes)
        one_hot = (jnp.arange(own_part.shape[0])[:, None] == wanted[None, :]).astype(jnp.bfloat16)
        got = give_rows(rows_to_give(plan, turn, flat_grad), axes)
        return turn + 1, (total.astype(jnp.float32) + dense(one_hot, got)).astype(total.dtype)

    return lax.while_loop(lambda state: state[0] < rounds, body, (jnp.int32(1), own_part))[1]


def at_lane(tile, lane, value):
    row = lax.broadcasted_iota(jnp.int32, tile.shape, 0)
    column = lax.broadcasted_iota(jnp.int32, tile.shape, 1)
    return tile + jnp.where((row == 0) & (column == lane), value, 0.0)


def total_sum(values):
    return jnp.sum(jnp.sum(values, axis=0, keepdims=True), axis=1, keepdims=True)


def table_kernel(
    own_rows,
    wanted_ref,
    returned_ref,
    moved_ref,
    part_ref,
    tile_ref,
    hidden_loss_ref,
    head_loss_ref,
    last_loss_ref,
    out_ref,
    up_ref,
    down_ref,
    last_ref,
    grad_ref,
    place_ref,
    qkv_ref,
    vector_ref,
    sum_ref,
):
    rows = grad_ref.shape[0]
    first = pl.program_id(0) * rows
    spot = lax.broadcasted_iota(jnp.int32, (rows, wanted_ref.shape[1]), 0) + first
    hot = (spot == wanted_ref[...]).astype(jnp.bfloat16)
    grads = dense(hot, returned_ref[...])
    grads = grads + (moved_ref[...].astype(jnp.float32) + part_ref[...].astype(jnp.float32))
    row = lax.broadcasted_iota(jnp.int32, grads.shape, 0) + first
    grads = jnp.where(row < own_rows, grads, 0.0)
    grad_ref[...] = grads

    @pl.when(pl.program_id(0) == 0)
    def _():
        sum_ref[...] = tile_ref[...]
        for loss_ref in (hidden_loss_ref, head_loss_ref, last_loss_ref):
            sum_ref[...] = at_lane(sum_ref[...], 1, total_sum(loss_ref[...]))
        width, places = last_ref.shape[2], place_ref.shape[1]
        for part in range(3):
            qkv_ref[:, part * width : (part + 1) * width] = last_ref[part]
        place_ref[...] = last_ref[3][:, :places]
        vectors = last_ref[3][:, places : places + 128].T
        vector_ref[...] = vectors[: vector_ref.shape[0], :]
        for other in (out_ref, up_ref, down_ref, place_ref, qkv_ref, vector_ref):
            sum_ref[...] = at_lane(sum_ref[...], 0, total_sum(other[...] * other[...]))

    sum_ref[...] = at_lane(sum_ref[...], 0, total_sum(grads * grads))


def update_kernel(own_rows, steps, every_ref, *refs):
    weights, grads, firsts, seconds = [refs[7 * k : 7 * k + 7] for k in range(4)]
    moments, squares, updates = [refs[7 * k : 7 * k + 7] for k in range(4, 7)]
    total_ref, sum_ref = refs[49:]
    totals = jnp.sum(every_ref[...], axis=0)
    count = totals[0:1, 2:3]
    norm = jnp.sqrt(totals[0:1, 0:1]) / count
    factor = jnp.minimum(1.0, CLIP_NORM / norm) / count

    def step(place, live=None):
        weight = weights[place][...]
        clipped = grads[place][...] * factor
        moment = BETA_ONE * firsts[place][...] + (1.0 - BETA_ONE) * clipped
        square = BETA_TWO * seconds[place][...] + (1.0 - BETA_TWO) * clipped * clipped
        update = (
            moment
            * (1.0 / (1.0 - BETA_ONE**STEP))
            / (jnp.sqrt(square * (1.0 / (1.0 - BETA_TWO**STEP))) + ADAM_EPS)
            + DECAY_RATE * weight
        )
        moments[place][...] = moment
        squares[place][...] = square
        updates[place][...] = update
        if live is not None:
            update = jnp.where(live, update, 0.0)
        sum_ref[...] = at_lane(sum_ref[...], place, total_sum(update * update))

    @pl.when(pl.program_id(0) == 0)
    def _():
        total_ref[...] = at_lane(totals, 127, norm)
        sum_ref[...] = jnp.zeros_like(sum_ref)

    for place in range(1, 7):

        @pl.when(pl.program_id(0) == place % steps)
        def _():
            step(place)

    row = lax.broadcasted_iota(jnp.int32, weights[0].shape, 0)
    step(0, row + pl.program_id(0) * weights[0].shape[0] < own_rows)


def weight_kernel(steps, every_ref, total_ref, *refs):
    weights, updates, outs = refs[:7], refs[7:14], refs[14:21]
    sum_ref = refs[21]
    update_norms = jnp.sqrt(jnp.sum(every_ref[...], axis=0))

    def step(place):
        norm = jnp.sqrt(total_ref[0:1, 3 + place : 4 + place])
        ratio = LEARN_RATE * (norm / update_norms[0:1, place : place + 1])
        outs[place][...] = weights[place][...] - ratio * updates[place][...]

    @pl.when(pl.program_id(0) == 0)
    def _():
        sum_ref[...] = update_norms

    for place in range(1, 7):

        @pl.when(pl.program_id(0) == place % steps)
        def _():
            step(place)

    step(0)


def hidden_order(values, row_width):
    lead = values.shape[:-1]
    return jnp.swapaxes(values.reshape(lead + (row_width, -1)), -1, -2).reshape(lead + (-1,))


def hidden_back(values, row_width):
    lead = values.shape[:-1]
    return jnp.swapaxes(values.reshape(lead + (-1, row_width)), -1, -2).reshape(lead + (-1,))


def column_blocks(values, row_width):
    return [values[:, c : c + row_width] for c in range(0, values.shape[1], row_width)]


def on_device(
    token_ids,
    true_mask,
    keep_layer,
    picked,
    teacher_hidden,
    teacher_logits,
    embed_table,
    pos_table,
    query_key_value_weight,
    output_weight,
    up_weight,
    down_weight,
    gains_biases,
    first_embed,
    first_pos,
    first_qkv,
    first_out,
    first_up,
    first_down,
    first_gains,
    second_embed,
    second_pos,
    second_qkv,
    second_out,
    second_up,
    second_down,
    second_gains,
):
    axes = AXES
    n_dp, n_fs = lax.axis_size(SPLIT), lax.axis_size("fsdp")
    n_dev = n_dp * n_fs
    i_fs = lax.axis_index("fsdp")
    masters = (
        embed_table,
        pos_table,
        query_key_value_weight,
        output_weight,
        up_weight,
        down_weight,
        gains_biases,
    )
    firsts = (first_embed, first_pos, first_qkv, first_out, first_up, first_down, first_gains)
    seconds = (
        second_embed,
        second_pos,
        second_qkv,
        second_out,
        second_up,
        second_down,
        second_gains,
    )
    seq_count, seq_len = token_ids.shape
    own_rows, row_width = embed_table.shape
    ff = up_weight.shape[1]
    in_rows = query_key_value_weight.shape[0]
    n_tok = seq_count * seq_len
    n_pick = picked.shape[0] * picked.shape[1]
    vocab = own_rows * n_dev
    block_rows = own_rows * n_fs

    table_low = embed_table.astype(jnp.bfloat16)
    pack_width = 3 * row_width + row_width + ff + ff + seq_len
    gain_width = -(-14 // 128) * 128
    packed_low = jnp.concatenate(
        [
            query_key_value_weight,
            output_weight,
            hidden_order(up_weight, row_width),
            down_weight.reshape(in_rows, ff),
            pos_table.T,
            jnp.pad(gains_biases.T, ((0, 0), (0, gain_width - 14))),
        ],
        axis=1,
    ).astype(jnp.bfloat16)
    gathered = lax.all_gather(packed_low, axes, axis=0, tiled=True)
    plan = route_plan(token_ids.reshape(-1), true_mask.reshape(-1) > 0, own_rows, n_dev)
    wanted, rounds = exchange_wanted(plan, 0, axes)
    ring = [(z, (z + 1) % n_fs) for z in range(n_fs)]
    padded = -(-own_rows // 16) * 16
    lanes = -(-own_rows // 128) * 128
    first_table = jnp.pad(table_low, ((0, padded - own_rows), (0, 0)))
    arrived = ask_rows(plan, wanted, table_low, axes)

    targets = parcels_of(teacher_logits.reshape(n_pick, vocab), own_rows, lanes, n_dev)
    arrived, targets = lax.optimization_barrier((arrived, targets))
    targets = lax.all_to_all(
        targets.reshape(n_dp, n_fs, n_pick, lanes), SPLIT, split_axis=0, concat_axis=0
    )
    tile = jnp.zeros((8, 128), jnp.float32)
    scalars = [jnp.sum(true_mask.astype(jnp.float32))]
    scalars += [jnp.sum(member * member) for member in masters]
    for place, value in enumerate(scalars):
        tile = at_lane(tile, place + 2, value)
    arrived, first_table, tile = lax.optimization_barrier((arrived, first_table, tile))
    tables = [first_table, lax.ppermute(first_table, "fsdp", ring)]

    i_dp = lax.axis_index(SPLIT)
    token_rows = place_rows(plan, 0, arrived)
    token_rows = more_rows(plan, rounds, token_rows, table_low, axes)

    def pass_table(*later):
        newest, *later = lax.optimization_barrier((tables[-1], *later))
        if len(tables) < n_fs:
            tables.append(lax.ppermute(newest, "fsdp", ring))
        return later

    places = lax.rem(i_fs - jnp.arange(n_fs, dtype=jnp.int32) + n_fs, n_fs)

    rows = seq_len // 2
    n_block = seq_len // rows
    keeps = (keep_layer > 0).astype(jnp.int32)
    trues = jnp.sum(true_mask, axis=1)
    lengths = trues * keeps
    pick_column = picked.reshape(-1, 1)
    bf16, f32 = jnp.bfloat16, jnp.float32

    def by_seq(width, array=None):
        spec = ((rows, width), lambda s, b, *_: (s * n_block + b, 0))
        return spec if array is None else (array, *spec)

    def by_block(width, array=None):
        spec = ((rows, width), lambda b, s, *_: (s * n_block + b, 0))
        return spec if array is None else (array, *spec)

    def whole(shape):
        return (shape, lambda *_: (0,) * len(shape))

    def weight(width, place):
        return (gathered, (row_width, width), lambda *_: (0, place))

    (gathered,) = pass_table(gathered)
    vectors = weight(gain_width, pack_width // gain_width)
    qkv_weight = weight(3 * row_width, 0)
    out_weight = weight(row_width, 3)
    up_weight_low, down_weight_low = weight(ff, 1), weight(ff, 2)
    first_place = (4 * row_width + 2 * ff) // rows
    embedded, flat_in, flat_low, packed = row_kernel(
        enter_kernel,
        (lengths,),
        [
            by_block(row_width, token_rows),
            (gathered, (row_width, rows), lambda b, s, *_: (0, first_place + b)),
            vectors,
            qkv_weight,
        ],
        [
            ((n_tok, row_width), f32, *by_block(row_width)),
            ((n_tok, row_width), f32, *by_block(row_width)),
            ((n_tok, row_width), bf16, *by_block(row_width)),
            ((n_tok, 3 * row_width), bf16, *by_block(3 * row_width)),
        ],
        (n_block, seq_count),
    )
    mixed_output = attend(lengths, packed)
    up_bias = hidden_order(
        gathered[:, pack_width + 10 : pack_width + 14].astype(f32).T.reshape(1, -1), row_width
    )
    pick_count = picked.shape[1]
    picks = (pick_column, (pick_count, 1), lambda s, b, *_: (s, 0))
    (
        joined_one,
        normed_low,
        gelu_slopes,
        gelu_activated,
        joined_two,
        grad_start,
        chosen,
        hidden_loss,
    ) = row_kernel(
        feed_kernel,
        (lengths, trues),
        [
            by_seq(row_width, mixed_output),
            by_seq(row_width, flat_in),
            by_seq(row_width, teacher_hidden.reshape(n_tok, row_width)),
            picks,
            vectors,
            (up_bias, *whole((1, ff))),
            out_weight,
            up_weight_low,
            down_weight_low,
        ],
        [
            ((n_tok, row_width), f32, *by_seq(row_width)),
            ((n_tok, row_width), bf16, *by_seq(row_width)),
            ((n_tok, ff), bf16, *by_seq(ff)),
            ((n_tok, ff), bf16, *by_seq(ff)),
            ((n_tok, row_width), f32, *by_seq(row_width)),
            ((n_tok, row_width), f32, *by_seq(row_width)),
            ((n_pick, row_width), bf16, (pick_count, row_width), lambda s, b, *_: (s, 0)),
            ((8, row_width), f32, *whole((8, row_width))),
        ],
        (seq_count, n_block),
        [pltpu.VMEM((rows, row_width), f32)],
    )

    if n_fs > 2:
        (chosen,) = pass_table(chosen)
    all_chosen = lax.all_gather(chosen, SPLIT, axis=0, tiled=True)
    while len(tables) < n_fs:
        (all_chosen,) = pass_table(all_chosen)
    slopes, chosen_part, head_loss = head_products(
        places[:-1], all_chosen, targets, tables[:-1], [], jnp.float32
    )
    last_slopes, chosen_part, last_loss = head_products(
        places[-1:], all_chosen, targets, tables[-1:], [chosen_part], jnp.bfloat16
    )
    many = n_dp * n_pick
    all_picked = (all_chosen, (many, row_width), lambda d: (0, 0))
    (head_part,) = row_kernel(
        head_first_kernel,
        (),
        [(slopes, (1, many, padded), lambda d: (1, 0, 0)), all_picked],
        [((padded, row_width), bf16, (padded, row_width), lambda d: (0, 0))],
        (1,),
    )
    head_sums = [lax.ppermute(head_part, "fsdp", ring)]
    last_slopes, grad_chosen = lax.optimization_barrier((last_slopes, chosen_part))
    grad_chosen = lax.all_to_all(
        grad_chosen.reshape(n_dp, n_pick, row_width), SPLIT, split_axis=0, concat_axis=0
    )
    head_parts = row_kernel(
        head_grad_kernel,
        (),
        [
            (
                slopes,
                (1, many, padded),
                lambda d: (jnp.where(d < n_fs - 3, d + 2, 0), 0, 0),
            ),
            (last_slopes, (1, many, padded), lambda d: (0, 0, 0)),
            all_picked,
        ],
        [((padded, row_width), bf16, (padded, row_width), lambda d: (0, 0))] * (n_fs - 1),
        (n_fs - 1,),
    )

    def pass_sum(*later):
        newest, *later = lax.optimization_barrier((head_sums[-1], *later))
        step = len(head_sums)
        if step + 1 < n_fs:
            total = newest.astype(f32) + head_parts[step - 1].astype(f32)
            head_sums.append(lax.ppermute(total.astype(bf16), "fsdp", ring))
        return later

    grad_chosen, *head_parts = pass_sum(grad_chosen, *head_parts)
    for _ in range(n_fs - 4):
        (grad_chosen,) = pass_sum(grad_chosen)

    (
        grad_final,
        grad_joined_one,
        grad_mixed,
        grad_attention,
        grad_feed,
        grad_hidden,
        sums_one,
        hidden_sums,
    ) = row_kernel(
        unfeed_kernel,
        (lengths,),
        [
            by_seq(row_width, grad_start),
            (grad_chosen, (n_dp, pick_count, row_width), lambda s, b, *_: (0, s, 0)),
            picks,
            by_seq(row_width, joined_one),
            by_seq(ff, gelu_slopes),
            by_seq(row_width, joined_two),
            vectors,
            out_weight,
            up_weight_low,
            down_weight_low,
        ],
        [
            ((n_tok, row_width), f32, *by_seq(row_width)),
            ((n_tok, row_width), f32, *by_seq(row_width)),
            ((n_tok, row_width), bf16, *by_seq(row_width)),
            ((n_tok, row_width), bf16, *by_seq(row_width)),
            ((n_tok, row_width), bf16, *by_seq(row_width)),
            ((n_tok, ff), bf16, *by_seq(ff)),
            ((6, 8, row_width), f32, *whole((6, 8, row_width))),
            ((8, ff), f32, *whole((8, ff))),
        ],
        (seq_count, n_block),
    )
    member = lax.axis_index("pair").reshape(1).astype(jnp.int32)
    n_plane = lax.axis_size("plane")
    share = row_width // (2 * n_plane)
    halves = pltpu.VMEM((n_plane, 2, share, row_width), bf16)

    def dealt(columns):
        out = (
            (columns, n_plane, share, row_width),
            bf16,
            (1, n_plane, share, row_width),
            lambda j, *_: (j, 0, 0, 0),
        )
        return [out, out]

    def full(array):
        return (array, *whole(array.shape))

    blocks = ff // row_width
    early_kept, early_given = row_kernel(
        early_kernel,
        (member,),
        [
            full(mixed_output),
            full(grad_attention),
            full(normed_low),
            (
                grad_hidden,
                (n_tok, row_width),
                lambda j, *_: (0, jnp.clip(j - 1, 0, blocks - 1)),
            ),
            (
                gelu_activated,
                (n_tok, row_width),
                lambda j, *_: (0, jnp.clip(j - 1 - blocks, 0, blocks - 1)),
            ),
            full(grad_feed),
        ],
        dealt(1 + 2 * blocks),
        (1 + 2 * blocks,),
        [halves],
    )
    up_rows = hidden_back(jnp.sum(hidden_sums, axis=0, keepdims=True), row_width)
    early_kept, early_given = pass_sum(early_kept, early_given)
    early = sum_in_pair(early_kept, early_given)
    grad_mixed, early, up_rows = lax.optimization_barrier((grad_mixed, early, up_rows))
    early = sum_in_plane(early)
    grad_parts = attend(lengths, packed, grad_mixed)
    flat_grad, place_grad, sums_two = row_kernel(
        leave_kernel,
        (lengths, keeps),
        [by_block(row_width, part) for part in grad_parts]
        + [
            by_block(row_width, grad_joined_one),
            by_block(row_width, grad_final),
            by_block(row_width, embedded),
            vectors,
            qkv_weight,
        ],
        [
            ((n_tok, row_width), bf16, *by_block(row_width)),
            ((row_width, seq_len), bf16, (row_width, rows), lambda b, s, *_: (0, b)),
            ((4, 8, row_width), f32, *whole((4, 8, row_width))),
        ],
        (n_block, seq_count),
        [pltpu.VMEM((rows, row_width), f32)],
    )
    flat_grad, early, head_sums[-1] = lax.optimization_barrier(
        (flat_grad, early, head_sums[-1])
    )
    early = lax.psum_scatter(
        early.reshape(early.shape[0], -1, row_width), "fsdp", scatter_dimension=1, tiled=True
    ).astype(f32)
    given_rows = rows_to_give(plan, 0, flat_grad)
    given_rows, *grad_parts = lax.optimization_barrier((given_rows, *grad_parts))
    returned = give_rows(given_rows, axes)
    own_part = more_given(plan, rounds, flat_grad, own_rows, head_parts[n_fs - 2], axes)
    late_kept, late_given = row_kernel(
        late_kernel,
        (member,),
        [full(flat_low)]
        + [full(part) for part in grad_parts]
        + [
            full(place_grad),
            full(sums_one),
            full(sums_two),
            full(up_rows.reshape(4, row_width)),
        ],
        dealt(4),
        (4,),
        [
            halves,
            pltpu.VMEM((row_width, row_width), f32),
            pltpu.VMEM((gain_width, row_width), f32),
        ],
    )
    late_kept, late_given, own_part = lax.optimization_barrier(
        (late_kept, late_given, own_part)
    )
    last = sum_in_plane(sum_in_pair(late_kept, late_given, 4))
    early, last = lax.optimization_barrier((early, last))
    last = sum_in_line(last)
    early_grads = (
        early[0],
        jnp.transpose(early[1 : 1 + blocks], (1, 2, 0)).reshape(in_rows, ff),
        jnp.swapaxes(early[1 + blocks :], 0, 1).reshape(-1, row_width),
    )
    rows = 400 if own_rows > 400 else 208
    steps = -(-own_rows // rows)

    def by_row(array=None, width=row_width):
        spec = ((rows, width), lambda r, *_: (r, 0))
        return spec if array is None else (array, *spec)

    table_grad, place_sums, qkv_sums, vector_sums, tile = row_kernel(
        functools.partial(table_kernel, own_rows),
        (),
        [
            full(wanted.reshape(1, -1)),
            full(returned),
            by_row(head_sums[-1]),
            by_row(own_part),
            full(tile),
            full(hidden_loss),
            full(head_loss),
            full(last_loss),
        ]
        + [full(grad) for grad in early_grads]
        + [full(last)],
        [
            ((own_rows, row_width), f32, *by_row()),
            ((in_rows, seq_len), f32, *whole((in_rows, seq_len))),
            ((in_rows, 3 * row_width), f32, *whole((in_rows, 3 * row_width))),
            (gains_biases.shape, f32, *whole(gains_biases.shape)),
            ((8, 128), f32, *whole((8, 128))),
        ],
        (steps,),
    )

    def exchange(tile):
        return lax.all_to_all(
            jnp.broadcast_to(tile[None], (n_dev, 8, 128)), axes, split_axis=0, concat_axis=0
        )

    def turned(arrays):
        return [array.T if place == 1 else array for place, array in enumerate(arrays)]

    def specs(arrays):
        return [by_row(arrays[0])] + [full(array) for array in arrays[1:]]

    weights = turned(masters)
    like = [
        (array.shape, f32, *(whole(array.shape) if place else by_row()))
        for place, array in enumerate(weights)
    ]
    tile_out = ((8, 128), f32, *whole((8, 128)))
    *results, totals, tile = row_kernel(
        functools.partial(update_kernel, own_rows, steps),
        (),
        [full(exchange(tile))]
        + specs(weights)
        + specs([table_grad, place_sums, qkv_sums, *early_grads, vector_sums])
        + specs(turned(firsts))
        + specs(turned(seconds)),
        like * 3 + [tile_out, tile_out],
        (steps,),
    )
    new_moments, new_squares = turned(results[:7]), turned(results[7:14])
    *new_weights, update_norms = row_kernel(
        functools.partial(weight_kernel, steps),
        (),
        [full(exchange(tile)), full(totals)] + specs(weights) + specs(results[14:]),
        like + [tile_out],
        (steps,),
    )
    new_weights = turned(new_weights)
    loss_sum, token_count, grad_norm = totals[0, 1], totals[0, 2], totals[0, 127]
    matrix_norms = jnp.stack([jnp.sqrt(totals[0, 3:10]), update_norms[0, :7]])
    return (
        loss_sum,
        token_count,
        grad_norm,
        new_weights[0],
        new_weights[1],
        new_weights[2],
        new_weights[3],
        new_weights[4],
        new_weights[5],
        new_weights[6],
        new_moments[0],
        new_moments[1],
        new_moments[2],
        new_moments[3],
        new_moments[4],
        new_moments[5],
        new_moments[6],
        new_squares[0],
        new_squares[1],
        new_squares[2],
        new_squares[3],
        new_squares[4],
        new_squares[5],
        new_squares[6],
        matrix_norms,
    )


def solution(mesh):
    split = Mesh(
        mesh.devices.reshape(mesh.shape["dp"] // 2, 2, mesh.shape["fsdp"]), AXES
    )
    placed = (
        P(AXES, None),
        P(AXES, None),
        P(AXES),
        P(AXES, None),
        P(AXES, None, None),
        P(AXES, None, None),
        P(AXES, None),
        P(None, AXES),
        P(AXES, None),
        P(AXES, None),
        P(AXES, None),
        P(AXES, None),
        P(None, AXES),
        P(AXES, None),
        P(None, AXES),
        P(AXES, None),
        P(AXES, None),
        P(AXES, None),
        P(AXES, None),
        P(None, AXES),
        P(AXES, None),
        P(None, AXES),
        P(AXES, None),
        P(AXES, None),
        P(AXES, None),
        P(AXES, None),
        P(None, AXES),
    )
    return jax.shard_map(
        on_device,
        mesh=split,
        in_specs=placed,
        out_specs=(
            P(),
            P(),
            P(),
            P(AXES, None),
            P(None, AXES),
            P(AXES, None),
            P(AXES, None),
            P(AXES, None),
            P(AXES, None),
            P(None, AXES),
            P(AXES, None),
            P(None, AXES),
            P(AXES, None),
            P(AXES, None),
            P(AXES, None),
            P(AXES, None),
            P(None, AXES),
            P(AXES, None),
            P(None, AXES),
            P(AXES, None),
            P(AXES, None),
            P(AXES, None),
            P(AXES, None),
            P(None, AXES),
            P(),
        ),
        check_vma=False,
    )
```
